32 devices in a mesh: batch: 2 (over y), seq: 16 (over z, x, core).
Axes of the slice: x: 2, y: 2, z: 4, core: 2. Of those that a mesh axis runs over, the one named last changes fastest.
Arguments:
- inputs: bfloat16 [2, 4, 2048, 768], P(None, 'batch', 'seq'), may hold values from -6 to 6
- seg_ids: int32 [2, 4, 2048], P(None, 'batch', 'seq'), may hold values from 0 to 8, as said below
- cotangent: bfloat16 [2, 4, 2048, 768], P(None, 'batch', 'seq'), may hold values from -6 to 6
- projection: bfloat16 [12, 64, 256], replicated, may hold values from -6 to 6
- w_qkv: bfloat16 [768, 2304], P(('batch', 'seq')), may hold values from -0.21875 to 0.21875
- b_qkv: bfloat16 [2304], P(('batch', 'seq')), may hold values from -4 to 4
- w_o: bfloat16 [768, 768], P(('batch', 'seq')), may hold values from -1.25 to 1.25
- b_o: bfloat16 [768], P(('batch', 'seq')), may hold values from -4 to 4
- ln1_gain: bfloat16 [768], P(('batch', 'seq')), may hold values from 0.099609375 to 1.8984375
- ln1_bias: bfloat16 [768], P(('batch', 'seq')), may hold values from -4 to 4
- w_in: bfloat16 [768, 3072], P(('batch', 'seq')), may hold values from -0.21875 to 0.21875
- b_in: bfloat16 [3072], P(('batch', 'seq')), may hold values from -4 to 4
- w_out: bfloat16 [3072, 768], P(('batch', 'seq')), may hold values from -0.109375 to 0.109375
- b_out: bfloat16 [768], P(('batch', 'seq')), may hold values from -4 to 4
- ln2_gain: bfloat16 [768], P(('batch', 'seq')), may hold values from 0.099609375 to 1.8984375
- ln2_bias: bfloat16 [768], P(('batch', 'seq')), may hold values from -4 to 4
Outputs:
- output: bfloat16 [2, 4, 2048, 768], P(None, 'batch', 'seq')
- input_grad: bfloat16 [2, 4, 2048, 768], P(None, 'batch', 'seq')
- grad_w_qkv: float32 [768, 2304], P(('batch', 'seq'))
- grad_b_qkv: float32 [2304], P(('batch', 'seq'))
- grad_w_o: float32 [768, 768], P(('batch', 'seq'))
- grad_b_o: float32 [768], P(('batch', 'seq'))
- grad_ln1_gain: float32 [768], P(('batch', 'seq'))
- grad_ln1_bias: float32 [768], P(('batch', 'seq'))
- grad_w_in: float32 [768, 3072], P(('batch', 'seq'))
- grad_b_in: float32 [3072], P(('batch', 'seq'))
- grad_w_out: float32 [3072, 768], P(('batch', 'seq'))
- grad_b_out: float32 [768], P(('batch', 'seq'))
- grad_ln2_gain: float32 [768], P(('batch', 'seq'))
- grad_ln2_bias: float32 [768], P(('batch', 'seq'))
The draws below stay inside these ranges and needn't reach their ends.
Inputs may be any that keep to these rules, and one draw needn't show every extreme that they name: `seg_ids`: along each sequence the ids start at 0 and rise by 0 or 1 from one token to the next; equal ids form one segment. Of the 2 sequences that share a micro-batch and an index of batch, one is a single segment; each of the others has exactly 16 // 2 + 1 segments.
All inputs are finite; a program needn't handle non-finite values.
Results may differ from the reference program's by a relative error of at most 0.03.
Values may be sent and summed in bfloat16 or wider, within the bound.
No kernel may reach another device: no remote copies, remote signals or barrier semaphores. Data moves between devices by JAX's collectives and lax.ppermute only.
A program may use at most 320 MiB of HBM per device.

```python
import jax
import jax.numpy as jnp
from jax import lax

D = 768
HEADS = 12
HEAD_DIM = 64
FF = 3072
FEATS = 256
MICRO = 2
BLOCK = 128
SEQS = 2
SEQ_LEN = 2048
SEQS_ALL = 4
N_SEQ = 16


def draw_seg_ids(key, part):
    key = jax.random.fold_in(key, 7)
    pick_key, start_key = jax.random.split(key)
    group_count = SEQS_ALL // SEQS
    row_count = MICRO * SEQS_ALL
    start_count = N_SEQ // 2
    picked = jax.random.randint(pick_key, (MICRO, group_count, 1), 0, SEQS)
    single = (jnp.arange(SEQS)[None, None, :] == picked).reshape(row_count)
    row_keys = jax.random.split(start_key, row_count)
    orders = jax.vmap(lambda one_key: jax.random.permutation(one_key, SEQ_LEN - 1))(row_keys)
    chosen = (orders[:, :start_count] + 1).astype(jnp.int32)
    row_index = jnp.broadcast_to(jnp.arange(row_count)[:, None], chosen.shape)
    starts = jnp.zeros((row_count, SEQ_LEN), jnp.int32).at[row_index, chosen].set(1)
    starts = starts * (1 - single.astype(jnp.int32))[:, None]
    idents = jnp.cumsum(starts, axis=1).astype(jnp.int32)
    return idents.reshape(MICRO, SEQS_ALL, SEQ_LEN)


def level_of(rng, shape, pieces, least, high):
    level, own = 1.0, jax.random.fold_in(rng, 6)
    for position, blocks in pieces:
        steps = jnp.exp(jax.random.uniform(jax.random.fold_in(own, position), (blocks,), jnp.float32, least / len(pieces), high / len(pieces)))
        level = level * jnp.repeat(steps, shape[position] // blocks).reshape([-1 if axis == position else 1 for axis in range(len(shape))])
    return level


def gaussian(stream_key, extent, deviation, reach, pieces=(), held_as=jnp.bfloat16):
    drawn = jax.random.normal(stream_key, extent, jnp.float32) * deviation
    if len(pieces) > 0:
        drawn = level_of(stream_key, extent, pieces, -0.22, 0.18) * drawn
    return jnp.clip(drawn, min=-reach, max=reach).astype(held_as)


def setup_inputs(seed: int = 0) -> dict:
    streams_of = jax.random.split(jax.random.key(seed), 17)
    inputs = gaussian(streams_of[0], (MICRO, SEQS_ALL, SEQ_LEN, D), 1.0, 6.0, ((1, 2), (2, 16)))
    seg_ids = draw_seg_ids(jax.random.fold_in(streams_of[16], 71), 0)
    cotangent = gaussian(streams_of[2], (MICRO, SEQS_ALL, SEQ_LEN, D), 1.0, 6.0, ((1, 2), (2, 16)))
    projection = gaussian(streams_of[3], (HEADS, HEAD_DIM, FEATS), 1.0, 6.0)
    w_qkv = gaussian(streams_of[4], (D, 3 * D), D ** -0.5, 0.21875, ((0, 32),))
    b_qkv = gaussian(streams_of[5], (3 * D,), 0.3, 4.0, ((0, 32),))
    w_o = gaussian(streams_of[6], (D, D), (D // 32) ** -0.5, 1.25, ((0, 32),))
    b_o = gaussian(streams_of[7], (D,), 0.3, 4.0, ((0, 32),))
    ln1_gain = jnp.clip(1.0 + 0.18 * jax.random.normal(streams_of[8], (D,), jnp.float32), 0.099609375, 1.8984375).astype(jnp.bfloat16)
    ln1_bias = gaussian(streams_of[9], (D,), 0.3, 4.0, ((0, 32),))
    w_in = gaussian(streams_of[10], (D, FF), D ** -0.5, 0.21875, ((0, 32),))
    b_in = gaussian(streams_of[11], (FF,), 0.3, 4.0, ((0, 32),))
    w_out = gaussian(streams_of[12], (FF, D), FF ** -0.5, 0.109375, ((0, 32),))
    b_out = gaussian(streams_of[13], (D,), 0.3, 4.0, ((0, 32),))
    ln2_gain = jnp.clip(1.0 + 0.18 * jax.random.normal(streams_of[14], (D,), jnp.float32), 0.099609375, 1.8984375).astype(jnp.bfloat16)
    ln2_bias = gaussian(streams_of[15], (D,), 0.3, 4.0, ((0, 32),))
    return dict(inputs=inputs, seg_ids=seg_ids, cotangent=cotangent, projection=projection, w_qkv=w_qkv, b_qkv=b_qkv, w_o=w_o, b_o=b_o, ln1_gain=ln1_gain, ln1_bias=ln1_bias, w_in=w_in, b_in=b_in, w_out=w_out, b_out=b_out, ln2_gain=ln2_gain, ln2_bias=ln2_bias)


@jax.custom_vjp
def lower_precision(v):
    return lax.optimization_barrier(v.astype(jnp.bfloat16)).astype(jnp.float32)

@jax.custom_vjp
def lower_precision_reverse(v):
    return v

def low_keep(v):
    return (lower_precision(v), None)

def low_pass(kept, grad):
    return (grad,)

def back_keep(v):
    return (v, None)

def back_low(kept, grad):
    return (lower_precision(grad),)
lower_precision.defvjp(low_keep, low_pass)
lower_precision_reverse.defvjp(back_keep, back_low)
norm_eps = 1e-05
precision_highest = lax.Precision.HIGHEST

def layer_norm(row_vals, gain_vec, shift_vec):
    centred = row_vals - lax.optimization_barrier(jnp.mean(row_vals, axis=-1, keepdims=True))
    spread = lax.optimization_barrier(jnp.mean(centred * centred, axis=-1, keepdims=True))
    return centred * lax.rsqrt(spread + norm_eps) * gain_vec + shift_vec

def features(row_vals, project):
    logits = lower_precision_reverse(jnp.einsum('lhd,hdm->lhm', row_vals, project, precision=precision_highest))
    halves = 0.5 * lax.optimization_barrier(jnp.sum(row_vals * row_vals, axis=-1, keepdims=True))
    return lower_precision(jnp.exp(logits - halves) * FEATS ** (-0.5))

def block_step(carried, block_data):
    prefix_state, pre_total, pre_ident = carried
    query_features, key_feat, value_matrix, idents = block_data
    idents_f = idents.astype(jnp.float32)
    places = jnp.arange(BLOCK)
    causal = places[:, None] >= places[None, :]
    same_seg = idents[:, None] == idents[None, :]
    seg_mask = jnp.logical_and(causal, same_seg).astype(jnp.float32)
    scores = jnp.einsum('thm,jhm->htj', query_features, key_feat, precision=precision_highest)
    attn_mat = lower_precision(lower_precision_reverse(scores * seg_mask[None]))
    num_in = jnp.einsum('htj,jhd->thd', attn_mat, value_matrix, precision=precision_highest)
    den_in = jnp.transpose(lax.optimization_barrier(jnp.sum(attn_mat, axis=-1)))
    carry_gate = (idents_f == pre_ident).astype(jnp.float32)
    numerator_input = jnp.einsum('igl,glf->igf', query_features, lower_precision(prefix_state), precision=precision_highest)
    den_x = jnp.einsum('thm,hm->th', query_features, lower_precision(pre_total), precision=precision_highest)
    numerator = lower_precision_reverse(num_in + carry_gate[:, None, None] * numerator_input)
    denominator = lower_precision_reverse(den_in + carry_gate[:, None] * den_x)
    attended = numerator / denominator[:, :, None]
    last_ident = idents_f[-1]
    tail_gate = (idents_f == last_ident).astype(jnp.float32)
    masked_key_rows = key_feat * tail_gate[:, None, None]
    trailing_state = lower_precision_reverse(jnp.einsum('cwg,cwf->wgf', masked_key_rows, value_matrix, precision=precision_highest))
    tail_total = lower_precision_reverse(lax.optimization_barrier(jnp.sum(masked_key_rows, axis=0)))
    joined = (last_ident == pre_ident).astype(jnp.float32)
    carried_next = (trailing_state + joined * prefix_state, tail_total + joined * pre_total, last_ident)
    return (carried_next, attended)

def layer(row_vals, idents, project, params):
    w_qkv, b_qkv, w_o, b_o, gain_one, shift_one, w_in, b_in, w_out, b_out, gain_two, shift_two = params
    qkv = lower_precision_reverse(jnp.dot(row_vals, w_qkv, precision=precision_highest, preferred_element_type=jnp.float32) + b_qkv)
    feat_scale = HEAD_DIM ** (-0.25)
    queries = lower_precision(qkv[:, :D] * feat_scale).reshape(SEQ_LEN, HEADS, HEAD_DIM)
    key_rows = lower_precision(qkv[:, D:2 * D] * feat_scale).reshape(SEQ_LEN, HEADS, HEAD_DIM)
    value_matrix = lower_precision(qkv[:, 2 * D:]).reshape(SEQ_LEN, HEADS, HEAD_DIM)
    query_features = features(queries, project)
    key_feat = features(key_rows, project)
    blocks = (query_features.reshape(N_SEQ, BLOCK, HEADS, FEATS), key_feat.reshape(N_SEQ, BLOCK, HEADS, FEATS), value_matrix.reshape(N_SEQ, BLOCK, HEADS, HEAD_DIM), idents.reshape(N_SEQ, BLOCK))
    initial = (jnp.zeros((HEADS, FEATS, HEAD_DIM), jnp.float32), jnp.zeros((HEADS, FEATS), jnp.float32), jnp.array(-1.0, jnp.float32))
    unused, attended = lax.scan(jax.checkpoint(block_step), initial, blocks)
    mixed_heads = lower_precision(attended.reshape(SEQ_LEN, D))
    branch = lower_precision_reverse(jnp.dot(mixed_heads, w_o, precision=precision_highest, preferred_element_type=jnp.float32) + b_o)
    hidden_one = layer_norm(row_vals + branch, gain_one, shift_one)
    inner_pre = lower_precision_reverse(jnp.dot(lower_precision(hidden_one), w_in, precision=precision_highest, preferred_element_type=jnp.float32) + b_in)
    active = lower_precision(jax.nn.gelu(inner_pre, approximate=False))
    outer_out = lower_precision_reverse(jnp.dot(active, w_out, precision=precision_highest, preferred_element_type=jnp.float32) + b_out)
    return layer_norm(hidden_one + outer_out, gain_two, shift_two)

def reference(inputs, seg_ids, cotangent, projection, w_qkv, b_qkv, w_o, b_o, ln1_gain, ln1_bias, w_in, b_in, w_out, b_out, ln2_gain, ln2_bias):
    params = tuple((weight.astype(jnp.float32) for weight in (w_qkv, b_qkv, w_o, b_o, ln1_gain, ln1_bias, w_in, b_in, w_out, b_out, ln2_gain, ln2_bias)))
    project = projection.astype(jnp.float32)
    seq_count = MICRO * SEQS_ALL
    rows_all = inputs.reshape(seq_count, SEQ_LEN, D)
    idents_all = seg_ids.reshape(seq_count, SEQ_LEN)
    cot_all = cotangent.reshape(seq_count, SEQ_LEN, D)

    def per_sequence(totals, sample):
        row_block, idents, cot_rows = sample

        def forward_fn(rows_in, params_in):
            return layer(rows_in, idents, project, params_in)
        result, pullback = jax.vjp(forward_fn, row_block.astype(jnp.float32), params)
        row_grad, param_grad = pullback(cot_rows.astype(jnp.float32))
        totals = jax.tree.map(lambda acc_left, acc_new: acc_left + acc_new, totals, param_grad)
        return (totals, (result.astype(jnp.bfloat16), row_grad.astype(jnp.bfloat16)))
    zero_set = tuple((jnp.zeros_like(weight) for weight in params))
    totals, (outputs, grads_in) = lax.scan(per_sequence, zero_set, (rows_all, idents_all, cot_all))
    return (outputs.reshape(MICRO, SEQS_ALL, SEQ_LEN, D), grads_in.reshape(MICRO, SEQS_ALL, SEQ_LEN, D), totals[0], totals[1], totals[2], totals[3], totals[4], totals[5], totals[6], totals[7], totals[8], totals[9], totals[10], totals[11])
```

```python
from functools import partial

import jax
import jax.numpy as jnp
from jax import lax
from jax.sharding import PartitionSpec as P

norm_eps = 1e-05
bf16 = jnp.bfloat16
f32 = jnp.float32
AXES = ("batch", "seq")


def flat_xor(value, mask):
    n = lax.axis_size("batch") * lax.axis_size("seq")
    return lax.ppermute(value, AXES, [(i, i ^ mask) for i in range(n)])


def log2(n):
    return n.bit_length() - 1


def gather_order(nb, ns, swap):
    seq_bits = list(range(log2(ns)))
    batch_bits = [log2(ns) + b for b in range(log2(nb))]
    low, mid, high = seq_bits[0], seq_bits[1], seq_bits[2:]
    cross = [mid] + batch_bits if not swap else batch_bits + [mid]
    return high[::-1] + cross + [low]


def my_flat():
    return lax.axis_index("batch") * lax.axis_size("seq") + lax.axis_index("seq")


def gather_rows(shard, swap):
    nb, ns = lax.axis_size("batch"), lax.axis_size("seq")
    nbits = log2(nb * ns)
    me = my_flat()
    shape = shard.shape
    buf = shard.reshape((1,) * nbits + shape)
    for bit in gather_order(nb, ns, swap):
        axis = nbits - 1 - bit
        other = flat_xor(buf, 1 << bit)
        mine = (me >> bit) & 1
        buf = jnp.where(
            mine == 1,
            jnp.concatenate([other, buf], axis),
            jnp.concatenate([buf, other], axis),
        )
    return buf.reshape((nb * ns * shape[0],) + shape[1:])


def scatter_rows(full, swap):
    nb, ns = lax.axis_size("batch"), lax.axis_size("seq")
    nbits = log2(nb * ns)
    me = my_flat()
    rows = full.shape[0] // (nb * ns)
    buf = full.reshape((2,) * nbits + (rows,) + full.shape[1:])
    for bit in gather_order(nb, ns, swap)[::-1]:
        axis = nbits - 1 - bit
        mine = (me >> bit) & 1
        keep = lax.dynamic_index_in_dim(buf, mine, axis, True)
        send = lax.dynamic_index_in_dim(buf, 1 - mine, axis, True)
        got = flat_xor(send.astype(bf16), 1 << bit)
        buf = keep.astype(f32) + got.astype(f32)
    return buf.reshape((rows,) + full.shape[1:]).astype(f32)


def seq_perm(value, pairs):
    return lax.ppermute(value, "seq", pairs)


def exclusive_scan(tails, ids, rev):
    n = lax.axis_size("seq")
    place = lax.axis_index("seq")
    if rev:
        ids = ids[::-1]
    p = n - 1 - place if rev else place

    def at(q):
        return n - 1 - q if rev else q

    def move(value, pairs):
        return seq_perm(value, [(at(a), at(b)) for a, b in pairs])

    def key(q):
        return lax.dynamic_index_in_dim(ids, jnp.clip(q, 0, n - 1), 0, False)

    def gate(a, b):
        return (key(a) == key(b)).astype(f32)

    def gated(g, value):
        return g.reshape(g.shape + (1,) * (value.ndim - 1)) * value.astype(f32)

    c = p & 1
    x = (p >> 1) & 1
    base = p - (p & 3)
    pair = p - c
    seqs = tails.shape[0]
    rest = tails.shape[2:]
    parts = tails.reshape((seqs, 2, 2) + rest)

    def pick(a, i, axis):
        return lax.dynamic_index_in_dim(a, i, axis, False)

    core = [(i, i ^ 1) for i in range(n)]
    across = [(i, i ^ 2) for i in range(n)]
    own = pick(parts, c, 2)
    other = move(pick(parts, 1 - c, 2), core)
    first = jnp.where(c == 0, own, other)
    second = jnp.where(c == 0, other, own)
    pair_sum = second.astype(f32) + gated(gate(pair, pair + 1), first)
    pair_mine = pick(pair_sum, x, 1)
    pair_other = move(pick(pair_sum, 1 - x, 1).astype(bf16), across).astype(f32)
    low = jnp.where(x == 0, pair_mine, pair_other)
    high = jnp.where(x == 0, pair_other, pair_mine)
    total = high + gated(gate(base + 1, base + 3), low)
    before = jnp.zeros_like(total)
    step = 1
    while step * 4 < n:
        got = move(
            total.astype(bf16), [(i, i + 4 * step) for i in range(n - 4 * step)]
        )
        source = base + 3 - 4 * step
        before = before + gated(gate(source, base - 1), got)
        total = total + gated(gate(source, base + 3), got)
        step *= 2
    before_high = low + gated(gate(base - 1, base + 1), before)
    mine = jnp.where(x == 0, before, before_high)
    theirs = jnp.where(x == 0, before_high, before)
    got = move(theirs.astype(bf16), across)
    mine_b = mine.astype(bf16)
    entry = jnp.where(x == 0, jnp.stack([mine_b, got], 1), jnp.stack([got, mine_b], 1))
    after = first.astype(f32) + gated(gate(pair - 1, pair), entry)
    after_b = after.astype(bf16)
    mine = jnp.where(c == 0, entry, after_b)
    theirs = jnp.where(c == 0, after_b, entry)
    got = move(theirs, core)
    result = jnp.where(c == 0, jnp.stack([mine, got], 2), jnp.stack([got, mine], 2))
    return result.reshape(tails.shape)


def norm_forward(row_vals, gain_vec, shift_vec):
    centred = row_vals - jnp.mean(row_vals, axis=-1, keepdims=True)
    inv_std = lax.rsqrt(jnp.mean(centred * centred, axis=-1, keepdims=True) + norm_eps)
    normed = centred * inv_std
    return (normed * gain_vec + shift_vec, normed, inv_std)


def norm_backward(grad_out, normed, inv_std, gain_vec):
    grad_normed = grad_out * gain_vec
    return inv_std * (
        grad_normed
        - jnp.mean(grad_normed, axis=-1, keepdims=True)
        - normed * jnp.mean(grad_normed * normed, axis=-1, keepdims=True)
    )


def feature_map(rows_b, projection):
    logits = jnp.einsum("schd,hdm->schm", rows_b, projection, preferred_element_type=f32)
    rows_wide = rows_b.astype(f32)
    halves = 0.5 * jnp.sum(rows_wide * rows_wide, axis=-1, keepdims=True)
    return jnp.exp(logits - halves) * projection.shape[2] ** (-0.5)


def feature_back(grad_feat, feat_full, rows_b, projection, feat_scale):
    grad_logit = grad_feat * feat_full
    grad_half = -jnp.sum(grad_logit, axis=-1, keepdims=True)
    grad_rows = jnp.einsum(
        "schm,hdm->schd",
        grad_logit.astype(bf16),
        projection,
        preferred_element_type=f32,
    )
    return (grad_rows + grad_half * rows_b.astype(f32)) * feat_scale


def pack_state(state, total):
    s, h, m, d = state.shape
    a = jnp.transpose(state, (0, 1, 3, 2)).astype(bf16).reshape(s, 4, h // 4 * d, m)
    b = total.astype(bf16).reshape(s, 4, h // 4, m)
    return jnp.concatenate([a, b], axis=2)


def unpack_state(packed, heads, d):
    s, _, _, m = packed.shape
    cut = heads // 4 * d
    a = packed[:, :, :cut].reshape(s, heads, d, m)
    b = packed[:, :, cut:].reshape(s, heads, m)
    return jnp.transpose(a, (0, 1, 3, 2)), b


def body(
    inputs,
    seg_ids,
    cotangent,
    projection,
    w_qkv,
    b_qkv,
    w_o,
    b_o,
    ln1_gain,
    ln1_bias,
    w_in,
    b_in,
    w_out,
    b_out,
    ln2_gain,
    ln2_bias,
):
    micro, seqs_micro, block_len, model_width = inputs.shape
    head_count, head_dim, feat_count = projection.shape
    n_seq = lax.axis_size("seq")
    n_dev = lax.axis_size("batch") * n_seq
    place = lax.axis_index("seq")
    seqs = micro * seqs_micro
    rows = seqs * block_len
    feat_scale = head_dim ** (-0.25)
    head_shape = (seqs, block_len, head_count, head_dim)

    vectors = (b_qkv, b_o, ln1_gain, ln1_bias, b_in, b_out, ln2_gain, ln2_bias)
    sizes = [v.shape[0] for v in vectors]
    packed = gather_rows(jnp.concatenate(vectors)[None], False)
    cuts = [sum(sizes[:i]) for i in range(len(sizes) + 1)]
    (b_qkv_f, b_o_f, gain_one, shift_one, b_in_f, b_out_f, gain_two, shift_two) = (
        packed[:, cuts[i] : cuts[i + 1]].reshape(-1).astype(f32) for i in range(len(sizes))
    )
    idents = seg_ids.reshape(seqs, block_len)
    last_all = lax.all_gather(idents[:, -1].astype(f32), "seq")
    half = w_qkv.shape[1] // 2
    w_qkv_f = jnp.concatenate(
        [gather_rows(w_qkv[:, :half], False), gather_rows(w_qkv[:, half:], True)], axis=1
    )
    w_o_f = gather_rows(w_o, False)
    w_in_f = gather_rows(w_in, False)
    w_out_f = gather_rows(w_out, True)

    tokens_rows = inputs.reshape(rows, model_width)
    qkv = jnp.dot(tokens_rows, w_qkv_f, preferred_element_type=f32) + b_qkv_f
    queries = (qkv[:, :model_width] * feat_scale).astype(bf16).reshape(head_shape)
    key_rows = (
        (qkv[:, model_width : 2 * model_width] * feat_scale).astype(bf16).reshape(head_shape)
    )
    value_matrix = qkv[:, 2 * model_width :].astype(bf16).reshape(head_shape)
    query_full = feature_map(queries, projection)
    key_full = feature_map(key_rows, projection)
    query_features = query_full.astype(bf16)
    key_feat = key_full.astype(bf16)

    idents_f = idents.astype(f32)
    last_ident = idents_f[:, -1]
    tail_gate = (idents_f == last_ident[:, None]).astype(f32)
    key_tail = key_feat * tail_gate.astype(bf16)[:, :, None, None]
    trailing_state = jnp.einsum(
        "sjhm,sjhd->shmd", key_tail, value_matrix, preferred_element_type=f32
    )
    tail_total = jnp.sum(key_tail, axis=1, dtype=f32)
    pre_state = exclusive_scan(pack_state(trailing_state, tail_total), last_all, False)
    state_b, total_b = unpack_state(pre_state, head_count, head_dim)

    pre_all = jnp.concatenate([-jnp.ones_like(last_all[:1]), last_all[:-1]], axis=0)
    pre_ident = lax.dynamic_index_in_dim(pre_all, place, 0, False)
    carry_gate = (idents_f == pre_ident[:, None]).astype(f32)

    places = jnp.arange(block_len)
    causal = places[:, None] >= places[None, :]
    seg_mask = jnp.logical_and(causal[None], idents[:, :, None] == idents[:, None, :]).astype(f32)
    scores = jnp.einsum("sthm,sjhm->shtj", query_features, key_feat, preferred_element_type=f32)
    attn_mat = (scores * seg_mask[:, None]).astype(bf16)
    num_in = jnp.einsum("shtj,sjhd->sthd", attn_mat, value_matrix, preferred_element_type=f32)
    den_in = jnp.transpose(jnp.sum(attn_mat, axis=-1, dtype=f32), (0, 2, 1))
    numerator = num_in + carry_gate[:, :, None, None] * jnp.einsum(
        "schm,shmd->schd", query_features, state_b, preferred_element_type=f32
    )
    denominator = den_in + carry_gate[:, :, None] * jnp.einsum(
        "schm,shm->sch", query_features, total_b, preferred_element_type=f32
    )
    attended = numerator / denominator[..., None]
    mixed_heads = attended.astype(bf16).reshape(rows, model_width)
    branch = jnp.dot(mixed_heads, w_o_f, preferred_element_type=f32) + b_o_f
    hidden_one, normed_one, inv_one = norm_forward(
        tokens_rows.astype(f32) + branch, gain_one, shift_one
    )
    hidden_b = hidden_one.astype(bf16)
    inner_pre = jnp.dot(hidden_b, w_in_f, preferred_element_type=f32) + b_in_f
    active, gelu_pull = jax.vjp(partial(jax.nn.gelu, approximate=False), inner_pre)
    active_b = active.astype(bf16)
    outer_out = jnp.dot(active_b, w_out_f, preferred_element_type=f32) + b_out_f
    result, normed_two, inv_two = norm_forward(hidden_one + outer_out, gain_two, shift_two)
    cot_rows = cotangent.reshape(rows, model_width).astype(f32)
    grad_gain_two = jnp.sum(cot_rows * normed_two, axis=0)
    grad_shift_two = jnp.sum(cot_rows, axis=0)
    grad_res_two = norm_backward(cot_rows, normed_two, inv_two, gain_two)
    grad_outer = grad_res_two.astype(bf16)
    grad_w_out = jnp.einsum("rf,rd->fd", active_b, grad_outer, preferred_element_type=f32)
    g_w_out = scatter_rows(grad_w_out.astype(bf16), True)
    grad_b_out = jnp.sum(grad_outer, axis=0, dtype=f32)
    grad_active = jnp.dot(grad_outer, w_out_f.T, preferred_element_type=f32)
    (grad_inner,) = gelu_pull(grad_active)
    grad_inner_b = grad_inner.astype(bf16)
    grad_w_in = jnp.einsum("rd,rf->df", hidden_b, grad_inner_b, preferred_element_type=f32)
    g_w_in = scatter_rows(grad_w_in.astype(bf16), False)
    grad_b_in = jnp.sum(grad_inner_b, axis=0, dtype=f32)
    grad_hidden = jnp.dot(grad_inner_b, w_in_f.T, preferred_element_type=f32) + grad_res_two
    grad_gain_one = jnp.sum(grad_hidden * normed_one, axis=0)
    grad_shift_one = jnp.sum(grad_hidden, axis=0)
    grad_res_one = norm_backward(grad_hidden, normed_one, inv_one, gain_one)
    grad_branch = grad_res_one.astype(bf16)
    grad_w_o = jnp.einsum("rk,rd->kd", mixed_heads, grad_branch, preferred_element_type=f32)
    g_w_o = scatter_rows(grad_w_o.astype(bf16), False)
    grad_b_o = jnp.sum(grad_branch, axis=0, dtype=f32)
    grad_att = jnp.dot(grad_branch, w_o_f.T, preferred_element_type=f32).reshape(head_shape)
    grad_num = (grad_att / denominator[..., None]).astype(bf16)
    grad_den = (-jnp.sum(grad_att * attended, axis=-1) / denominator).astype(bf16)
    grad_den_f = grad_den.astype(f32)
    query_gated = query_features * carry_gate.astype(bf16)[:, :, None, None]
    grad_state = jnp.einsum("schm,schd->shmd", query_gated, grad_num, preferred_element_type=f32)
    grad_total = jnp.einsum("schm,sch->shm", query_gated, grad_den, preferred_element_type=f32)
    back = exclusive_scan(pack_state(grad_state, grad_total), pre_all, True)
    back_state_b, back_total_b = unpack_state(back, head_count, head_dim)

    grad_mat = jnp.einsum("sthd,sjhd->shtj", grad_num, value_matrix, preferred_element_type=f32)
    grad_mat = grad_mat + jnp.transpose(grad_den_f, (0, 2, 1))[..., None]
    grad_score = (grad_mat * seg_mask[:, None]).astype(bf16)
    grad_value = jnp.einsum("shtj,sthd->sjhd", attn_mat, grad_num, preferred_element_type=f32)
    grad_query = jnp.einsum("shtj,sjhm->sthm", grad_score, key_feat, preferred_element_type=f32)
    grad_query = grad_query + carry_gate[:, :, None, None] * (
        jnp.einsum("schd,shmd->schm", grad_num, state_b, preferred_element_type=f32)
        + grad_den_f[..., None] * total_b.astype(f32)[:, None]
    )
    grad_key = jnp.einsum("shtj,sthm->sjhm", grad_score, query_features, preferred_element_type=f32)
    grad_key = grad_key + tail_gate[:, :, None, None] * (
        jnp.einsum("sjhd,shmd->sjhm", value_matrix, back_state_b, preferred_element_type=f32)
        + back_total_b.astype(f32)[:, None]
    )
    grad_value = grad_value + jnp.einsum(
        "sjhm,shmd->sjhd", key_tail, back_state_b, preferred_element_type=f32
    )
    grad_q = feature_back(grad_query, query_full, queries, projection, feat_scale)
    grad_k = feature_back(grad_key, key_full, key_rows, projection, feat_scale)
    grad_qkv = jnp.concatenate(
        [
            grad_q.reshape(rows, model_width),
            grad_k.reshape(rows, model_width),
            grad_value.reshape(rows, model_width),
        ],
        axis=1,
    ).astype(bf16)
    grad_w_qkv = jnp.einsum("rd,rk->dk", tokens_rows, grad_qkv, preferred_element_type=f32)
    gw = grad_w_qkv.astype(bf16)
    g_w_qkv = jnp.concatenate(
        [scatter_rows(gw[:, :half], False), scatter_rows(gw[:, half:], True)], axis=1
    )
    grad_b_qkv = jnp.sum(grad_qkv, axis=0, dtype=f32)
    grad_tokens = jnp.dot(grad_qkv, w_qkv_f.T, preferred_element_type=f32) + grad_res_one

    vec_grads = (
        grad_b_qkv,
        grad_b_o,
        grad_gain_one,
        grad_shift_one,
        grad_b_in,
        grad_b_out,
        grad_gain_two,
        grad_shift_two,
    )
    vec = jnp.concatenate([v.reshape(n_dev, -1) for v in vec_grads], axis=1)
    vec = scatter_rows(vec, False)[0]
    (g_b_qkv, g_b_o, g_gain_one, g_shift_one, g_b_in, g_b_out, g_gain_two, g_shift_two) = (
        vec[cuts[i] : cuts[i + 1]] for i in range(len(sizes))
    )
    out_rows = result.astype(bf16).reshape(inputs.shape)
    grad_rows = grad_tokens.astype(bf16).reshape(inputs.shape)
    return (
        out_rows,
        grad_rows,
        g_w_qkv,
        g_b_qkv,
        g_w_o,
        g_b_o,
        g_gain_one,
        g_shift_one,
        g_w_in,
        g_b_in,
        g_w_out,
        g_b_out,
        g_gain_two,
        g_shift_two,
    )


def solution(mesh):
    rows = P(AXES, None)
    vec = P(AXES)
    tok = P(None, "batch", "seq", None)
    in_specs = (
        tok,
        P(None, "batch", "seq"),
        tok,
        P(),
        rows,
        vec,
        rows,
        vec,
        vec,
        vec,
        rows,
        vec,
        rows,
        vec,
        vec,
        vec,
    )
    out_specs = (tok, tok, rows, vec, rows, vec, vec, vec, rows, vec, rows, vec, vec, vec)
    return jax.shard_map(body, mesh=mesh, in_specs=in_specs, out_specs=out_specs, check_vma=False)
```

```python
import math
from functools import partial

import jax
import jax.numpy as jnp
from jax import lax
from jax.experimental import pallas as pl
from jax.experimental.pallas import tpu as pltpu
from jax.sharding import PartitionSpec as P

norm_eps = 1e-05
bf16 = jnp.bfloat16
f32 = jnp.float32
AXES = ("batch", "seq")


def flat_xor(value, mask):
    n = lax.axis_size("batch") * lax.axis_size("seq")
    return lax.ppermute(value, AXES, [(i, i ^ mask) for i in range(n)])


def log2(n):
    return n.bit_length() - 1


def gather_order(nb, ns, swap):
    seq_bits = list(range(log2(ns)))
    batch_bits = [log2(ns) + b for b in range(log2(nb))]
    low, mid, high = seq_bits[0], seq_bits[1], seq_bits[2:]
    cross = [mid] + batch_bits if not swap else batch_bits + [mid]
    return high[::-1] + cross + [low]


def my_flat():
    return lax.axis_index("batch") * lax.axis_size("seq") + lax.axis_index("seq")


def gather_rows(shard, swap):
    nb, ns = lax.axis_size("batch"), lax.axis_size("seq")
    nbits = log2(nb * ns)
    me = my_flat()
    shape = shard.shape
    buf = shard.reshape((1,) * nbits + shape)
    for bit in gather_order(nb, ns, swap):
        axis = nbits - 1 - bit
        other = flat_xor(buf, 1 << bit)
        mine = (me >> bit) & 1
        buf = jnp.where(
            mine == 1,
            jnp.concatenate([other, buf], axis),
            jnp.concatenate([buf, other], axis),
        )
    return buf.reshape((nb * ns * shape[0],) + shape[1:])


class Scatter:
    def __init__(self, buf, swap, send=None):
        nbits = log2(lax.axis_size("batch") * lax.axis_size("seq"))
        self.bits = gather_order(lax.axis_size("batch"), lax.axis_size("seq"), swap)[::-1]
        self.send = send
        self.buf = buf if send is not None else buf.reshape((2,) * nbits + buf.shape[1:])
        self.tail = buf.shape[1:]
        self.nbits = nbits

    def step(self, beside=0.0):
        bit = self.bits.pop(0)
        axis = self.nbits - 1 - bit
        mine = (my_flat() >> bit) & 1
        if self.send is None:
            keep = lax.dynamic_index_in_dim(self.buf, mine, axis, True)
            send = lax.dynamic_index_in_dim(self.buf, 1 - mine, axis, True)
        else:
            keep, send, self.send = self.buf, self.send, None
        got = flat_xor(send, 1 << bit)
        buf = keep.astype(f32) + got.astype(f32) + beside
        if self.bits:
            buf = buf.astype(bf16)
        else:
            buf = buf.reshape(self.tail)
        if keep.ndim == 3 and self.bits:
            buf = buf.reshape((2,) * (self.nbits - 1) + (1,) + self.tail)
        self.buf = buf
        return buf

    def rest(self, beside=0.0):
        self.step(beside)
        while self.bits:
            self.step()
        return self.buf


def seq_perm(value, pairs):
    return lax.ppermute(value, "seq", pairs)


def exclusive_scan(tails, ids, rev, beside):
    beside = list(beside)
    n = lax.axis_size("seq")
    place = lax.axis_index("seq")
    if rev:
        ids = ids[::-1]
    p = n - 1 - place if rev else place

    def at(q):
        return n - 1 - q if rev else q

    def move(value, pairs):
        return seq_perm(value, [(at(a), at(b)) for a, b in pairs])

    def key(q):
        return lax.dynamic_index_in_dim(ids, jnp.clip(q, 0, n - 1), 0, False)

    def gate(a, b):
        return (key(a) == key(b)).astype(f32)

    def gated(g, value):
        return g.reshape(g.shape + (1,) * (value.ndim - 1)) * value.astype(f32)

    c = p & 1
    x = (p >> 1) & 1
    base = p - (p & 3)
    pair = p - c
    seqs = tails.shape[0]
    rest = tails.shape[2:]
    parts = tails.reshape((seqs, 2, 2) + rest)

    def pick(a, i, axis):
        return lax.dynamic_index_in_dim(a, i, axis, False)

    core = [(i, i ^ 1) for i in range(n)]
    across = [(i, i ^ 2) for i in range(n)]
    own = pick(parts, c, 2)
    other = move(pick(parts, 1 - c, 2), core)
    first = jnp.where(c == 0, own, other)
    second = jnp.where(c == 0, other, own)
    pair_sum = second.astype(f32) + gated(gate(pair, pair + 1), first)
    pair_mine = pick(pair_sum, x, 1)
    pair_other = move(pick(pair_sum, 1 - x, 1).astype(bf16), across).astype(f32)
    low = jnp.where(x == 0, pair_mine, pair_other)
    high = jnp.where(x == 0, pair_other, pair_mine)
    total = high + gated(gate(base + 1, base + 3), low)
    before = jnp.zeros_like(total)
    step = 1
    while step * 4 < n:
        total = total + (beside.pop(0) if beside else 0.0)
        got = move(
            total.astype(bf16), [(i, i + 4 * step) for i in range(n - 4 * step)]
        )
        source = base + 3 - 4 * step
        before = before + gated(gate(source, base - 1), got)
        total = total + gated(gate(source, base + 3), got)
        step *= 2
    before_high = low + gated(gate(base - 1, base + 1), before)
    mine = jnp.where(x == 0, before, before_high)
    theirs = jnp.where(x == 0, before_high, before) + sum(beside, jnp.zeros((1, 1), f32))
    got = move(theirs.astype(bf16), across)
    mine_b = mine.astype(bf16)
    entry = jnp.where(x == 0, jnp.stack([mine_b, got], 1), jnp.stack([got, mine_b], 1))
    after = first.astype(f32) + gated(gate(pair - 1, pair), entry)
    after_b = after.astype(bf16)
    mine = jnp.where(c == 0, entry, after_b)
    theirs = jnp.where(c == 0, after_b, entry)
    got = move(theirs, core)
    result = jnp.where(c == 0, jnp.stack([mine, got], 2), jnp.stack([got, mine], 2))
    return result.reshape(tails.shape)


NT = (((1,), (1,)), ((), ()))
VMEM_LIMIT = 56 * 1024 * 1024


def mm(a, b):
    return jnp.dot(a, b, preferred_element_type=f32)


def mm_nt(a, b):
    return lax.dot_general(a, b, NT, preferred_element_type=f32)


def lane_low(shape, half):
    return lax.broadcasted_iota(jnp.int32, shape, 1) < half


def half_sums(value, low):
    first = jnp.sum(jnp.where(low, value, 0.0), axis=1, keepdims=True)
    second = jnp.sum(jnp.where(low, 0.0, value), axis=1, keepdims=True)
    return first, second


def state_rows(ref, s, h, heads, d):
    per = heads // 4
    return ref[s, h // per, pl.ds((h % per) * d, d), :]


def total_rows(ref, s, heads, d):
    per = heads // 4
    out = []
    for q in range(4):
        rows = ref[s, q, pl.ds(per * d, 16), :].astype(f32)
        out += [rows[j : j + 1] for j in range(per)]
    return out


def features_kernel(
    block, heads, d, x_ref, wa_ref, wb_ref, b_ref, proj_ref, tg_ref,
    q_ref, k_ref, v_ref, phq_ref, phk_ref, tail_ref, z_scr,
):
    width = heads * d
    m = proj_ref.shape[2]
    pair = 2 * d
    scale = d ** (-0.25)
    root = m ** (-0.5)
    x = x_ref[...]
    rows = x.shape[0]
    low = lane_low((rows, pair), d)
    chunk = width // 2
    for t, (z_ref, ph_ref) in ((1, (k_ref, phk_ref)), (2, (v_ref, None)), (0, (q_ref, phq_ref))):
        for i in range(2):
            col = t * width + i * chunk
            w = wa_ref[:, col : col + chunk] if col < 3 * chunk else wb_ref[:, col - 3 * chunk : col - 2 * chunk]
            z = mm(x, w) + b_ref[:, col : col + chunk]
            z = (z * scale if ph_ref is not None else z).astype(bf16)
            z_ref[:, i * chunk : (i + 1) * chunk] = z
            if ph_ref is None:
                continue
            for p in range(chunk // pair):
                zp = z[:, p * pair : (p + 1) * pair]
                zf = zp.astype(f32)
                sums = half_sums(zf * zf, low)
                for e in range(2):
                    h = 2 * (i * (chunk // pair) + p) + e
                    u = mm(zp, proj_ref[h])
                    ph_ref[:, h * m : (h + 1) * m] = (jnp.exp(u - 0.5 * sums[e]) * root).astype(bf16)
    per = heads // 4
    for s in range(rows // block):
        r = slice(s * block, (s + 1) * block)
        tg = tg_ref[r, :].astype(bf16)
        for p in range(heads // 2):
            v_t = v_ref[r, p * pair : (p + 1) * pair].T
            for e in range(2):
                h = 2 * p + e
                kt = phk_ref[r, h * m : (h + 1) * m] * tg
                lhs = jnp.concatenate([v_t[e * d : (e + 1) * d], jnp.ones((16, block), bf16)], 0)
                res = mm(lhs, kt)
                tail_ref[s, h // per, pl.ds((h % per) * d, d), :] = res[:d].astype(bf16)
                z_scr[h % per : h % per + 1, :] = res[d : d + 1]
                if h % per == per - 1:
                    tail_ref[s, h // per, pl.ds(per * d, 16), :] = z_scr[...].astype(bf16)


def local_kernel(
    block, heads, d, phq_ref, phk_ref, v_ref, col_ref, row_ref, amat_ref, nd_ref, done_ref
):
    done_ref[...] = jnp.zeros_like(done_ref)
    m = phq_ref.shape[1] // heads
    pair = 2 * d
    low = lane_low((block, pair), d)
    t_ix = lax.broadcasted_iota(jnp.int32, (block, block), 0)
    j_ix = lax.broadcasted_iota(jnp.int32, (block, block), 1)
    causal = t_ix >= j_ix
    for s in range(v_ref.shape[0] // block):
        r = slice(s * block, (s + 1) * block)
        mask = jnp.logical_and(causal, col_ref[r, 0:1] == row_ref[s])
        for p in range(heads // 2):
            v_pair = v_ref[r, p * pair : (p + 1) * pair]
            for e in range(2):
                h = 2 * p + e
                sc = mm_nt(phq_ref[r, h * m : (h + 1) * m], phk_ref[r, h * m : (h + 1) * m])
                am = jnp.where(mask, sc, 0.0).astype(bf16)
                amat_ref[s, h] = am
                v_one = jnp.where(low if e == 0 else ~low, v_pair, jnp.ones_like(v_pair))
                nd_ref[r, h * pair : (h + 1) * pair] = mm(am, v_one)


def layer_norm(row_vals, gain, shift):
    inv = 1.0 / row_vals.shape[1]
    centred = row_vals - jnp.sum(row_vals, axis=1, keepdims=True) * inv
    rs = lax.rsqrt(jnp.sum(centred * centred, axis=1, keepdims=True) * inv + norm_eps)
    normed = centred * rs
    return normed * gain + shift, normed, rs


def layer_norm_back(dn, normed, rs):
    inv = 1.0 / dn.shape[1]
    mean = jnp.sum(dn, axis=1, keepdims=True) * inv
    proj = jnp.sum(dn * normed, axis=1, keepdims=True) * inv
    return rs * (dn - mean - normed * proj)


def group_rows(shard_rows):
    return math.lcm(shard_rows, 16) // shard_rows


def natural_rows(stage, out_ref, shard_rows, width):
    groups = stage.shape[1] // width
    per = group_rows(shard_rows)
    unit = per * shard_rows

    def one(i, carry):
        cols = [
            stage[pl.ds(pl.multiple_of(i * unit, 16), unit), g * width : (g + 1) * width]
            for g in range(groups)
        ]
        pieces = [c[j * shard_rows : (j + 1) * shard_rows] for j in range(per) for c in cols]
        out_ref[pl.ds(pl.multiple_of(i * unit * groups, 16), unit * groups), :] = jnp.concatenate(
            pieces, axis=0
        )
        return carry

    lax.fori_loop(0, stage.shape[0] // unit, one, 0)


def middle_kernel(
    block, heads, d, ff_chunk,
    shard_rows, x_ref, cot_ref, phq_ref, nd_ref, pre_ref, gate_ref, others_hbm, w_out_hbm,
    b_in_ref, vec_ref,
    y_ref, dr1_ref, dnum_ref, dden_ref, dpre_ref, attn_ref, dao_ref, h1_ref, act_ref, dfo_ref,
    df_ref, sums_ref, sum_in_ref,
    attf, rden, dgel, z_scr, w_o_ref, w_in_ref, w_out_ref, stage, sems,
):
    step = pl.program_id(0)
    m = phq_ref.shape[1] // heads
    width = heads * d
    ff = w_in_ref.shape[1]

    def copies():
        out = [
            pltpu.make_async_copy(others_hbm.at[:, pl.ds(0, width)], w_o_ref, sems.at[0]),
            pltpu.make_async_copy(others_hbm.at[:, pl.ds(width, ff)], w_in_ref, sems.at[1]),
        ]
        if shard_rows:
            src, dst = others_hbm.at[:, pl.ds(width + ff, ff)], stage
        else:
            src, dst = w_out_hbm, w_out_ref
        return out + [pltpu.make_async_copy(src, dst, sems.at[2])]

    @pl.when(step == 0)
    def _():
        for c in copies():
            c.start()

    pair = 2 * d
    low = lane_low((block, pair), d)
    rows = x_ref.shape[0]
    seqs = rows // block
    ones = jnp.ones((d, 1), f32)
    for s in range(seqs):
        r = slice(s * block, (s + 1) * block)
        g = gate_ref[r, 2:3]
        zs = total_rows(pre_ref, s, heads, d)
        for p in range(heads // 2):
            tot = []
            for e in range(2):
                h = 2 * p + e
                st = state_rows(pre_ref, s, h, heads, d)
                zb = (ones * zs[h]).astype(bf16)
                rhs = jnp.concatenate([st, zb] if e == 0 else [zb, st], 0)
                tot.append(
                    nd_ref[r, h * pair : (h + 1) * pair]
                    + g * mm_nt(phq_ref[r, h * m : (h + 1) * m], rhs)
                )
            num = jnp.where(low, tot[0], tot[1])
            den = pltpu.roll(jnp.where(low, tot[1], tot[0]), d, 1)
            rd = 1.0 / den
            c = slice(p * pair, (p + 1) * pair)
            att = num * rd
            attf[r, c] = att
            rden[r, c] = rd
            attn_ref[r, c] = att.astype(bf16)
    b_o, gain1, shift1, b_out, gain2, shift2 = (vec_ref[i : i + 1, :] for i in range(6))

    @pl.when(step == 0)
    def _():
        for c in copies():
            c.wait()
        if shard_rows:
            natural_rows(stage, w_out_ref, shard_rows, width)

    r1 = x_ref[...].astype(f32) + mm(attn_ref[...], w_o_ref[...]) + b_o
    h1, n1, rs1 = layer_norm(r1, gain1, shift1)
    h1b = h1.astype(bf16)
    h1_ref[...] = h1b
    fo = None
    for c0 in range(0, ff, ff_chunk):
        c = slice(c0, c0 + ff_chunk)
        f = mm(h1b, w_in_ref[:, c]) + b_in_ref[:, c]
        phi = 0.5 + 0.5 * lax.erf(f * (0.5**0.5))
        act = (f * phi).astype(bf16)
        act_ref[:, c] = act
        dgel[:, c] = phi + f * (jnp.exp(-0.5 * f * f) * (1.0 / (2.0 * math.pi) ** 0.5))
        part = mm(act, w_out_ref[c, :])
        fo = part if fo is None else fo + part
    y, n2, rs2 = layer_norm(h1 + fo + b_out, gain2, shift2)
    y_ref[...] = y.astype(bf16)
    dy = cot_ref[...].astype(f32)

    def add_sum(i, value):
        row = jnp.sum(value, axis=0, keepdims=True)

        @pl.when(step == 0)
        def _():
            sums_ref[i : i + 1, :] = row

        @pl.when(step > 0)
        def _():
            sums_ref[i : i + 1, :] += row

    add_sum(4, dy * n2)
    add_sum(5, dy)
    dr2 = layer_norm_back(dy * gain2, n2, rs2)
    dfo = dr2.astype(bf16)
    dfo_ref[...] = dfo
    add_sum(3, dfo.astype(f32))
    dh1 = dr2
    for c0 in range(0, ff, ff_chunk):
        c = slice(c0, c0 + ff_chunk)
        df = (mm_nt(dfo, w_out_ref[c, :]) * dgel[:, c]).astype(bf16)
        df_ref[:, c] = df
        row = jnp.sum(df.astype(f32), axis=0, keepdims=True)

        @pl.when(step == 0)
        def _():
            sum_in_ref[:, c] = row

        @pl.when(step > 0)
        def _():
            sum_in_ref[:, c] += row

        dh1 = dh1 + mm_nt(df, w_in_ref[:, c])
    add_sum(1, dh1 * n1)
    add_sum(2, dh1)
    dr1 = layer_norm_back(dh1 * gain1, n1, rs1)
    dr1_ref[...] = dr1
    dao = dr1.astype(bf16)
    dao_ref[...] = dao
    add_sum(0, dao.astype(f32))
    dattn = mm_nt(dao, w_o_ref[...])
    dnum_ref[...] = (dattn * rden[...]).astype(bf16)
    prod = dattn * attf[...]
    lane = lax.broadcasted_iota(jnp.int32, (rows, 128), 1)
    low_rows = lane_low((rows, pair), d)
    dden = jnp.zeros((rows, 128), f32)
    for p in range(heads // 2):
        c = slice(p * pair, (p + 1) * pair)
        sums = half_sums(prod[:, c], low_rows)
        for e in range(2):
            col = -sums[e] * rden[:, p * pair + e * d : p * pair + e * d + 1]
            dden = jnp.where(lane == 2 * p + e, col, dden)
    dden = dden.astype(bf16).astype(f32)
    dden_ref[...] = dden
    per = heads // 4
    for s in range(seqs):
        r = slice(s * block, (s + 1) * block)
        g = gate_ref[r, 2:3]
        ddt = (dden[r] * g).T[:16].astype(bf16)
        for p in range(heads // 2):
            gdt = (dnum_ref[r, p * pair : (p + 1) * pair] * g.astype(bf16)).T
            for e in range(2):
                h = 2 * p + e
                lhs = jnp.concatenate([gdt[e * d : (e + 1) * d], ddt], 0)
                res = mm(lhs, phq_ref[r, h * m : (h + 1) * m])
                dpre_ref[s, h // per, pl.ds((h % per) * d, d), :] = res[:d].astype(bf16)
                z_scr[h % per : h % per + 1, :] = res[d + h : d + h + 1]
                if h % per == per - 1:
                    dpre_ref[s, h // per, pl.ds(per * d, 16), :] = z_scr[...].astype(bf16)


def back_query_kernel(
    block, heads, d,
    q_ref, v_ref, phq_ref, phk_ref, amat_ref, dnum_ref, dden_ref, pre_ref, gate_ref, row_ref,
    proj_ref,
    dq_ref, dv_ref, dsct_ref, done_ref,
):
    done_ref[...] = jnp.zeros_like(done_ref)
    m = phq_ref.shape[1] // heads
    pair = 2 * d
    scale = d ** (-0.25)
    low = lane_low((block, pair), d)
    t_ix = lax.broadcasted_iota(jnp.int32, (block, block), 0)
    j_ix = lax.broadcasted_iota(jnp.int32, (block, block), 1)
    causal = t_ix >= j_ix
    for s in range(q_ref.shape[0] // block):
        r = slice(s * block, (s + 1) * block)
        g = gate_ref[r, 2:3]
        gb = g.astype(bf16)
        mask = jnp.logical_and(causal, gate_ref[r, 0:1] == row_ref[s])
        zs = total_rows(pre_ref, s, heads, d)
        for p in range(heads // 2):
            c = slice(p * pair, (p + 1) * pair)
            dn = dnum_ref[r, c]
            v_pair = v_ref[r, c]
            qp = q_ref[r, c].astype(f32)
            st = jnp.concatenate(
                [state_rows(pre_ref, s, 2 * p, heads, d), state_rows(pre_ref, s, 2 * p + 1, heads, d)], 0
            )
            dv = None
            dq = None
            for e in range(2):
                h = 2 * p + e
                mine = low if e == 0 else ~low
                hm = slice(h * m, (h + 1) * m)
                dnm = jnp.where(mine, dn, jnp.zeros_like(dn))
                dd = dden_ref[r, h : h + 1]
                dsc = jnp.where(mask, mm_nt(dnm, v_pair) + dd, 0.0)
                dsct_ref[s, h] = dsc.T.astype(bf16)
                dph = mm(
                    jnp.concatenate([dsc.astype(bf16), dnm * gb], 1),
                    jnp.concatenate([phk_ref[r, hm], st], 0),
                ) + (g * dd) * zs[h]
                t = dph * phq_ref[r, hm].astype(f32)
                part = mm_nt(t.astype(bf16), proj_ref[h]) - jnp.where(
                    mine, jnp.sum(t, axis=1, keepdims=True) * qp, 0.0
                )
                dq = part if dq is None else dq + part
                part = mm(amat_ref[s, h].T, dnm)
                dv = part if dv is None else dv + part
            dq_ref[r, c] = (dq * scale).astype(bf16)
            dv_ref[r, c] = dv


def back_key_kernel(
    block, heads, d,
    k_ref, v_ref, phq_ref, phk_ref, dv_ref, dsct_ref, dtail_ref, gate_ref, proj_ref,
    dkv_ref,
):
    m = phq_ref.shape[1] // heads
    pair = 2 * d
    width = heads * d
    scale = d ** (-0.25)
    low = lane_low((block, pair), d)
    for s in range(k_ref.shape[0] // block):
        r = slice(s * block, (s + 1) * block)
        tg = gate_ref[r, 1:2]
        tgb = tg.astype(bf16)
        zs = total_rows(dtail_ref, s, heads, d)
        for p in range(heads // 2):
            c = slice(p * pair, (p + 1) * pair)
            v_pair = v_ref[r, c]
            kp = k_ref[r, c].astype(f32)
            ds = jnp.concatenate(
                [
                    state_rows(dtail_ref, s, 2 * p, heads, d),
                    state_rows(dtail_ref, s, 2 * p + 1, heads, d),
                ],
                0,
            )
            dk = None
            inter = []
            for e in range(2):
                h = 2 * p + e
                mine = low if e == 0 else ~low
                hm = slice(h * m, (h + 1) * m)
                vm = jnp.where(mine, v_pair, jnp.zeros_like(v_pair)) * tgb
                phk = phk_ref[r, hm]
                dph = mm(
                    jnp.concatenate([dsct_ref[s, h], vm], 1),
                    jnp.concatenate([phq_ref[r, hm], ds], 0),
                ) + tg * zs[h]
                t = dph * phk.astype(f32)
                part = mm_nt(t.astype(bf16), proj_ref[h]) - jnp.where(
                    mine, jnp.sum(t, axis=1, keepdims=True) * kp, 0.0
                )
                dk = part if dk is None else dk + part
                inter.append(mm_nt(phk, ds))
            dkv_ref[r, c] = (dk * scale).astype(bf16)
            dv = dv_ref[r, c] + tg * jnp.where(low, inter[0], inter[1])
            dkv_ref[r, width + p * pair : width + (p + 1) * pair] = dv.astype(bf16)


def params(micros):
    return dict(
        compiler_params=pltpu.CompilerParams(
            dimension_semantics=("arbitrary",), vmem_limit_bytes=VMEM_LIMIT
        ),
        cost_estimate=pl.CostEstimate(
            flops=int(micros * 1e9), bytes_accessed=int(micros * 1e6), transcendentals=0
        ),
    )


def row_spec(rows, cols):
    return pl.BlockSpec((rows, cols), lambda i: (i, 0))


def lead_spec(shape):
    return pl.BlockSpec(shape, lambda i: (i,) + (0,) * (len(shape) - 1))


def whole_spec(shape):
    return pl.BlockSpec(shape, lambda i: (0,) * len(shape))


def sds(shape, dtype):
    return jax.ShapeDtypeStruct(shape, dtype)


STEP_SEQS = 2
STATE_PAD = 16


def state_shape(seqs, heads, d, m):
    return (seqs, 4, heads // 4 * d + STATE_PAD, m)


def call_features(x, wa, wb, b, proj, tg, block, heads, d):
    rows, width = x.shape
    m = proj.shape[2]
    n = STEP_SEQS * block
    st = state_shape(STEP_SEQS, heads, d, m)
    return pl.pallas_call(
        partial(features_kernel, block, heads, d),
        grid=(rows // n,),
        in_specs=[
            row_spec(n, width), whole_spec(wa.shape), whole_spec(wb.shape), whole_spec(b.shape),
            whole_spec(proj.shape), row_spec(n, 1),
        ],
        out_specs=[row_spec(n, width)] * 3 + [row_spec(n, heads * m)] * 2 + [lead_spec(st)],
        out_shape=[sds((rows, width), bf16)] * 3
        + [sds((rows, heads * m), bf16)] * 2
        + [sds((rows // block,) + st[1:], bf16)],
        scratch_shapes=[pltpu.VMEM((16, m), f32)],
        name="features",
        **params(10),
    )(x, wa, wb, b, proj, tg)


def call_local(phq, phk, v, gates, id_rows, block, heads, d):
    rows = v.shape[0]
    n = STEP_SEQS * block
    return pl.pallas_call(
        partial(local_kernel, block, heads, d),
        grid=(rows // n,),
        in_specs=[
            row_spec(n, phq.shape[1]), row_spec(n, phk.shape[1]), row_spec(n, v.shape[1]),
            row_spec(n, gates.shape[1]), lead_spec((STEP_SEQS, 1, block)),
        ],
        out_specs=[
            lead_spec((STEP_SEQS, heads, block, block)), row_spec(n, heads * 2 * d),
            whole_spec((1, 1)),
        ],
        out_shape=[
            sds((rows // block, heads, block, block), bf16), sds((rows, heads * 2 * d), f32),
            sds((1, 1), f32),
        ],
        name="local",
        **params(8),
    )(phq, phk, v, gates, id_rows)


def call_middle(x, cot, phq, nd, pre, gates, others, w_out, shard_rows, b_in, vec, block, heads, d):
    rows, width = x.shape
    ff = b_in.shape[1]
    m = phq.shape[1] // heads
    n = STEP_SEQS * block
    st = (STEP_SEQS,) + pre.shape[1:]
    return pl.pallas_call(
        partial(middle_kernel, block, heads, d, 768, shard_rows),
        grid=(rows // n,),
        in_specs=[
            row_spec(n, width), row_spec(n, width), row_spec(n, phq.shape[1]),
            row_spec(n, nd.shape[1]), lead_spec(st), row_spec(n, gates.shape[1]),
            pl.BlockSpec(memory_space=pl.ANY), pl.BlockSpec(memory_space=pl.ANY),
            whole_spec(b_in.shape), whole_spec(vec.shape),
        ],
        out_specs=[
            row_spec(n, width), row_spec(n, width), row_spec(n, width), row_spec(n, 128),
            lead_spec(st), row_spec(n, width), row_spec(n, width), row_spec(n, width),
            row_spec(n, ff), row_spec(n, width), row_spec(n, ff), whole_spec((8, width)),
            whole_spec((1, ff)),
        ],
        out_shape=[
            sds((rows, width), bf16), sds((rows, width), f32), sds((rows, width), bf16),
            sds((rows, 128), f32), sds(pre.shape, bf16), sds((rows, width), bf16),
            sds((rows, width), bf16), sds((rows, width), bf16), sds((rows, ff), bf16),
            sds((rows, width), bf16), sds((rows, ff), bf16), sds((8, width), f32),
            sds((1, ff), f32),
        ],
        scratch_shapes=[
            pltpu.VMEM((n, width), f32), pltpu.VMEM((n, width), f32), pltpu.VMEM((n, ff), f32),
            pltpu.VMEM((16, m), f32), pltpu.VMEM((width, width), bf16),
            pltpu.VMEM((width, ff), bf16), pltpu.VMEM((ff, width), bf16),
            pltpu.VMEM((width, ff) if shard_rows else (16, 128), bf16),
            pltpu.SemaphoreType.DMA((3,)),
        ],
        name="middle",
        **params(31),
    )(x, cot, phq, nd, pre, gates, others, w_out, b_in, vec)


def call_back_query(
    half, q, v, phq, phk, amat, dnum, dden, pre, gates, id_rows, proj, ties, block, heads, d
):
    rows, width = q.shape
    n = STEP_SEQS * block
    sq = (STEP_SEQS, heads, block, block)

    def rs(cols):
        return pl.BlockSpec((n, cols), lambda i: (half, 0))

    def ls(shape):
        return pl.BlockSpec(shape, lambda i: (half,) + (0,) * (len(shape) - 1))

    def kernel(*refs):
        back_query_kernel(block, heads, d, *refs[:11], *refs[11 + len(ties) :])

    return pl.pallas_call(
        kernel,
        grid=(1,),
        in_specs=[
            rs(width), rs(width), rs(phq.shape[1]), rs(phk.shape[1]), ls(sq), rs(width), rs(128),
            ls((STEP_SEQS,) + pre.shape[1:]), rs(gates.shape[1]), ls((STEP_SEQS, 1, block)),
            whole_spec(proj.shape),
        ]
        + [pl.BlockSpec(memory_space=pl.ANY)] * len(ties),
        out_specs=[row_spec(n, width), row_spec(n, width), lead_spec(sq), whole_spec((1, 1))],
        out_shape=[
            sds((n, width), bf16), sds((n, width), f32), sds(sq, bf16), sds((1, 1), f32),
        ],
        name="back_query",
        **params(8),
    )(q, v, phq, phk, amat, dnum, dden, pre, gates, id_rows, proj, *ties)


def call_back_key(k, v, phq, phk, dvs, dscts, dtail, gates, proj, ties, block, heads, d):
    rows, width = k.shape
    n = STEP_SEQS * block
    sq = (STEP_SEQS, heads, block, block)
    steps = rows // n

    def kernel(k_ref, v_ref, phq_ref, phk_ref, *refs):
        for i in range(steps):

            @pl.when(pl.program_id(0) == i)
            def _():
                back_key_kernel(
                    block, heads, d, k_ref, v_ref, phq_ref, phk_ref, refs[i], refs[steps + i],
                    *refs[2 * steps : 2 * steps + 3], refs[-1],
                )

    return pl.pallas_call(
        kernel,
        grid=(steps,),
        in_specs=[
            row_spec(n, width), row_spec(n, width), row_spec(n, phq.shape[1]),
            row_spec(n, phk.shape[1]),
        ]
        + [whole_spec((n, width))] * steps
        + [whole_spec(sq)] * steps
        + [
            lead_spec((STEP_SEQS,) + dtail.shape[1:]), row_spec(n, gates.shape[1]),
            whole_spec(proj.shape),
        ]
        + [pl.BlockSpec(memory_space=pl.ANY)] * len(ties),
        out_specs=row_spec(n, 2 * width),
        out_shape=sds((rows, 2 * width), bf16),
        name="back_key",
        **params(13),
    )(k, v, phq, phk, *dvs, *dscts, dtail, gates, proj, *ties)


TN = (((0,), (0,)), ((), ()))


def mm_tn(a, b):
    return lax.dot_general(a, b, TN, preferred_element_type=f32)


def pack_kernel(shard_rows, w_o_ref, w_in_ref, w_out_ref, out_ref):
    width, ff = w_o_ref.shape[1], w_in_ref.shape[1]
    out_ref[:, :width] = w_o_ref[...]
    out_ref[:, width : width + ff] = w_in_ref[...]
    rows = w_out_ref[...]
    for g in range(rows.shape[0] // shard_rows):
        c = width + ff + g * width
        out_ref[:, c : c + width] = rows[g * shard_rows : (g + 1) * shard_rows]


def call_pack(w_o, w_in, w_out):
    cols = w_o.shape[1] + w_in.shape[1] + w_out.size // w_o.shape[0]
    return pl.pallas_call(
        partial(pack_kernel, w_o.shape[0]),
        out_shape=sds((w_o.shape[0], cols), bf16),
        name="pack",
    )(w_o, w_in, w_out)


def part_store(core, refs, index, value):
    kept, sent, rows, cols = refs
    (kept if index % 2 == core else sent)[index // 2, rows, cols] = value


def by_core(kernel, core_ref):
    for core in range(2):
        pl.when(core_ref[0] == core)(partial(kernel, core))


def grads_kernel(
    shard_rows, core_ref, attn_ref, dao_ref, h1_ref, df_ref, act_ref, dfo_ref, vec_ref,
    keep_i, send_i, keep_o, send_o, done_ref,
):
    done_ref[...] = jnp.zeros_like(done_ref)
    by_core(
        partial(
            grads_parts, shard_rows, attn_ref, dao_ref, h1_ref, df_ref, act_ref, dfo_ref, vec_ref,
            keep_i, send_i, keep_o, send_o,
        ),
        core_ref,
    )


def grads_parts(
    shard_rows, attn_ref, dao_ref, h1_ref, df_ref, act_ref, dfo_ref, vec_ref,
    keep_i, send_i, keep_o, send_o, core,
):
    width = dao_ref.shape[1]
    ff = df_ref.shape[1]
    groups = ff // width
    tall = groups * shard_rows
    count = vec_ref.shape[0]
    every = slice(None)
    dfo = dfo_ref[...]
    chunk = act_ref.shape[1] // groups
    per = chunk // tall
    for c in range(groups):
        res = mm_tn(act_ref[:, c * chunk : (c + 1) * chunk], dfo).astype(bf16)
        for j in range(per):
            part_store(
                core, (keep_o, send_o, slice(0, tall), every), c * per + j,
                res[j * tall : (j + 1) * tall],
            )
    res = mm_tn(attn_ref[...], dao_ref[...]).astype(bf16)
    for j in range(count):
        part_store(
            core, (keep_o, send_o, slice(tall, tall + shard_rows), every), j,
            res[j * shard_rows : (j + 1) * shard_rows],
        )
    h1 = h1_ref[...]
    for g in range(groups):
        res = mm_tn(h1, df_ref[:, g * width : (g + 1) * width]).astype(bf16)
        for j in range(count):
            part_store(
                core, (keep_i, send_i, every, slice(g * width, (g + 1) * width)), j,
                res[j * shard_rows : (j + 1) * shard_rows],
            )
    for j in range(count):
        part_store(core, (keep_i, send_i, every, slice(ff, ff + vec_ref.shape[2])), j, vec_ref[j])


def call_grads(core, attn, dao, h1, df, act, dfo, vec, shard_rows):
    rows, width = dao.shape
    ff = df.shape[1]
    steps = 2
    n_dev = width // shard_rows
    small = (n_dev // 2, shard_rows, ff + vec.shape[2])
    tall = (n_dev // 2, shard_rows * (ff // width + 1), width)

    def cut(shape):
        return lead_spec((shape[0] // steps,) + shape[1:])

    return pl.pallas_call(
        partial(grads_kernel, shard_rows),
        grid=(steps,),
        in_specs=[
            pl.BlockSpec(memory_space=pltpu.SMEM),
            pl.BlockSpec((rows, width // steps), lambda i: (0, i)), whole_spec(dao.shape),
            pl.BlockSpec((rows, width // steps), lambda i: (0, i)), whole_spec(df.shape),
            pl.BlockSpec((rows, ff // steps), lambda i: (0, i)), whole_spec(dfo.shape),
            cut(vec.shape),
        ],
        out_specs=[cut(small), cut(small), cut(tall), cut(tall), whole_spec((1, 1))],
        out_shape=[sds(small, bf16), sds(small, bf16), sds(tall, bf16), sds(tall, bf16)]
        + [sds((1, 1), f32)],
        name="grads",
        **params(10),
    )(core, attn, dao, h1, df, act, dfo, vec)


def first_grads_kernel(
    shard_rows, ties, core_ref, x_ref, dq_ref, dkv_ref, *refs
):
    by_core(partial(first_grads_parts, shard_rows, x_ref, dq_ref, dkv_ref, *refs[ties:]), core_ref)


def first_grads_parts(
    shard_rows, x_ref, dq_ref, dkv_ref, keep_a, send_a, keep_b, send_b, core
):
    width = dq_ref.shape[1]
    chunk = width // 2
    x = x_ref[...]
    step = pl.program_id(0)
    count = x_ref.shape[1] // shard_rows
    n_dev = 2 * count
    every = slice(None)
    sums = []
    for i in range(6):
        src, c0 = (dq_ref, i * chunk) if i < 2 else (dkv_ref, (i - 2) * chunk)
        b = src[:, c0 : c0 + chunk]
        sums.append(jnp.sum(b.astype(f32), axis=0, keepdims=True))
        res = mm_tn(x, b).astype(bf16)
        refs = (keep_a, send_a) if i < 3 else (keep_b, send_b)
        cols = slice((i % 3) * chunk, (i % 3 + 1) * chunk)
        for j in range(count):
            part_store(core, refs + (every, cols), j, res[j * shard_rows : (j + 1) * shard_rows])
    total = 3 * width
    piece = total // n_dev
    row = jnp.broadcast_to(jnp.concatenate(sums, axis=1), (8, total))
    first = lax.broadcasted_iota(jnp.int32, (shard_rows, 128), 0) == 0
    for j in range(count):
        two = [
            pltpu.roll(row, (total - piece * (j + i * count)) % total, 1)[:1, :128] for i in range(2)
        ]
        mine = jnp.where(first, jnp.where(step == 0, two[0], two[1]), 0.0).astype(bf16)
        part_store(core, (keep_a, send_a, every, slice(3 * chunk, 3 * chunk + 128)), j, mine)


def call_first_grads(core, x, dq, dkv, ties, shard_rows):
    rows, width = x.shape
    steps = 2
    half = 3 * width // 2
    n_dev = width // shard_rows
    shapes = [(n_dev // 2, shard_rows, half + 128)] * 2 + [(n_dev // 2, shard_rows, half)] * 2
    return pl.pallas_call(
        partial(first_grads_kernel, shard_rows, len(ties)),
        grid=(steps,),
        in_specs=[
            pl.BlockSpec(memory_space=pltpu.SMEM),
            pl.BlockSpec((rows, width // steps), lambda i: (0, i)), whole_spec(dq.shape),
            whole_spec(dkv.shape),
        ]
        + [pl.BlockSpec(memory_space=pl.ANY)] * len(ties),
        out_specs=[lead_spec((t[0] // steps,) + t[1:]) for t in shapes],
        out_shape=[sds(t, bf16) for t in shapes],
        name="first_grads",
        **params(6),
    )(core, x, dq, dkv, *ties)


def input_grad_kernel(dq_ref, dkv_ref, wa_ref, wb_ref, dr1_ref, out_ref, done_ref):
    done_ref[...] = jnp.zeros_like(done_ref)
    width = dq_ref.shape[1]
    chunk = width // 2
    acc = dr1_ref[...]
    for i in range(6):
        src, c0 = (dq_ref, i * chunk) if i < 2 else (dkv_ref, (i - 2) * chunk)
        w_ref = wa_ref if i < 3 else wb_ref
        acc = acc + mm_nt(src[:, c0 : c0 + chunk], w_ref[:, (i % 3) * chunk : (i % 3 + 1) * chunk])
    out_ref[...] = acc.astype(bf16)


def call_input_grad(dq, dkv, wa, wb, dr1, n):
    rows, width = dq.shape
    return pl.pallas_call(
        input_grad_kernel,
        grid=(rows // n,),
        in_specs=[
            row_spec(n, width), row_spec(n, 2 * width), whole_spec(wa.shape), whole_spec(wb.shape),
            row_spec(n, width),
        ],
        out_specs=[row_spec(n, width), whole_spec((1, 1))],
        out_shape=[sds((rows, width), bf16), sds((1, 1), f32)],
        name="input_grad",
        **params(6),
    )(dq, dkv, wa, wb, dr1)


def body(
    inputs,
    seg_ids,
    cotangent,
    projection,
    w_qkv,
    b_qkv,
    w_o,
    b_o,
    ln1_gain,
    ln1_bias,
    w_in,
    b_in,
    w_out,
    b_out,
    ln2_gain,
    ln2_bias,
):
    micro, seqs_micro, block, width = inputs.shape
    heads, d, m = projection.shape
    n_seq = lax.axis_size("seq")
    n_dev = lax.axis_size("batch") * n_seq
    place = lax.axis_index("seq")
    seqs = micro * seqs_micro
    rows = seqs * block

    vectors = (b_qkv, b_o, ln1_gain, ln1_bias, b_in, b_out, ln2_gain, ln2_bias)
    sizes = [v.shape[0] for v in vectors]
    cuts = [sum(sizes[:i]) for i in range(len(sizes) + 1)]
    idents = seg_ids.reshape(seqs, block)
    shard_rows = w_qkv.shape[0]
    tiled = shard_rows % 8 == 0
    carried = vectors + (idents[:, -1].astype(bf16),)
    if tiled:
        flat = jnp.stack([jnp.pad(t, (0, 128 - t.shape[0])) for t in carried])
        cuts = [128 * i for i in range(len(carried) + 1)]
    else:
        flat = jnp.concatenate(carried)
        flat = jnp.pad(flat, (0, -flat.shape[0] % 128)).reshape(-1, 128)
    used = flat.shape[0]
    flat = jnp.pad(flat, ((0, shard_rows - used), (0, 0)))
    half = w_qkv.shape[1] // 2
    w_a = gather_rows(jnp.concatenate([w_qkv[:, :half], flat], axis=1), False)
    w_b = gather_rows(w_qkv[:, half:], True)
    packed = w_a[:, half:].reshape(n_dev, shard_rows, 128)[:, :used]
    b_qkv_f = packed[:, 0, : sizes[0]].reshape(1, -1).astype(f32)
    packed = packed.reshape(n_dev, -1)
    (b_o_f, gain_one, shift_one, b_in_f, b_out_f, gain_two, shift_two) = (
        packed[:, cuts[i] : cuts[i] + sizes[i]].reshape(1, -1).astype(f32)
        for i in range(1, len(sizes))
    )
    at = cuts[len(sizes)]
    ids_all = packed[:, at : at + seqs].reshape(-1, n_seq, seqs).astype(f32)
    last_all = lax.dynamic_index_in_dim(ids_all, lax.axis_index("batch"), 0, False)

    f_cols = w_in.shape[1]
    groups = w_out.shape[0] // shard_rows
    if tiled:
        others = call_pack(w_o, w_in, w_out)
    else:
        others = jnp.concatenate(
            [w_o, w_in] + [w_out[i * shard_rows : (i + 1) * shard_rows] for i in range(groups)],
            axis=1,
        )
    others = lax.all_gather(others, AXES, axis=0, tiled=True)
    w_out_f = others
    if not tiled:
        w_out_f = (
            others[:, width + f_cols :]
            .reshape(n_dev, shard_rows, groups, width)
            .transpose(0, 2, 1, 3)
            .reshape(-1, width)
        )

    pre_all = jnp.concatenate([-jnp.ones_like(last_all[:1]), last_all[:-1]], axis=0)
    pre_ident = lax.dynamic_index_in_dim(pre_all, place, 0, False)
    idents_f = idents.astype(f32)
    tail_gate = (idents_f == idents_f[:, -1:]).astype(f32)
    gates = jnp.stack(
        [
            idents_f,
            tail_gate,
            (idents_f == pre_ident[:, None]).astype(f32),
        ],
        axis=-1,
    ).reshape(rows, 3)
    gates = jnp.pad(gates, ((0, 0), (0, 5)))
    id_rows = idents_f[:, None, :]
    zero = jnp.zeros_like(projection[::2])
    proj = jnp.stack(
        [
            jnp.concatenate([projection[0::2], zero], axis=1),
            jnp.concatenate([zero, projection[1::2]], axis=1),
        ],
        axis=1,
    ).reshape(heads, 2 * d, m)

    x = inputs.reshape(rows, width)
    dims = (block, heads, d)
    q, k, v, phq, phk, tails = call_features(
        x, w_a, w_b, b_qkv_f, proj, tail_gate.reshape(rows, 1), *dims
    )
    amat, nd, done = call_local(phq, phk, v, gates, id_rows, *dims)
    pre = exclusive_scan(tails, last_all, False, (done,))
    vec = jnp.concatenate([b_o_f, gain_one, shift_one, b_out_f, gain_two, shift_two] + [b_o_f] * 2)
    (y, dr1, dnum, dden, dpre, attn, dao, h1, act, dfo, df, sums, sum_in) = call_middle(
        x, cotangent.reshape(rows, width), phq, nd, pre, gates, others, w_out_f,
        shard_rows if tiled else 0, b_in_f, vec, *dims,
    )
    core = (place & 1).astype(jnp.int32).reshape(1)

    def grad(a, b):
        return mm_tn(a, b).astype(bf16)

    vec_grads = (sums[0], sums[1], sums[2], sum_in[0], sums[3], sums[4], sums[5])
    pieces = [t.reshape(n_dev, -1) for t in vec_grads]
    if tiled:
        vec = jnp.stack([jnp.pad(t, ((0, 0), (0, 128 - t.shape[1]))) for t in pieces], axis=1)
        places = [128 * i for i in range(len(pieces))]
    else:
        vec = jnp.concatenate(pieces, axis=1)
        vec = jnp.pad(vec, ((0, 0), (0, -vec.shape[1] % 128))).reshape(n_dev, -1, 128)
        places = [cuts[i] - cuts[1] for i in range(1, len(sizes))]
    used = vec.shape[1]
    vec = jnp.pad(vec, ((0, 0), (0, shard_rows - used), (0, 0))).astype(bf16)
    beside = ()
    if tiled:
        keep_i, send_i, keep_o, send_o, done = call_grads(
            core, attn, dao, h1, df, act, dfo, vec, shard_rows
        )
        beside = (done,)
        scatter_i = Scatter(keep_i, True, send_i)
        scatter_o = Scatter(keep_o, True, send_o)
    else:
        scatter_i = Scatter(
            jnp.concatenate([grad(h1, df).reshape(n_dev, shard_rows, -1), vec], axis=2), True
        )
        tall = jnp.concatenate(
            [
                grad(act, dfo).reshape(n_dev, -1, width),
                grad(attn, dao).reshape(n_dev, -1, width),
            ],
            axis=1,
        )
        scatter_o = Scatter(tall, True)
    ties = [(), (scatter_i.step(), scatter_o.step())]
    halves = [
        call_back_query(
            i, q, v, phq, phk, amat, dnum, dden, pre, gates, id_rows, proj,
            ties[i] if i < len(ties) else (), *dims
        )
        for i in range(seqs // STEP_SEQS)
    ]
    dqs, dvs, dscts, dones = zip(*halves)
    back = exclusive_scan(dpre, pre_all, True, beside + tuple(dones))
    dq = jnp.concatenate(dqs)
    ties = (scatter_i.step(),)
    dkv = call_back_key(k, v, phq, phk, dvs, dscts, back, gates, proj, ties, *dims)
    dx, done = call_input_grad(dq, dkv, w_a, w_b, dr1, STEP_SEQS * block)
    ties = (scatter_o.step(),)
    if tiled:
        keep_a, send_a, keep_b, send_b = call_first_grads(core, x, dq, dkv, ties, shard_rows)
        scatter_a = Scatter(keep_a, False, send_a)
        scatter_b = Scatter(keep_b, True, send_b)
    else:
        dqkv = jnp.concatenate([dq, dkv], axis=1)
        gw = grad(x, dqkv).reshape(n_dev, shard_rows, -1)
        vec = jnp.sum(dqkv, axis=0, dtype=f32).reshape(n_dev, 1, -1)
        vec = jnp.pad(vec, ((0, 0), (0, shard_rows - 1), (0, 128 - sizes[0]))).astype(bf16)
        scatter_a = Scatter(jnp.concatenate([gw[:, :, :half], vec], axis=2), False)
        scatter_b = Scatter(gw[:, :, half:], True)
    scatter_a.step()
    scatter_b.step()
    part_a = scatter_a.rest(done)
    part_b = scatter_b.rest(done)
    part_i = scatter_i.rest()
    part_o = scatter_o.rest()
    g_w_out, g_w_o = part_o[: w_out.shape[0]], part_o[w_out.shape[0] :]
    g_w_in = part_i[:, :f_cols]
    vec = part_i[:used, f_cols:].reshape(-1)
    (g_b_o, g_gain_one, g_shift_one, g_b_in, g_b_out, g_gain_two, g_shift_two) = (
        vec[at : at + size] for at, size in zip(places, sizes[1:])
    )
    g_w_qkv = jnp.concatenate([part_a[:, :half], part_b], axis=1)
    g_b_qkv = part_a[0, half : half + sizes[0]]
    return (
        y.reshape(inputs.shape),
        dx.reshape(inputs.shape),
        g_w_qkv,
        g_b_qkv,
        g_w_o,
        g_b_o,
        g_gain_one,
        g_shift_one,
        g_w_in,
        g_b_in,
        g_w_out,
        g_b_out,
        g_gain_two,
        g_shift_two,
    )


def solution(mesh):
    rows = P(AXES, None)
    vec = P(AXES)
    tok = P(None, "batch", "seq", None)
    in_specs = (
        tok,
        P(None, "batch", "seq"),
        tok,
        P(),
        rows,
        vec,
        rows,
        vec,
        vec,
        vec,
        rows,
        vec,
        rows,
        vec,
        vec,
        vec,
    )
    out_specs = (tok, tok, rows, vec, rows, vec, vec, vec, rows, vec, rows, vec, vec, vec)
    return jax.shard_map(body, mesh=mesh, in_specs=in_specs, out_specs=out_specs, check_vma=False)
```

```python
import math
from functools import partial

import jax
import jax.numpy as jnp
from jax import lax
from jax.experimental import pallas as pl
from jax.experimental.pallas import tpu as pltpu
from jax.sharding import PartitionSpec as P

norm_eps = 1e-05
bf16 = jnp.bfloat16
f32 = jnp.float32
AXES = ("batch", "seq")


def flat_xor(value, mask):
    n = lax.axis_size("batch") * lax.axis_size("seq")
    return lax.ppermute(value, AXES, [(i, i ^ mask) for i in range(n)])


def log2(n):
    return n.bit_length() - 1


def gather_order(nb, ns, swap):
    seq_bits = list(range(log2(ns)))
    batch_bits = [log2(ns) + b for b in range(log2(nb))]
    low, mid, high = seq_bits[0], seq_bits[1], seq_bits[2:]
    cross = [mid] + batch_bits if not swap else batch_bits + [mid]
    return high[::-1] + cross + [low]


def my_flat():
    return lax.axis_index("batch") * lax.axis_size("seq") + lax.axis_index("seq")


def gather_rows(shard, swap):
    nb, ns = lax.axis_size("batch"), lax.axis_size("seq")
    nbits = log2(nb * ns)
    me = my_flat()
    shape = shard.shape
    buf = shard.reshape((1,) * nbits + shape)
    for bit in gather_order(nb, ns, swap):
        axis = nbits - 1 - bit
        other = flat_xor(buf, 1 << bit)
        mine = (me >> bit) & 1
        buf = jnp.where(
            mine == 1,
            jnp.concatenate([other, buf], axis),
            jnp.concatenate([buf, other], axis),
        )
    return buf.reshape((nb * ns * shape[0],) + shape[1:])


class Gather:
    def __init__(self, shard, swap):
        self.bits = gather_order(lax.axis_size("batch"), lax.axis_size("seq"), swap)
        self.order = tuple(self.bits[:-1])
        self.buf = shard.reshape((1,) + shard.shape[-2:])

    def step(self):
        other = flat_xor(self.buf, 1 << self.bits.pop(0))
        if self.bits:
            self.buf = jnp.concatenate([self.buf, other], axis=0)
        else:
            self.other = other
        return self.buf

    def rest(self):
        while self.bits:
            self.step()
        return self.buf, self.other


def slot(order, me, device):
    far = me ^ device
    at = (far >> order[0]) & 1
    for j in range(1, len(order)):
        at = at + (((far >> order[j]) & 1) << j)
    return at


class Scatter:
    def __init__(self, buf, swap, send=None):
        nbits = log2(lax.axis_size("batch") * lax.axis_size("seq"))
        self.bits = gather_order(lax.axis_size("batch"), lax.axis_size("seq"), swap)[::-1]
        self.send = send
        self.buf = buf if send is not None else buf.reshape((2,) * nbits + buf.shape[1:])
        self.tail = buf.shape[1:]
        self.nbits = nbits

    def step(self, beside=0.0):
        bit = self.bits.pop(0)
        axis = self.nbits - 1 - bit
        mine = (my_flat() >> bit) & 1
        if self.send is None:
            keep = lax.dynamic_index_in_dim(self.buf, mine, axis, True)
            send = lax.dynamic_index_in_dim(self.buf, 1 - mine, axis, True)
        else:
            keep, send, self.send = self.buf, self.send, None
        got = flat_xor(send, 1 << bit)
        buf = keep.astype(f32) + got.astype(f32) + beside
        if self.bits:
            buf = buf.astype(bf16)
        else:
            buf = buf.reshape(self.tail)
        if keep.ndim == 3 and self.bits:
            buf = buf.reshape((2,) * (self.nbits - 1) + (1,) + self.tail)
        self.buf = buf
        return buf

    def rest(self):
        while self.bits:
            self.step()
        return self.buf


def seq_perm(value, pairs):
    return lax.ppermute(value, "seq", pairs)


def exclusive_scan(tails, ids, rev, beside, final=lambda value: value):
    n = lax.axis_size("seq")
    place = lax.axis_index("seq")
    if rev:
        ids = ids[::-1]
    p = n - 1 - place if rev else place

    def at(q):
        return n - 1 - q if rev else q

    def move(value, pairs):
        return seq_perm(value, [(at(a), at(b)) for a, b in pairs])

    def gated(g, value):
        return g * value.astype(f32)

    c = p & 1
    x = (p >> 1) & 1
    base = p - (p & 3)
    pair = p - c
    seqs = tails.shape[0]
    rest = tails.shape[2:]
    wanted = [(pair, pair + 1), (base + 1, base + 3), (base - 1, base + 1), (pair - 1, pair)]
    step = 1
    while step * 4 < n:
        wanted += [(base + 3 - 4 * step, base - 1), (base + 3 - 4 * step, base + 3)]
        step *= 2
    where = jnp.stack([jnp.clip(t, 0, n - 1) for pair_of in wanted for t in pair_of])
    chosen = (where[:, None] == jnp.arange(n)[None, :]).astype(f32)
    keys = jnp.sum(chosen[:, :, None] * ids[None], axis=1)
    gates = (keys[0::2] == keys[1::2]).astype(f32)
    gates = jnp.broadcast_to(gates[:, :, None, None], gates.shape + (1, rest[-1]))
    gate_core, gate_pair, gate_plane, gate_entry = (gates[i] for i in range(4))
    parts = tails.reshape((seqs, 2, 2) + rest)

    def pick(a, i, axis):
        return lax.dynamic_index_in_dim(a, i, axis, False)

    core = [(i, i ^ 1) for i in range(n)]
    across = [(i, i ^ 2) for i in range(n)]
    own = pick(parts, c, 2)
    other = move(pick(parts, 1 - c, 2), core)
    first = jnp.where(c == 0, own, other)
    second = jnp.where(c == 0, other, own)
    pair_sum = second.astype(f32) + gated(gate_core[:, None], first)
    pair_mine = pick(pair_sum, x, 1)
    sent = pick(pair_sum, 1 - x, 1).astype(bf16)
    beside = beside(sent)
    pair_other = move(sent, across).astype(f32)
    low = jnp.where(x == 0, pair_mine, pair_other)
    high = jnp.where(x == 0, pair_other, pair_mine)
    total = high + gated(gate_pair, low)
    before = jnp.zeros_like(total)
    step = 1
    while step * 4 < n:
        total = total + (beside.pop(0) if beside else 0.0)
        got = move(
            total.astype(bf16), [(i, i + 4 * step) for i in range(n - 4 * step)]
        )
        at_step = 4 + 2 * log2(step)
        before = before + gated(gates[at_step], got)
        total = total + gated(gates[at_step + 1], got)
        step *= 2
    before_high = low + gated(gate_plane, before)
    mine = jnp.where(x == 0, before, before_high)
    theirs = jnp.where(x == 0, before_high, before) + sum(beside, jnp.zeros((1, 1), f32))
    got = move(theirs.astype(bf16), across)
    mine_b = mine.astype(bf16)
    entry = jnp.where(x == 0, jnp.stack([mine_b, got], 1), jnp.stack([got, mine_b], 1))
    after = first.astype(f32) + gated(gate_entry[:, None], entry)
    after_b = after.astype(bf16)
    mine = jnp.where(c == 0, entry, after_b)
    theirs = final(jnp.where(c == 0, after_b, entry))
    got = move(theirs, core)
    result = jnp.where(c == 0, jnp.stack([mine, got], 2), jnp.stack([got, mine], 2))
    return result.reshape(tails.shape)


NT = (((1,), (1,)), ((), ()))
VMEM_LIMIT = 56 * 1024 * 1024


def mm(a, b):
    return jnp.dot(a, b, preferred_element_type=f32)


def mm_nt(a, b):
    return lax.dot_general(a, b, NT, preferred_element_type=f32)


def lane_low(shape, half):
    return lax.broadcasted_iota(jnp.int32, shape, 1) < half


def half_sums(value, low):
    first = jnp.sum(jnp.where(low, value, 0.0), axis=1, keepdims=True)
    second = jnp.sum(jnp.where(low, 0.0, value), axis=1, keepdims=True)
    return first, second


def state_rows(ref, s, h, heads, d):
    per = heads // 4
    return ref[s, h // per, pl.ds((h % per) * d, d), :]


def total_rows(ref, s, heads, d):
    per = heads // 4
    out = []
    for q in range(4):
        rows = ref[s, q, pl.ds(per * d, 16), :].astype(f32)
        out += [rows[j : j + 1] for j in range(per)]
    return out


def pair_rows(first, second, core):
    return jnp.concatenate([first, second] if core == 0 else [second, first], axis=0)


def lay_out(pieces, width, out_ref):
    tiles = out_ref.shape[1] // 128
    lane = lax.broadcasted_iota(jnp.int32, (8, 128), 1)
    acc = [jnp.zeros((8, 128), f32)] * tiles
    for j, piece in enumerate(pieces):
        t, s = divmod(j * width, 128)
        turned = pltpu.roll(jnp.where(lane < width, piece, 0.0), s, 1) if s else jnp.where(lane < width, piece, 0.0)
        if s + width <= 128:
            acc[t] = acc[t] + turned
        else:
            acc[t] = acc[t] + jnp.where(lane >= s, turned, 0.0)
            acc[t + 1] = acc[t + 1] + jnp.where(lane < s, turned, 0.0)
    for t in range(tiles):
        out_ref[:, t * 128 : (t + 1) * 128] = acc[t]


def cut_out(values, width, count):
    tiles = values.shape[1] // 128
    lane = lax.broadcasted_iota(jnp.int32, (8, 128), 1)
    out = []
    for j in range(count):
        t, s = divmod(j * width, 128)
        piece = values[:, t * 128 : (t + 1) * 128]
        if s + width > 128:
            piece = jnp.where(lane >= s, piece, values[:, (t + 1) * 128 : (t + 2) * 128])
        out.append(pltpu.roll(piece, 128 - s, 1) if s else piece)
    return out


def fill_first(orders, shard_rows, piece, me_ref, wa_ref, wb_ref, bias, own_a, oth_a, own_b, oth_b, core):
    me = me_ref[0]
    unit = 2 * shard_rows
    count = wa_ref.shape[0] // unit

    def one(j, carry):
        rows = pl.ds(pl.multiple_of(j * unit, 16), unit)
        p = slot(orders[0], me, 2 * j)
        wa_ref[rows, :] = pair_rows(own_a[p], oth_a[p], core)
        p = slot(orders[1], me, 2 * j)
        wb_ref[rows, :] = pair_rows(own_b[p], oth_b[p], core)
        return carry

    lax.fori_loop(0, count, one, 0)
    first = wa_ref.shape[1] - 128
    pieces = []
    for j in range(count):
        two = wa_ref[j * unit : (j + 1) * unit, first:].astype(f32)
        pieces += [two[i * shard_rows : i * shard_rows + 8] for i in range(2)]
    lay_out(pieces, piece, bias)


def features_tiled_kernel(
    block, heads, d, orders, shard_rows, me_ref, x_ref, own_a, oth_a, own_b, oth_b, proj_ref, tg_ref,
    q_ref, k_ref, v_ref, phq_ref, phk_ref, tail_ref, wa_ref, wb_ref, z_scr, bias,
):
    @pl.when(pl.program_id(0) == 0)
    def _():
        piece = bias.shape[1] // (wa_ref.shape[0] // shard_rows)
        for core in range(2):
            pl.when(me_ref[0] % 2 == core)(
                partial(
                    fill_first, orders, shard_rows, piece, me_ref, wa_ref, wb_ref, bias,
                    own_a, oth_a, own_b, oth_b, core,
                )
            )

    features_kernel(
        block, heads, d, x_ref, wa_ref, wb_ref, bias, proj_ref, tg_ref,
        q_ref, k_ref, v_ref, phq_ref, phk_ref, tail_ref, z_scr,
    )


def features_kernel(
    block, heads, d, x_ref, wa_ref, wb_ref, b_ref, proj_ref, tg_ref,
    q_ref, k_ref, v_ref, phq_ref, phk_ref, tail_ref, z_scr,
):
    width = heads * d
    m = proj_ref.shape[2]
    pair = 2 * d
    scale = d ** (-0.25)
    root = m ** (-0.5)
    x = x_ref[...]
    rows = x.shape[0]
    low = lane_low((rows, pair), d)
    chunk = width // 2
    for t, (z_ref, ph_ref) in ((1, (k_ref, phk_ref)), (2, (v_ref, None)), (0, (q_ref, phq_ref))):
        for i in range(2):
            col = t * width + i * chunk
            w = wa_ref[:, col : col + chunk] if col < 3 * chunk else wb_ref[:, col - 3 * chunk : col - 2 * chunk]
            z = mm(x, w) + b_ref[0:1, col : col + chunk]
            z = (z * scale if ph_ref is not None else z).astype(bf16)
            z_ref[:, i * chunk : (i + 1) * chunk] = z
            if ph_ref is None:
                continue
            for p in range(chunk // pair):
                zp = z[:, p * pair : (p + 1) * pair]
                zf = zp.astype(f32)
                sums = half_sums(zf * zf, low)
                for e in range(2):
                    h = 2 * (i * (chunk // pair) + p) + e
                    u = mm(zp, proj_ref[h])
                    ph_ref[:, h * m : (h + 1) * m] = (jnp.exp(u - 0.5 * sums[e]) * root).astype(bf16)
    per = heads // 4
    for s in range(rows // block):
        r = slice(s * block, (s + 1) * block)
        tg = tg_ref[r, :].astype(bf16)
        for p in range(heads // 2):
            v_t = v_ref[r, p * pair : (p + 1) * pair].T
            for e in range(2):
                h = 2 * p + e
                kt = phk_ref[r, h * m : (h + 1) * m] * tg
                lhs = jnp.concatenate([v_t[e * d : (e + 1) * d], jnp.ones((16, block), bf16)], 0)
                res = mm(lhs, kt)
                tail_ref[s, h // per, pl.ds((h % per) * d, d), :] = res[:d].astype(bf16)
                z_scr[h % per : h % per + 1, :] = res[d : d + 1]
                if h % per == per - 1:
                    tail_ref[s, h // per, pl.ds(per * d, 16), :] = z_scr[...].astype(bf16)


def local_kernel(
    block, heads, d, phq_ref, phk_ref, v_ref, col_ref, row_ref, amat_ref, nd_ref, done_ref
):
    done_ref[...] = jnp.zeros_like(done_ref)
    m = phq_ref.shape[1] // heads
    pair = 2 * d
    low = lane_low((block, pair), d)
    t_ix = lax.broadcasted_iota(jnp.int32, (block, block), 0)
    j_ix = lax.broadcasted_iota(jnp.int32, (block, block), 1)
    causal = t_ix >= j_ix
    for s in range(v_ref.shape[0] // block):
        r = slice(s * block, (s + 1) * block)
        mask = jnp.logical_and(causal, col_ref[r, 0:1] == row_ref[s])
        for p in range(heads // 2):
            v_pair = v_ref[r, p * pair : (p + 1) * pair]
            for e in range(2):
                h = 2 * p + e
                sc = mm_nt(phq_ref[r, h * m : (h + 1) * m], phk_ref[r, h * m : (h + 1) * m])
                am = jnp.where(mask, sc, 0.0).astype(bf16)
                amat_ref[s, h] = am
                v_one = jnp.where(low if e == 0 else ~low, v_pair, jnp.ones_like(v_pair))
                nd_ref[r, h * pair : (h + 1) * pair] = mm(am, v_one)


def layer_norm(row_vals, gain, shift):
    inv = 1.0 / row_vals.shape[1]
    centred = row_vals - jnp.sum(row_vals, axis=1, keepdims=True) * inv
    rs = lax.rsqrt(jnp.sum(centred * centred, axis=1, keepdims=True) * inv + norm_eps)
    normed = centred * rs
    return normed * gain + shift, normed, rs


def layer_norm_back(dn, normed, rs):
    inv = 1.0 / dn.shape[1]
    mean = jnp.sum(dn, axis=1, keepdims=True) * inv
    proj = jnp.sum(dn * normed, axis=1, keepdims=True) * inv
    return rs * (dn - mean - normed * proj)


def group_rows(shard_rows):
    return math.lcm(shard_rows, 16) // shard_rows


def natural_rows(stage, out_ref, shard_rows, width):
    groups = stage.shape[1] // width
    per = group_rows(shard_rows)
    unit = per * shard_rows

    def one(i, carry):
        cols = [
            stage[pl.ds(pl.multiple_of(i * unit, 16), unit), g * width : (g + 1) * width]
            for g in range(groups)
        ]
        pieces = [c[j * shard_rows : (j + 1) * shard_rows] for j in range(per) for c in cols]
        out_ref[pl.ds(pl.multiple_of(i * unit * groups, 16), unit * groups), :] = jnp.concatenate(
            pieces, axis=0
        )
        return carry

    lax.fori_loop(0, stage.shape[0] // unit, one, 0)


def fill_rest(shard_rows, w_out_ref, vec_scr, b_in_scr, stage, vec_stage):
    width = w_out_ref.shape[1]
    natural_rows(stage, w_out_ref, shard_rows, width)
    unit = 2 * shard_rows
    pieces = []
    for j in range(vec_stage.shape[0] // unit):
        two = vec_stage[j * unit : (j + 1) * unit, :].astype(f32)
        pieces += [two[i * shard_rows : i * shard_rows + 8] for i in range(2)]
    lay_out(pieces, shard_rows, vec_scr)
    lay_out(pieces, w_out_ref.shape[0] // len(pieces), b_in_scr)


def middle_kernel(
    block, heads, d, ff_chunk,
    tiled, shard_rows, x_ref, cot_ref, phq_ref, nd_ref, pre_ref, gate_ref,
    *refs
):
    ins = refs[: 1 if tiled else 5]
    middle_parts(
        block, heads, d, ff_chunk, tiled, shard_rows, x_ref, cot_ref, phq_ref, nd_ref,
        pre_ref, gate_ref, ins, *refs[len(ins) :],
    )


def middle_parts(
    block, heads, d, ff_chunk, tiled, shard_rows, x_ref, cot_ref, phq_ref, nd_ref, pre_ref,
    gate_ref, ins,
    y_ref, dr1_ref, dnum_ref, dden_ref, dpre_ref, attn_ref, dao_ref, h1_ref, act_ref, dfo_ref,
    df_ref, sums_ref, sum_in_ref,
    attf, rden, dgel, z_scr, w_o_ref, w_in_ref, w_out_ref, vec_ref, b_in_ref, sems, *stages
):
    step = pl.program_id(0)
    m = phq_ref.shape[1] // heads
    width = heads * d
    ff = w_in_ref.shape[1]

    def copies():
        if tiled:
            cuts = [0, width, width + ff, width + 2 * ff, width + 2 * ff + 128]
            sources = [ins[0].at[:, i:j] for i, j in zip(cuts, cuts[1:])]
            places = (w_o_ref, w_in_ref) + tuple(stages)
        else:
            sources, places = ins, (w_o_ref, w_in_ref, w_out_ref, vec_ref, b_in_ref)
        return [
            pltpu.make_async_copy(src, dst, sems.at[i])
            for i, (src, dst) in enumerate(zip(sources, places))
        ]

    @pl.when(step == 0)
    def _():
        for c in copies():
            c.start()

    pair = 2 * d
    low = lane_low((block, pair), d)
    rows = x_ref.shape[0]
    seqs = rows // block
    ones = jnp.ones((d, 1), f32)
    for s in range(seqs):
        r = slice(s * block, (s + 1) * block)
        g = gate_ref[r, 2:3]
        zs = total_rows(pre_ref, s, heads, d)
        for p in range(heads // 2):
            tot = []
            for e in range(2):
                h = 2 * p + e
                st = state_rows(pre_ref, s, h, heads, d)
                zb = (ones * zs[h]).astype(bf16)
                rhs = jnp.concatenate([st, zb] if e == 0 else [zb, st], 0)
                tot.append(
                    nd_ref[r, h * pair : (h + 1) * pair]
                    + g * mm_nt(phq_ref[r, h * m : (h + 1) * m], rhs)
                )
            num = jnp.where(low, tot[0], tot[1])
            den = pltpu.roll(jnp.where(low, tot[1], tot[0]), d, 1)
            rd = 1.0 / den
            c = slice(p * pair, (p + 1) * pair)
            att = num * rd
            attf[r, c] = att
            rden[r, c] = rd
            attn_ref[r, c] = att.astype(bf16)

    @pl.when(step == 0)
    def _():
        for c in copies():
            c.wait()
        if tiled:
            fill_rest(shard_rows, w_out_ref, vec_ref, b_in_ref, *stages)

    b_o, gain1, shift1, b_out, gain2, shift2 = (vec_ref[i : i + 1, :] for i in range(6))
    r1 = x_ref[...].astype(f32) + mm(attn_ref[...], w_o_ref[...]) + b_o
    h1, n1, rs1 = layer_norm(r1, gain1, shift1)
    h1b = h1.astype(bf16)
    h1_ref[...] = h1b
    fo = None
    for c0 in range(0, ff, ff_chunk):
        c = slice(c0, c0 + ff_chunk)
        f = mm(h1b, w_in_ref[:, c]) + b_in_ref[6:7, c]
        phi = 0.5 + 0.5 * lax.erf(f * (0.5**0.5))
        act = (f * phi).astype(bf16)
        act_ref[:, c] = act
        dgel[:, c] = phi + f * (jnp.exp(-0.5 * f * f) * (1.0 / (2.0 * math.pi) ** 0.5))
        part = mm(act, w_out_ref[c, :])
        fo = part if fo is None else fo + part
    y, n2, rs2 = layer_norm(h1 + fo + b_out, gain2, shift2)
    y_ref[...] = y.astype(bf16)
    dy = cot_ref[...].astype(f32)

    def add_sum(i, value):
        row = jnp.sum(value, axis=0, keepdims=True)

        @pl.when(step == 0)
        def _():
            sums_ref[i : i + 1, :] = row

        @pl.when(step > 0)
        def _():
            sums_ref[i : i + 1, :] += row

    add_sum(4, dy * n2)
    add_sum(5, dy)
    dr2 = layer_norm_back(dy * gain2, n2, rs2)
    dfo = dr2.astype(bf16)
    dfo_ref[...] = dfo
    add_sum(3, dfo.astype(f32))
    dh1 = dr2
    for c0 in range(0, ff, ff_chunk):
        c = slice(c0, c0 + ff_chunk)
        df = (mm_nt(dfo, w_out_ref[c, :]) * dgel[:, c]).astype(bf16)
        df_ref[:, c] = df
        row = jnp.sum(df.astype(f32), axis=0, keepdims=True)

        @pl.when(step == 0)
        def _():
            sum_in_ref[:, c] = row

        @pl.when(step > 0)
        def _():
            sum_in_ref[:, c] += row

        dh1 = dh1 + mm_nt(df, w_in_ref[:, c])
    add_sum(1, dh1 * n1)
    add_sum(2, dh1)
    dr1 = layer_norm_back(dh1 * gain1, n1, rs1)
    dr1_ref[...] = dr1
    dao = dr1.astype(bf16)
    dao_ref[...] = dao
    add_sum(0, dao.astype(f32))
    dattn = mm_nt(dao, w_o_ref[...])
    dnum_ref[...] = (dattn * rden[...]).astype(bf16)
    prod = dattn * attf[...]
    lane = lax.broadcasted_iota(jnp.int32, (rows, 128), 1)
    low_rows = lane_low((rows, pair), d)
    dden = jnp.zeros((rows, 128), f32)
    for p in range(heads // 2):
        c = slice(p * pair, (p + 1) * pair)
        sums = half_sums(prod[:, c], low_rows)
        for e in range(2):
            col = -sums[e] * rden[:, p * pair + e * d : p * pair + e * d + 1]
            dden = jnp.where(lane == 2 * p + e, col, dden)
    dden = dden.astype(bf16).astype(f32)
    dden_ref[...] = dden
    per = heads // 4
    for s in range(seqs):
        r = slice(s * block, (s + 1) * block)
        g = gate_ref[r, 2:3]
        ddt = (dden[r] * g).T[:16].astype(bf16)
        for p in range(heads // 2):
            gdt = (dnum_ref[r, p * pair : (p + 1) * pair] * g.astype(bf16)).T
            for e in range(2):
                h = 2 * p + e
                lhs = jnp.concatenate([gdt[e * d : (e + 1) * d], ddt], 0)
                res = mm(lhs, phq_ref[r, h * m : (h + 1) * m])
                dpre_ref[s, h // per, pl.ds((h % per) * d, d), :] = res[:d].astype(bf16)
                z_scr[h % per : h % per + 1, :] = res[d + h : d + h + 1]
                if h % per == per - 1:
                    dpre_ref[s, h // per, pl.ds(per * d, 16), :] = z_scr[...].astype(bf16)


def back_query_kernel(
    block, heads, d,
    q_ref, v_ref, phq_ref, phk_ref, amat_ref, dnum_ref, dden_ref, pre_ref, gate_ref, row_ref,
    proj_ref,
    dq_ref, dv_ref, dsct_ref, done_ref,
):
    done_ref[...] = jnp.zeros_like(done_ref)
    m = phq_ref.shape[1] // heads
    pair = 2 * d
    scale = d ** (-0.25)
    low = lane_low((block, pair), d)
    t_ix = lax.broadcasted_iota(jnp.int32, (block, block), 0)
    j_ix = lax.broadcasted_iota(jnp.int32, (block, block), 1)
    causal = t_ix >= j_ix
    for s in range(q_ref.shape[0] // block):
        r = slice(s * block, (s + 1) * block)
        g = gate_ref[r, 2:3]
        gb = g.astype(bf16)
        mask = jnp.logical_and(causal, gate_ref[r, 0:1] == row_ref[s])
        zs = total_rows(pre_ref, s, heads, d)
        for p in range(heads // 2):
            c = slice(p * pair, (p + 1) * pair)
            dn = dnum_ref[r, c]
            v_pair = v_ref[r, c]
            qp = q_ref[r, c].astype(f32)
            st = jnp.concatenate(
                [state_rows(pre_ref, s, 2 * p, heads, d), state_rows(pre_ref, s, 2 * p + 1, heads, d)], 0
            )
            dv = None
            dq = None
            for e in range(2):
                h = 2 * p + e
                mine = low if e == 0 else ~low
                hm = slice(h * m, (h + 1) * m)
                dnm = jnp.where(mine, dn, jnp.zeros_like(dn))
                dd = dden_ref[r, h : h + 1]
                dsc = jnp.where(mask, mm_nt(dnm, v_pair) + dd, 0.0)
                dsct_ref[s, h] = dsc.T.astype(bf16)
                dph = mm(
                    jnp.concatenate([dsc.astype(bf16), dnm * gb], 1),
                    jnp.concatenate([phk_ref[r, hm], st], 0),
                ) + (g * dd) * zs[h]
                t = dph * phq_ref[r, hm].astype(f32)
                part = mm_nt(t.astype(bf16), proj_ref[h]) - jnp.where(
                    mine, jnp.sum(t, axis=1, keepdims=True) * qp, 0.0
                )
                dq = part if dq is None else dq + part
                part = mm(amat_ref[s, h].T, dnm)
                dv = part if dv is None else dv + part
            dq_ref[r, c] = (dq * scale).astype(bf16)
            dv_ref[r, c] = dv


def back_key_kernel(
    block, heads, d,
    k_ref, v_ref, phq_ref, phk_ref, dv_ref, dsct_ref, dtail_ref, gate_ref, proj_ref,
    dkv_ref,
):
    m = phq_ref.shape[1] // heads
    pair = 2 * d
    width = heads * d
    scale = d ** (-0.25)
    low = lane_low((block, pair), d)
    for s in range(k_ref.shape[0] // block):
        r = slice(s * block, (s + 1) * block)
        tg = gate_ref[r, 1:2]
        tgb = tg.astype(bf16)
        zs = total_rows(dtail_ref, s, heads, d)
        for p in range(heads // 2):
            c = slice(p * pair, (p + 1) * pair)
            v_pair = v_ref[r, c]
            kp = k_ref[r, c].astype(f32)
            ds = jnp.concatenate(
                [
                    state_rows(dtail_ref, s, 2 * p, heads, d),
                    state_rows(dtail_ref, s, 2 * p + 1, heads, d),
                ],
                0,
            )
            dk = None
            inter = []
            for e in range(2):
                h = 2 * p + e
                mine = low if e == 0 else ~low
                hm = slice(h * m, (h + 1) * m)
                vm = jnp.where(mine, v_pair, jnp.zeros_like(v_pair)) * tgb
                phk = phk_ref[r, hm]
                dph = mm(
                    jnp.concatenate([dsct_ref[s, h], vm], 1),
                    jnp.concatenate([phq_ref[r, hm], ds], 0),
                ) + tg * zs[h]
                t = dph * phk.astype(f32)
                part = mm_nt(t.astype(bf16), proj_ref[h]) - jnp.where(
                    mine, jnp.sum(t, axis=1, keepdims=True) * kp, 0.0
                )
                dk = part if dk is None else dk + part
                inter.append(mm_nt(phk, ds))
            dkv_ref[r, c] = (dk * scale).astype(bf16)
            dv = dv_ref[r, c] + tg * jnp.where(low, inter[0], inter[1])
            dkv_ref[r, width + p * pair : width + (p + 1) * pair] = dv.astype(bf16)


def params(micros):
    return dict(
        compiler_params=pltpu.CompilerParams(
            dimension_semantics=("arbitrary",), vmem_limit_bytes=VMEM_LIMIT
        ),
        cost_estimate=pl.CostEstimate(
            flops=int(micros * 1e9), bytes_accessed=int(micros * 1e6), transcendentals=0
        ),
    )


def row_spec(rows, cols):
    return pl.BlockSpec((rows, cols), lambda i: (i, 0))


def lead_spec(shape):
    return pl.BlockSpec(shape, lambda i: (i,) + (0,) * (len(shape) - 1))


def whole_spec(shape):
    return pl.BlockSpec(shape, lambda i: (0,) * len(shape))


def sds(shape, dtype):
    return jax.ShapeDtypeStruct(shape, dtype)


STEP_SEQS = 2
STATE_PAD = 16


def state_shape(seqs, heads, d, m):
    return (seqs, 4, heads // 4 * d + STATE_PAD, m)


def call_features(x, wa, wb, b, proj, tg, block, heads, d):
    rows, width = x.shape
    m = proj.shape[2]
    n = STEP_SEQS * block
    st = state_shape(STEP_SEQS, heads, d, m)
    return pl.pallas_call(
        partial(features_kernel, block, heads, d),
        grid=(rows // n,),
        in_specs=[
            row_spec(n, width), whole_spec(wa.shape), whole_spec(wb.shape), whole_spec(b.shape),
            whole_spec(proj.shape), row_spec(n, 1),
        ],
        out_specs=[row_spec(n, width)] * 3 + [row_spec(n, heads * m)] * 2 + [lead_spec(st)],
        out_shape=[sds((rows, width), bf16)] * 3
        + [sds((rows, heads * m), bf16)] * 2
        + [sds((rows // block,) + st[1:], bf16)],
        scratch_shapes=[pltpu.VMEM((16, m), f32)],
        name="features",
        **params(10),
    )(x, wa, wb, b, proj, tg)


def call_features_tiled(x, a, b, proj, tg, shard_rows, block, heads, d):
    rows, width = x.shape
    m = proj.shape[2]
    n = STEP_SEQS * block
    st = state_shape(STEP_SEQS, heads, d, m)
    parts = (a.buf, a.other, b.buf, b.other)
    wa, wb = (width, a.buf.shape[2]), (width, b.buf.shape[2])
    return pl.pallas_call(
        partial(features_tiled_kernel, block, heads, d, (a.order, b.order), shard_rows),
        grid=(rows // n,),
        in_specs=[pl.BlockSpec(memory_space=pltpu.SMEM), row_spec(n, width)]
        + [whole_spec(t.shape) for t in parts]
        + [whole_spec(proj.shape), row_spec(n, 1)],
        out_specs=[row_spec(n, width)] * 3
        + [row_spec(n, heads * m)] * 2
        + [lead_spec(st), whole_spec(wa), whole_spec(wb)],
        out_shape=[sds((rows, width), bf16)] * 3
        + [sds((rows, heads * m), bf16)] * 2
        + [sds((rows // block,) + st[1:], bf16), sds(wa, bf16), sds(wb, bf16)],
        scratch_shapes=[pltpu.VMEM((16, m), f32), pltpu.VMEM((8, 3 * width), f32)],
        name="features",
        **params(12),
    )(my_flat().astype(jnp.int32).reshape(1), x, *parts, proj, tg)


def call_local(phq, phk, v, gates, id_rows, block, heads, d):
    rows = v.shape[0]
    n = STEP_SEQS * block
    return pl.pallas_call(
        partial(local_kernel, block, heads, d),
        grid=(rows // n,),
        in_specs=[
            row_spec(n, phq.shape[1]), row_spec(n, phk.shape[1]), row_spec(n, v.shape[1]),
            row_spec(n, gates.shape[1]), lead_spec((STEP_SEQS, 1, block)),
        ],
        out_specs=[
            lead_spec((STEP_SEQS, heads, block, block)), row_spec(n, heads * 2 * d),
            whole_spec((1, 1)),
        ],
        out_shape=[
            sds((rows // block, heads, block, block), bf16), sds((rows, heads * 2 * d), f32),
            sds((1, 1), f32),
        ],
        name="local",
        **params(8),
    )(phq, phk, v, gates, id_rows)


def call_middle(x, cot, phq, nd, pre, gates, weights, tiled, shard_rows, ff, block, heads, d):
    rows, width = x.shape
    m = phq.shape[1] // heads
    n = STEP_SEQS * block
    st = (STEP_SEQS,) + pre.shape[1:]
    return pl.pallas_call(
        partial(middle_kernel, block, heads, d, 768, tiled, shard_rows),
        grid=(rows // n,),
        in_specs=[
            row_spec(n, width), row_spec(n, width), row_spec(n, phq.shape[1]),
            row_spec(n, nd.shape[1]), lead_spec(st), row_spec(n, gates.shape[1]),
        ]
        + [pl.BlockSpec(memory_space=pl.ANY)] * len(weights),
        out_specs=[
            row_spec(n, width), row_spec(n, width), row_spec(n, width), row_spec(n, 128),
            lead_spec(st), row_spec(n, width), row_spec(n, width), row_spec(n, width),
            row_spec(n, ff), row_spec(n, width), row_spec(n, ff), whole_spec((8, width)),
            whole_spec((1, ff)),
        ],
        out_shape=[
            sds((rows, width), bf16), sds((rows, width), f32), sds((rows, width), bf16),
            sds((rows, 128), f32), sds(pre.shape, bf16), sds((rows, width), bf16),
            sds((rows, width), bf16), sds((rows, width), bf16), sds((rows, ff), bf16),
            sds((rows, width), bf16), sds((rows, ff), bf16), sds((8, width), f32),
            sds((1, ff), f32),
        ],
        scratch_shapes=[
            pltpu.VMEM((n, width), f32), pltpu.VMEM((n, width), f32), pltpu.VMEM((n, ff), f32),
            pltpu.VMEM((16, m), f32), pltpu.VMEM((width, width), bf16),
            pltpu.VMEM((width, ff), bf16), pltpu.VMEM((ff, width), bf16),
            pltpu.VMEM((8, width), f32), pltpu.VMEM((8, ff), f32), pltpu.SemaphoreType.DMA((5,)),
        ]
        + ([pltpu.VMEM((width, ff), bf16), pltpu.VMEM((width, 128), bf16)] if tiled else []),
        name="middle",
        **params(31),
    )(x, cot, phq, nd, pre, gates, *weights)


def call_back_query(
    half, q, v, phq, phk, amat, dnum, dden, pre, gates, id_rows, proj, ties, block, heads, d
):
    rows, width = q.shape
    n = STEP_SEQS * block
    sq = (STEP_SEQS, heads, block, block)

    def rs(cols):
        return pl.BlockSpec((n, cols), lambda i: (half, 0))

    def ls(shape):
        return pl.BlockSpec(shape, lambda i: (half,) + (0,) * (len(shape) - 1))

    def kernel(*refs):
        back_query_kernel(block, heads, d, *refs[:11], *refs[11 + len(ties) :])

    return pl.pallas_call(
        kernel,
        grid=(1,),
        in_specs=[
            rs(width), rs(width), rs(phq.shape[1]), rs(phk.shape[1]), ls(sq), rs(width), rs(128),
            ls((STEP_SEQS,) + pre.shape[1:]), rs(gates.shape[1]), ls((STEP_SEQS, 1, block)),
            whole_spec(proj.shape),
        ]
        + [pl.BlockSpec(memory_space=pl.ANY)] * len(ties),
        out_specs=[row_spec(n, width), row_spec(n, width), lead_spec(sq), whole_spec((1, 1))],
        out_shape=[
            sds((n, width), bf16), sds((n, width), f32), sds(sq, bf16), sds((1, 1), f32),
        ],
        name="back_query",
        **params(8),
    )(q, v, phq, phk, amat, dnum, dden, pre, gates, id_rows, proj, *ties)


def call_back_key(k, v, phq, phk, dvs, dscts, dtail, gates, proj, ties, block, heads, d):
    rows, width = k.shape
    n = STEP_SEQS * block
    sq = (STEP_SEQS, heads, block, block)
    steps = rows // n

    def kernel(k_ref, v_ref, phq_ref, phk_ref, *refs):
        for i in range(steps):

            @pl.when(pl.program_id(0) == i)
            def _():
                back_key_kernel(
                    block, heads, d, k_ref, v_ref, phq_ref, phk_ref, refs[i], refs[steps + i],
                    *refs[2 * steps : 2 * steps + 3], refs[-1],
                )

    return pl.pallas_call(
        kernel,
        grid=(steps,),
        in_specs=[
            row_spec(n, width), row_spec(n, width), row_spec(n, phq.shape[1]),
            row_spec(n, phk.shape[1]),
        ]
        + [whole_spec((n, width))] * steps
        + [whole_spec(sq)] * steps
        + [
            lead_spec((STEP_SEQS,) + dtail.shape[1:]), row_spec(n, gates.shape[1]),
            whole_spec(proj.shape),
        ]
        + [pl.BlockSpec(memory_space=pl.ANY)] * len(ties),
        out_specs=row_spec(n, 2 * width),
        out_shape=sds((rows, 2 * width), bf16),
        name="back_key",
        **params(13),
    )(k, v, phq, phk, *dvs, *dscts, dtail, gates, proj, *ties)


TN = (((0,), (0,)), ((), ()))


def mm_tn(a, b):
    return lax.dot_general(a, b, TN, preferred_element_type=f32)


def pack_kernel(shard_rows, w_o_ref, w_in_ref, w_out_ref, vec_ref, *refs):
    out_ref = refs[-1]
    rows = w_out_ref[...]
    parts = [w_o_ref[...], w_in_ref[...]]
    parts += [rows[i : i + shard_rows] for i in range(0, rows.shape[0], shard_rows)]
    parts += [vec_ref[...]]
    at = 0
    for part in parts:
        out_ref[:, at : at + part.shape[1]] = part
        at += part.shape[1]


def call_pack(w_o, w_in, w_out, vec, ties):
    rows = w_o.shape[0]
    cols = (w_o.size + w_in.size + w_out.size + vec.size) // rows
    return pl.pallas_call(
        partial(pack_kernel, rows),
        in_specs=[pl.BlockSpec(memory_space=pltpu.VMEM)] * 4
        + [pl.BlockSpec(memory_space=pl.ANY)] * len(ties),
        out_shape=sds((rows, cols), bf16),
        name="pack",
    )(w_o, w_in, w_out, vec, *ties)


def part_store(core, refs, index, value):
    kept, sent, rows, cols = refs
    (kept if index % 2 == core else sent)[index // 2, rows, cols] = value


def by_core(kernel, core_ref):
    for core in range(2):
        pl.when(core_ref[0] == core)(partial(kernel, core))


def grads_kernel(
    shard_rows, core_ref, attn_ref, dao_ref, h1_ref, df_ref, act_ref, dfo_ref, sums_ref, sum_in_ref,
    tie_ref, keep_i, send_i, keep_o, send_o, done_ref,
):
    done_ref[...] = jnp.zeros_like(done_ref)
    by_core(
        partial(
            grads_parts, shard_rows, attn_ref, dao_ref, h1_ref, df_ref, act_ref, dfo_ref, sums_ref,
            sum_in_ref, keep_i, send_i, keep_o, send_o,
        ),
        core_ref,
    )


def grads_parts(
    shard_rows, attn_ref, dao_ref, h1_ref, df_ref, act_ref, dfo_ref, sums_ref, sum_in_ref,
    keep_i, send_i, keep_o, send_o, core,
):
    width = dao_ref.shape[1]
    ff = df_ref.shape[1]
    groups = ff // width
    tall = groups * shard_rows
    count = h1_ref.shape[1] // shard_rows
    every = slice(None)
    dfo = dfo_ref[...]
    chunk = act_ref.shape[1] // groups
    per = chunk // tall
    for c in range(groups):
        res = mm_tn(act_ref[:, c * chunk : (c + 1) * chunk], dfo).astype(bf16)
        for j in range(per):
            part_store(
                core, (keep_o, send_o, slice(0, tall), every), c * per + j,
                res[j * tall : (j + 1) * tall],
            )
    res = mm_tn(attn_ref[...], dao_ref[...]).astype(bf16)
    for j in range(count):
        part_store(
            core, (keep_o, send_o, slice(tall, tall + shard_rows), every), j,
            res[j * shard_rows : (j + 1) * shard_rows],
        )
    h1 = h1_ref[...]
    for g in range(groups):
        res = mm_tn(h1, df_ref[:, g * width : (g + 1) * width]).astype(bf16)
        for j in range(count):
            part_store(
                core, (keep_i, send_i, every, slice(g * width, (g + 1) * width)), j,
                res[j * shard_rows : (j + 1) * shard_rows],
            )
    step = pl.program_id(0)
    small = cut_out(sums_ref[...], shard_rows, 2 * count)
    large = cut_out(jnp.broadcast_to(sum_in_ref[...], (8, ff)), groups * shard_rows, 2 * count)
    row = lax.broadcasted_iota(jnp.int32, (8, 128), 0)
    for j in range(count):
        a = jnp.where(step == 0, small[j], small[j + count])
        b = jnp.where(step == 0, large[j], large[j + count])
        value = jnp.concatenate(
            [jnp.where(row == 6, b, a), jnp.zeros((shard_rows - 8, 128), f32)], axis=0
        )
        part_store(core, (keep_i, send_i, every, slice(ff, ff + 128)), j, value.astype(bf16))


def call_grads(core, attn, dao, h1, df, act, dfo, sums, sum_in, tie, shard_rows):
    rows, width = dao.shape
    ff = df.shape[1]
    steps = 2
    n_dev = width // shard_rows
    small = (n_dev // 2, shard_rows, ff + 128)
    tall = (n_dev // 2, shard_rows * (ff // width + 1), width)

    def cut(shape):
        return lead_spec((shape[0] // steps,) + shape[1:])

    return pl.pallas_call(
        partial(grads_kernel, shard_rows),
        grid=(steps,),
        in_specs=[
            pl.BlockSpec(memory_space=pltpu.SMEM),
            pl.BlockSpec((rows, width // steps), lambda i: (0, i)), whole_spec(dao.shape),
            pl.BlockSpec((rows, width // steps), lambda i: (0, i)), whole_spec(df.shape),
            pl.BlockSpec((rows, ff // steps), lambda i: (0, i)), whole_spec(dfo.shape),
            whole_spec(sums.shape), whole_spec(sum_in.shape),
            pl.BlockSpec(memory_space=pl.ANY),
        ],
        out_specs=[cut(small), cut(small), cut(tall), cut(tall), whole_spec((1, 1))],
        out_shape=[sds(small, bf16), sds(small, bf16), sds(tall, bf16), sds(tall, bf16)]
        + [sds((1, 1), f32)],
        name="grads",
        **params(10),
    )(core, attn, dao, h1, df, act, dfo, sums, sum_in, tie)


def first_grads_kernel(
    shard_rows, ties, core_ref, x_ref, dq_ref, dkv_ref, *refs
):
    by_core(partial(first_grads_parts, shard_rows, x_ref, dq_ref, dkv_ref, *refs[ties:]), core_ref)


def first_grads_parts(
    shard_rows, x_ref, dq_ref, dkv_ref, keep_a, send_a, keep_b, send_b, core
):
    width = dq_ref.shape[1]
    chunk = width // 2
    x = x_ref[...]
    step = pl.program_id(0)
    count = x_ref.shape[1] // shard_rows
    n_dev = 2 * count
    every = slice(None)
    sums = []
    for i in range(6):
        src, c0 = (dq_ref, i * chunk) if i < 2 else (dkv_ref, (i - 2) * chunk)
        b = src[:, c0 : c0 + chunk]
        sums.append(jnp.sum(b.astype(f32), axis=0, keepdims=True))
        res = mm_tn(x, b).astype(bf16)
        refs = (keep_a, send_a) if i < 3 else (keep_b, send_b)
        cols = slice((i % 3) * chunk, (i % 3 + 1) * chunk)
        for j in range(count):
            part_store(core, refs + (every, cols), j, res[j * shard_rows : (j + 1) * shard_rows])
    row = jnp.broadcast_to(jnp.concatenate(sums, axis=1), (8, 3 * width))
    pieces = cut_out(row, 3 * width // n_dev, n_dev)
    for j in range(count):
        value = jnp.concatenate(
            [
                jnp.where(step == 0, pieces[j], pieces[j + count]),
                jnp.zeros((shard_rows - 8, 128), f32),
            ],
            axis=0,
        )
        cols = slice(3 * chunk, 3 * chunk + 128)
        part_store(core, (keep_a, send_a, every, cols), j, value.astype(bf16))


def call_first_grads(core, x, dq, dkv, ties, shard_rows):
    rows, width = x.shape
    steps = 2
    half = 3 * width // 2
    n_dev = width // shard_rows
    shapes = [(n_dev // 2, shard_rows, half + 128)] * 2 + [(n_dev // 2, shard_rows, half)] * 2
    return pl.pallas_call(
        partial(first_grads_kernel, shard_rows, len(ties)),
        grid=(steps,),
        in_specs=[
            pl.BlockSpec(memory_space=pltpu.SMEM),
            pl.BlockSpec((rows, width // steps), lambda i: (0, i)), whole_spec(dq.shape),
            whole_spec(dkv.shape),
        ]
        + [pl.BlockSpec(memory_space=pl.ANY)] * len(ties),
        out_specs=[lead_spec((t[0] // steps,) + t[1:]) for t in shapes],
        out_shape=[sds(t, bf16) for t in shapes],
        name="first_grads",
        **params(6),
    )(core, x, dq, dkv, *ties)


def input_grad_kernel(dq_ref, dkv_ref, wa_ref, wb_ref, dr1_ref, *refs):
    out_ref, done_ref = refs[-2:]
    done_ref[...] = jnp.zeros_like(done_ref)
    width = dq_ref.shape[1]
    chunk = width // 2
    acc = dr1_ref[...]
    for i in range(6):
        src, c0 = (dq_ref, i * chunk) if i < 2 else (dkv_ref, (i - 2) * chunk)
        w_ref = wa_ref if i < 3 else wb_ref
        acc = acc + mm_nt(src[:, c0 : c0 + chunk], w_ref[:, (i % 3) * chunk : (i % 3 + 1) * chunk])
    out_ref[...] = acc.astype(bf16)


def call_input_grad(dq, dkv, wa, wb, dr1, ties, n):
    rows, width = dq.shape
    return pl.pallas_call(
        input_grad_kernel,
        grid=(rows // n,),
        in_specs=[
            row_spec(n, width), row_spec(n, 2 * width), whole_spec(wa.shape), whole_spec(wb.shape),
            row_spec(n, width),
        ]
        + [pl.BlockSpec(memory_space=pl.ANY)] * len(ties),
        out_specs=[row_spec(n, width), whole_spec((1, 1))],
        out_shape=[sds((rows, width), bf16), sds((1, 1), f32)],
        name="input_grad",
        **params(6),
    )(dq, dkv, wa, wb, dr1, *ties)


def body(
    inputs,
    seg_ids,
    cotangent,
    projection,
    w_qkv,
    b_qkv,
    w_o,
    b_o,
    ln1_gain,
    ln1_bias,
    w_in,
    b_in,
    w_out,
    b_out,
    ln2_gain,
    ln2_bias,
):
    micro, seqs_micro, block, width = inputs.shape
    heads, d, m = projection.shape
    n_seq = lax.axis_size("seq")
    n_dev = lax.axis_size("batch") * n_seq
    place = lax.axis_index("seq")
    seqs = micro * seqs_micro
    rows = seqs * block

    vectors = (b_qkv, b_o, ln1_gain, ln1_bias, b_in, b_out, ln2_gain, ln2_bias)
    sizes = [v.shape[0] for v in vectors]
    cuts = [sum(sizes[:i]) for i in range(len(sizes) + 1)]
    idents = seg_ids.reshape(seqs, block)
    shard_rows = w_qkv.shape[0]
    tiled = shard_rows % 8 == 0
    ids_b = idents[:, -1].astype(bf16)

    def as_rows(parts):
        t = jnp.stack([jnp.pad(t, (0, 128 - t.shape[0])) for t in parts])
        return jnp.pad(t, ((0, shard_rows - len(parts)), (0, 0)))

    order = (1, 2, 3, 5, 6, 7, 4)
    half = w_qkv.shape[1] // 2
    x = inputs.reshape(rows, width)
    dims = (block, heads, d)
    idents_f = idents.astype(f32)
    tail_gate = (idents_f == idents_f[:, -1:]).astype(f32)
    zero = jnp.zeros_like(projection[::2])
    proj = jnp.stack(
        [
            jnp.concatenate([projection[0::2], zero], axis=1),
            jnp.concatenate([zero, projection[1::2]], axis=1),
        ],
        axis=1,
    ).reshape(heads, 2 * d, m)
    f_cols = w_in.shape[1]
    if tiled:
        first = jnp.concatenate([w_qkv[:, :half], as_rows((b_qkv, ids_b))], axis=1)
        gather_a, gather_b = Gather(first, False), Gather(w_qkv[:, half:], True)
        ties = ()
        for _ in range(1):
            ties = (gather_a.step(), gather_b.step())
        packed = call_pack(w_o, w_in, w_out, as_rows([vectors[i] for i in order]), ties)
        gather_a.rest()
        gather_b.rest()
        weights = (lax.all_gather(packed, AXES, axis=0, tiled=True),)
        ids = jnp.concatenate([t[:, 1, half : half + seqs] for t in (gather_a.buf, gather_a.other)])
        device = lax.axis_index("batch") * n_seq + jnp.arange(n_seq)
        index = slot(gather_a.order, my_flat(), device) + ((device ^ my_flat()) & 1) * (n_dev // 2)
        chosen = (index[:, None] == jnp.arange(n_dev)[None, :]).astype(f32)
        last_all = jnp.sum(chosen[:, :, None] * ids.astype(f32)[None], axis=1)
        q, k, v, phq, phk, tails, w_a, w_b = call_features_tiled(
            x, gather_a, gather_b, proj, tail_gate.reshape(rows, 1), shard_rows, *dims
        )
    else:
        flat = jnp.concatenate(vectors + (ids_b,))
        flat = jnp.pad(flat, (0, -flat.shape[0] % 128)).reshape(-1, 128)
        used = flat.shape[0]
        flat = jnp.pad(flat, ((0, shard_rows - used), (0, 0)))
        w_a = gather_rows(jnp.concatenate([w_qkv[:, :half], flat], axis=1), False)
        w_b = gather_rows(w_qkv[:, half:], True)
        packed = w_a[:, half:].reshape(n_dev, shard_rows, 128)[:, :used].reshape(n_dev, -1)
        whole = [
            packed[:, cuts[i] : cuts[i] + sizes[i]].reshape(1, -1).astype(f32)
            for i in range(len(sizes))
        ]
        ids_all = packed[:, cuts[-1] : cuts[-1] + seqs].reshape(-1, n_seq, seqs).astype(f32)
        last_all = lax.dynamic_index_in_dim(ids_all, lax.axis_index("batch"), 0, False)
        rows_of = [whole[i] for i in order[:6]]
        weights = (
            gather_rows(w_o, False), gather_rows(w_in, True), gather_rows(w_out, False),
            jnp.concatenate(rows_of + rows_of[:2]), jnp.concatenate([whole[4]] * 8),
        )
        q, k, v, phq, phk, tails = call_features(
            x, w_a, w_b, whole[0], proj, tail_gate.reshape(rows, 1), *dims
        )

    pre_all = jnp.concatenate([-jnp.ones_like(last_all[:1]), last_all[:-1]], axis=0)
    pre_ident = lax.dynamic_index_in_dim(pre_all, place, 0, False)
    gates = jnp.stack(
        [
            idents_f,
            tail_gate,
            (idents_f == pre_ident[:, None]).astype(f32),
        ],
        axis=-1,
    ).reshape(rows, 3)
    gates = jnp.pad(gates, ((0, 0), (0, 5)))
    id_rows = idents_f[:, None, :]
    amat, nd, done = call_local(phq, phk, v, gates, id_rows, *dims)
    pre = exclusive_scan(tails, last_all, False, lambda sent: [done])
    (y, dr1, dnum, dden, dpre, attn, dao, h1, act, dfo, df, sums, sum_in) = call_middle(
        x, cotangent.reshape(rows, width), phq, nd, pre, gates, weights, tiled,
        shard_rows, f_cols, *dims,
    )
    core = (place & 1).astype(jnp.int32).reshape(1)

    def grad(a, b):
        return mm_tn(a, b).astype(bf16)

    halves, scatters = [], []

    def run_beside(sent):
        zeros = []
        if tiled:
            keep_i, send_i, keep_o, send_o, done = call_grads(
                core, attn, dao, h1, df, act, dfo, sums, sum_in, sent, shard_rows
            )
            zeros = [0.0]
            wide, tall = (keep_i, True, send_i), (keep_o, False, send_o)
        else:
            pieces = [t.reshape(n_dev, -1) for t in [sums[i] for i in range(6)] + [sum_in[0]]]
            vec = jnp.concatenate(pieces, axis=1)
            vec = jnp.pad(vec, ((0, 0), (0, -vec.shape[1] % 128))).reshape(n_dev, -1, 128)
            vec = jnp.pad(vec, ((0, 0), (0, shard_rows - vec.shape[1]), (0, 0))).astype(bf16)
            wide = jnp.concatenate([grad(h1, df).reshape(n_dev, shard_rows, -1), vec], axis=2)
            tall = [grad(act, dfo).reshape(n_dev, -1, width), grad(attn, dao).reshape(n_dev, -1, width)]
            wide, tall = (wide, True), (jnp.concatenate(tall, axis=1), False)
        scatters.append(Scatter(*wide))
        scatters.append(Scatter(*tall))
        for i in range(seqs // STEP_SEQS):
            halves.append(
                call_back_query(
                    i, q, v, phq, phk, amat, dnum, dden, pre, gates, id_rows, proj,
                    (), *dims
                )
            )
        return zeros + [t[3] for t in halves]

    def start_scatters(value):
        first = [t.step() for t in scatters]
        value, *first = lax.optimization_barrier((value, *first))
        for t, buf in zip(scatters, first):
            t.buf = buf
        return value

    back = exclusive_scan(dpre, pre_all, True, run_beside, start_scatters)
    scatter_i, scatter_o = scatters
    dqs, dvs, dscts, dones = zip(*halves)
    dq = jnp.concatenate(dqs)
    ties = ()
    dkv = call_back_key(k, v, phq, phk, dvs, dscts, back, gates, proj, ties, *dims)
    ties = ()
    if tiled:
        keep_a, send_a, keep_b, send_b = call_first_grads(core, x, dq, dkv, ties, shard_rows)
        scatter_a = Scatter(keep_a, False, send_a)
        scatter_b = Scatter(keep_b, True, send_b)
    else:
        dqkv = jnp.concatenate([dq, dkv], axis=1)
        gw = grad(x, dqkv).reshape(n_dev, shard_rows, -1)
        vec = jnp.sum(dqkv, axis=0, dtype=f32).reshape(n_dev, 1, -1)
        vec = jnp.pad(vec, ((0, 0), (0, shard_rows - 1), (0, 128 - sizes[0]))).astype(bf16)
        scatter_a = Scatter(jnp.concatenate([gw[:, :, :half], vec], axis=2), False)
        scatter_b = Scatter(gw[:, :, half:], True)
    ties = (scatter_a.step(), scatter_b.step()) + (scatter_i.step(), scatter_o.step())
    dx, done = call_input_grad(dq, dkv, w_a, w_b, dr1, ties, STEP_SEQS * block)
    scatter_a.step(done)
    scatter_b.step(done)
    part_a = scatter_a.rest()
    part_b = scatter_b.rest()
    part_i = scatter_i.rest()
    part_o = scatter_o.rest()
    g_w_out, g_w_o = part_o[: w_out.shape[0]], part_o[w_out.shape[0] :]
    g_w_in = part_i[:, :f_cols]
    lengths = [sizes[i] for i in order]
    if tiled:
        vec_grads = [part_i[i, f_cols : f_cols + n] for i, n in enumerate(lengths)]
    else:
        vec = part_i[:, f_cols:].reshape(-1)
        starts = [sum(lengths[:i]) for i in range(len(lengths))]
        vec_grads = [vec[at : at + n] for at, n in zip(starts, lengths)]
    (g_b_o, g_gain_one, g_shift_one, g_b_out, g_gain_two, g_shift_two, g_b_in) = vec_grads
    g_w_qkv = jnp.concatenate([part_a[:, :half], part_b], axis=1)
    g_b_qkv = part_a[0, half : half + sizes[0]]
    return (
        y.reshape(inputs.shape),
        dx.reshape(inputs.shape),
        g_w_qkv,
        g_b_qkv,
        g_w_o,
        g_b_o,
        g_gain_one,
        g_shift_one,
        g_w_in,
        g_b_in,
        g_w_out,
        g_b_out,
        g_gain_two,
        g_shift_two,
    )


def solution(mesh):
    rows = P(AXES, None)
    vec = P(AXES)
    tok = P(None, "batch", "seq", None)
    in_specs = (
        tok,
        P(None, "batch", "seq"),
        tok,
        P(),
        rows,
        vec,
        rows,
        vec,
        vec,
        vec,
        rows,
        vec,
        rows,
        vec,
        vec,
        vec,
    )
    out_specs = (tok, tok, rows, vec, rows, vec, vec, vec, rows, vec, rows, vec, vec, vec)
    return jax.shard_map(body, mesh=mesh, in_specs=in_specs, out_specs=out_specs, check_vma=False)
```

```python
import math
from functools import partial

import jax
import jax.numpy as jnp
from jax import lax
from jax.experimental import pallas as pl
from jax.experimental.pallas import tpu as pltpu
from jax.sharding import PartitionSpec as P

norm_eps = 1e-05
bf16 = jnp.bfloat16
f32 = jnp.float32
AXES = ("batch", "seq")


def flat_xor(value, mask):
    n = lax.axis_size("batch") * lax.axis_size("seq")
    return lax.ppermute(value, AXES, [(i, i ^ mask) for i in range(n)])


def log2(n):
    return n.bit_length() - 1


def gather_order(nb, ns, swap):
    seq_bits = list(range(log2(ns)))
    batch_bits = [log2(ns) + b for b in range(log2(nb))]
    low, mid, high = seq_bits[0], seq_bits[1], seq_bits[2:]
    cross = [mid] + batch_bits if not swap else batch_bits + [mid]
    return high[::-1] + cross + [low]


def my_flat():
    return lax.axis_index("batch") * lax.axis_size("seq") + lax.axis_index("seq")


def gather_rows(shard, swap):
    nb, ns = lax.axis_size("batch"), lax.axis_size("seq")
    nbits = log2(nb * ns)
    me = my_flat()
    shape = shard.shape
    buf = shard.reshape((1,) * nbits + shape)
    for bit in gather_order(nb, ns, swap):
        axis = nbits - 1 - bit
        other = flat_xor(buf, 1 << bit)
        mine = (me >> bit) & 1
        buf = jnp.where(
            mine == 1,
            jnp.concatenate([other, buf], axis),
            jnp.concatenate([buf, other], axis),
        )
    return buf.reshape((nb * ns * shape[0],) + shape[1:])


class Gather:
    def __init__(self, shard, swap):
        self.bits = gather_order(lax.axis_size("batch"), lax.axis_size("seq"), swap)
        self.order = tuple(self.bits[:-1])
        self.buf = shard.reshape((1,) + shard.shape[-2:])

    def step(self):
        other = flat_xor(self.buf, 1 << self.bits.pop(0))
        if self.bits:
            self.buf = jnp.concatenate([self.buf, other], axis=0)
        else:
            self.other = other
        return self.buf

    def rest(self):
        while self.bits:
            self.step()
        return self.buf, self.other


def slot(order, me, device):
    far = me ^ device
    at = (far >> order[0]) & 1
    for j in range(1, len(order)):
        at = at + (((far >> order[j]) & 1) << j)
    return at


class Scatter:
    def __init__(self, buf, swap, send=None):
        nbits = log2(lax.axis_size("batch") * lax.axis_size("seq"))
        self.bits = gather_order(lax.axis_size("batch"), lax.axis_size("seq"), swap)[::-1]
        self.send = send
        self.buf = buf if send is not None else buf.reshape((2,) * nbits + buf.shape[1:])
        self.tail = buf.shape[1:]
        self.nbits = nbits

    def step(self, beside=0.0):
        bit = self.bits.pop(0)
        axis = self.nbits - 1 - bit
        mine = (my_flat() >> bit) & 1
        if self.send is None:
            keep = lax.dynamic_index_in_dim(self.buf, mine, axis, True)
            send = lax.dynamic_index_in_dim(self.buf, 1 - mine, axis, True)
        else:
            keep, send, self.send = self.buf, self.send, None
        got = flat_xor(send, 1 << bit)
        buf = keep.astype(f32) + got.astype(f32) + beside
        if self.bits:
            buf = buf.astype(bf16)
        else:
            buf = buf.reshape(self.tail)
        if keep.ndim == 3 and self.bits:
            buf = buf.reshape((2,) * (self.nbits - 1) + (1,) + self.tail)
        self.buf = buf
        return buf

    def rest(self):
        while self.bits:
            self.step()
        return self.buf


def seq_perm(value, pairs):
    return lax.ppermute(value, "seq", pairs)


def exclusive_scan(tails, ids, rev, beside, final=lambda value: value):
    n = lax.axis_size("seq")
    place = lax.axis_index("seq")
    if rev:
        ids = ids[::-1]
    p = n - 1 - place if rev else place

    def at(q):
        return n - 1 - q if rev else q

    def move(value, pairs):
        return seq_perm(value, [(at(a), at(b)) for a, b in pairs])

    def gated(g, value):
        return g * value.astype(f32)

    c = p & 1
    x = (p >> 1) & 1
    base = p - (p & 3)
    pair = p - c
    seqs = tails.shape[0]
    rest = tails.shape[2:]
    wanted = [(pair, pair + 1), (base + 1, base + 3), (base - 1, base + 1), (pair - 1, pair)]
    step = 1
    while step * 4 < n:
        wanted += [(base + 3 - 4 * step, base - 1), (base + 3 - 4 * step, base + 3)]
        step *= 2
    where = jnp.stack([jnp.clip(t, 0, n - 1) for pair_of in wanted for t in pair_of])
    chosen = (where[:, None] == jnp.arange(n)[None, :]).astype(f32)
    keys = jnp.sum(chosen[:, :, None] * ids[None], axis=1)
    gates = (keys[0::2] == keys[1::2]).astype(f32)
    gates = jnp.broadcast_to(gates[:, :, None, None], gates.shape + (1, rest[-1]))
    gate_core, gate_pair, gate_plane, gate_entry = (gates[i] for i in range(4))
    parts = tails.reshape((seqs, 2, 2) + rest)

    def pick(a, i, axis):
        return lax.dynamic_index_in_dim(a, i, axis, False)

    core = [(i, i ^ 1) for i in range(n)]
    across = [(i, i ^ 2) for i in range(n)]
    own = pick(parts, c, 2)
    other = move(pick(parts, 1 - c, 2), core)
    first = jnp.where(c == 0, own, other)
    second = jnp.where(c == 0, other, own)
    pair_sum = second.astype(f32) + gated(gate_core[:, None], first)
    pair_mine = pick(pair_sum, x, 1)
    sent = pick(pair_sum, 1 - x, 1).astype(bf16)
    beside = beside(sent)
    pair_other = move(sent, across).astype(f32)
    low = jnp.where(x == 0, pair_mine, pair_other)
    high = jnp.where(x == 0, pair_other, pair_mine)
    total = high + gated(gate_pair, low)
    before = jnp.zeros_like(total)
    step = 1
    while step * 4 < n:
        total = total + (beside.pop(0) if beside else 0.0)
        got = move(
            total.astype(bf16), [(i, i + 4 * step) for i in range(n - 4 * step)]
        )
        at_step = 4 + 2 * log2(step)
        before = before + gated(gates[at_step], got)
        total = total + gated(gates[at_step + 1], got)
        step *= 2
    before_high = low + gated(gate_plane, before)
    mine = jnp.where(x == 0, before, before_high)
    theirs = jnp.where(x == 0, before_high, before) + sum(beside, jnp.zeros((1, 1), f32))
    got = move(theirs.astype(bf16), across)
    mine_b = mine.astype(bf16)
    entry = jnp.where(x == 0, jnp.stack([mine_b, got], 1), jnp.stack([got, mine_b], 1))
    after = first.astype(f32) + gated(gate_entry[:, None], entry)
    after_b = after.astype(bf16)
    mine = jnp.where(c == 0, entry, after_b)
    theirs = final(jnp.where(c == 0, after_b, entry))
    got = move(theirs, core)
    result = jnp.where(c == 0, jnp.stack([mine, got], 2), jnp.stack([got, mine], 2))
    return result.reshape(tails.shape)


NT = (((1,), (1,)), ((), ()))
VMEM_LIMIT = 56 * 1024 * 1024


def mm(a, b):
    return jnp.dot(a, b, preferred_element_type=f32)


def mm_nt(a, b):
    return lax.dot_general(a, b, NT, preferred_element_type=f32)


def lane_low(shape, half):
    return lax.broadcasted_iota(jnp.int32, shape, 1) < half


def half_sums(value, low):
    first = jnp.sum(jnp.where(low, value, 0.0), axis=1, keepdims=True)
    second = jnp.sum(jnp.where(low, 0.0, value), axis=1, keepdims=True)
    return first, second


def state_rows(ref, s, h, heads, d):
    per = heads // 4
    return ref[s, h // per, pl.ds((h % per) * d, d), :]


def total_rows(ref, s, heads, d):
    per = heads // 4
    out = []
    for q in range(4):
        rows = ref[s, q, pl.ds(per * d, 16), :].astype(f32)
        out += [rows[j : j + 1] for j in range(per)]
    return out


def pair_rows(first, second, core):
    return jnp.concatenate([first, second] if core == 0 else [second, first], axis=0)


def lay_out(pieces, width, out_ref):
    tiles = out_ref.shape[1] // 128
    lane = lax.broadcasted_iota(jnp.int32, (8, 128), 1)
    acc = [jnp.zeros((8, 128), f32)] * tiles
    for j, piece in enumerate(pieces):
        t, s = divmod(j * width, 128)
        turned = pltpu.roll(jnp.where(lane < width, piece, 0.0), s, 1) if s else jnp.where(lane < width, piece, 0.0)
        if s + width <= 128:
            acc[t] = acc[t] + turned
        else:
            acc[t] = acc[t] + jnp.where(lane >= s, turned, 0.0)
            acc[t + 1] = acc[t + 1] + jnp.where(lane < s, turned, 0.0)
    for t in range(tiles):
        out_ref[:, t * 128 : (t + 1) * 128] = acc[t]


def cut_out(values, width, count):
    tiles = values.shape[1] // 128
    lane = lax.broadcasted_iota(jnp.int32, (8, 128), 1)
    out = []
    for j in range(count):
        t, s = divmod(j * width, 128)
        piece = values[:, t * 128 : (t + 1) * 128]
        if s + width > 128:
            piece = jnp.where(lane >= s, piece, values[:, (t + 1) * 128 : (t + 2) * 128])
        out.append(pltpu.roll(piece, 128 - s, 1) if s else piece)
    return out


def fill_first(orders, shard_rows, piece, me_ref, wa_ref, wb_ref, bias, own_a, oth_a, own_b, oth_b, core):
    me = me_ref[0]
    unit = 2 * shard_rows
    count = wa_ref.shape[0] // unit

    def one(j, carry):
        rows = pl.ds(pl.multiple_of(j * unit, 16), unit)
        p = slot(orders[0], me, 2 * j)
        wa_ref[rows, :] = pair_rows(own_a[p], oth_a[p], core)
        p = slot(orders[1], me, 2 * j)
        wb_ref[rows, :] = pair_rows(own_b[p], oth_b[p], core)
        return carry

    lax.fori_loop(0, count, one, 0)
    first = wa_ref.shape[1] - 128
    pieces = []
    for j in range(count):
        two = wa_ref[j * unit : (j + 1) * unit, first:].astype(f32)
        pieces += [two[i * shard_rows : i * shard_rows + 8] for i in range(2)]
    lay_out(pieces, piece, bias)


def features_tiled_kernel(
    block, heads, d, orders, shard_rows, me_ref, x_ref, own_a, oth_a, own_b, oth_b, proj_ref, tg_ref,
    q_ref, k_ref, v_ref, phq_ref, phk_ref, tail_ref, wa_ref, wb_ref, z_scr, bias,
):
    @pl.when(pl.program_id(0) == 0)
    def _():
        piece = bias.shape[1] // (wa_ref.shape[0] // shard_rows)
        for core in range(2):
            pl.when(me_ref[0] % 2 == core)(
                partial(
                    fill_first, orders, shard_rows, piece, me_ref, wa_ref, wb_ref, bias,
                    own_a, oth_a, own_b, oth_b, core,
                )
            )

    features_kernel(
        block, heads, d, x_ref, wa_ref, wb_ref, bias, proj_ref, tg_ref,
        q_ref, k_ref, v_ref, phq_ref, phk_ref, tail_ref, z_scr,
    )


def features_kernel(
    block, heads, d, x_ref, wa_ref, wb_ref, b_ref, proj_ref, tg_ref,
    q_ref, k_ref, v_ref, phq_ref, phk_ref, tail_ref, z_scr,
):
    width = heads * d
    m = proj_ref.shape[2]
    pair = 2 * d
    scale = d ** (-0.25)
    root = m ** (-0.5)
    x = x_ref[...]
    rows = x.shape[0]
    low = lane_low((rows, pair), d)
    chunk = width // 2
    for t, (z_ref, ph_ref) in ((1, (k_ref, phk_ref)), (2, (v_ref, None)), (0, (q_ref, phq_ref))):
        for i in range(2):
            col = t * width + i * chunk
            w = wa_ref[:, col : col + chunk] if col < 3 * chunk else wb_ref[:, col - 3 * chunk : col - 2 * chunk]
            z = mm(x, w) + b_ref[0:1, col : col + chunk]
            z = (z * scale if ph_ref is not None else z).astype(bf16)
            z_ref[:, i * chunk : (i + 1) * chunk] = z
            if ph_ref is None:
                continue
            for p in range(chunk // pair):
                zp = z[:, p * pair : (p + 1) * pair]
                zf = zp.astype(f32)
                sums = half_sums(zf * zf, low)
                for e in range(2):
                    h = 2 * (i * (chunk // pair) + p) + e
                    u = mm(zp, proj_ref[h])
                    ph_ref[:, h * m : (h + 1) * m] = (jnp.exp(u - 0.5 * sums[e]) * root).astype(bf16)
    per = heads // 4
    for s in range(rows // block):
        r = slice(s * block, (s + 1) * block)
        tg = tg_ref[r, :].astype(bf16)
        for p in range(heads // 2):
            v_t = v_ref[r, p * pair : (p + 1) * pair].T
            for e in range(2):
                h = 2 * p + e
                kt = phk_ref[r, h * m : (h + 1) * m] * tg
                lhs = jnp.concatenate([v_t[e * d : (e + 1) * d], jnp.ones((16, block), bf16)], 0)
                res = mm(lhs, kt)
                tail_ref[s, h // per, pl.ds((h % per) * d, d), :] = res[:d].astype(bf16)
                z_scr[h % per : h % per + 1, :] = res[d : d + 1]
                if h % per == per - 1:
                    tail_ref[s, h // per, pl.ds(per * d, 16), :] = z_scr[...].astype(bf16)


def local_kernel(
    block, heads, d, phq_ref, phk_ref, v_ref, col_ref, row_ref, amat_ref, nd_ref, done_ref
):
    done_ref[...] = jnp.zeros_like(done_ref)
    m = phq_ref.shape[1] // heads
    pair = 2 * d
    low = lane_low((block, pair), d)
    t_ix = lax.broadcasted_iota(jnp.int32, (block, block), 0)
    j_ix = lax.broadcasted_iota(jnp.int32, (block, block), 1)
    causal = t_ix >= j_ix
    for s in range(v_ref.shape[0] // block):
        r = slice(s * block, (s + 1) * block)
        mask = jnp.logical_and(causal, col_ref[r, 0:1] == row_ref[s])
        for p in range(heads // 2):
            v_pair = v_ref[r, p * pair : (p + 1) * pair]
            for e in range(2):
                h = 2 * p + e
                sc = mm_nt(phq_ref[r, h * m : (h + 1) * m], phk_ref[r, h * m : (h + 1) * m])
                am = jnp.where(mask, sc, 0.0).astype(bf16)
                amat_ref[s, h] = am
                v_one = jnp.where(low if e == 0 else ~low, v_pair, jnp.ones_like(v_pair))
                nd_ref[r, h * pair : (h + 1) * pair] = mm(am, v_one)


def layer_norm(row_vals, gain, shift):
    inv = 1.0 / row_vals.shape[1]
    centred = row_vals - jnp.sum(row_vals, axis=1, keepdims=True) * inv
    rs = lax.rsqrt(jnp.sum(centred * centred, axis=1, keepdims=True) * inv + norm_eps)
    normed = centred * rs
    return normed * gain + shift, normed, rs


def layer_norm_back(dn, normed, rs):
    inv = 1.0 / dn.shape[1]
    mean = jnp.sum(dn, axis=1, keepdims=True) * inv
    proj = jnp.sum(dn * normed, axis=1, keepdims=True) * inv
    return rs * (dn - mean - normed * proj)


def group_rows(shard_rows):
    return math.lcm(shard_rows, 16) // shard_rows


def natural_rows(stage, out_ref, shard_rows, width):
    groups = stage.shape[1] // width
    per = group_rows(shard_rows)
    unit = per * shard_rows

    def one(i, carry):
        cols = [
            stage[pl.ds(pl.multiple_of(i * unit, 16), unit), g * width : (g + 1) * width]
            for g in range(groups)
        ]
        pieces = [c[j * shard_rows : (j + 1) * shard_rows] for j in range(per) for c in cols]
        out_ref[pl.ds(pl.multiple_of(i * unit * groups, 16), unit * groups), :] = jnp.concatenate(
            pieces, axis=0
        )
        return carry

    lax.fori_loop(0, stage.shape[0] // unit, one, 0)


def fill_rest(shard_rows, w_out_ref, vec_scr, b_in_scr, stage, vec_stage):
    width = w_out_ref.shape[1]
    natural_rows(stage, w_out_ref, shard_rows, width)
    unit = 2 * shard_rows
    pieces = []
    for j in range(vec_stage.shape[0] // unit):
        two = vec_stage[j * unit : (j + 1) * unit, :].astype(f32)
        pieces += [two[i * shard_rows : i * shard_rows + 8] for i in range(2)]
    lay_out(pieces, shard_rows, vec_scr)
    lay_out(pieces, w_out_ref.shape[0] // len(pieces), b_in_scr)


def middle_kernel(
    block, heads, d, ff_chunk,
    tiled, shard_rows, x_ref, cot_ref, phq_ref, nd_ref, pre_ref, gate_ref,
    *refs
):
    ins = refs[: 1 if tiled else 5]
    middle_parts(
        block, heads, d, ff_chunk, tiled, shard_rows, x_ref, cot_ref, phq_ref, nd_ref,
        pre_ref, gate_ref, ins, *refs[len(ins) :],
    )


def middle_parts(
    block, heads, d, ff_chunk, tiled, shard_rows, x_ref, cot_ref, phq_ref, nd_ref, pre_ref,
    gate_ref, ins,
    y_ref, dr1_ref, dnum_ref, dden_ref, dpre_ref, attn_ref, dao_ref, h1_ref, act_ref, dfo_ref,
    df_ref, sums_ref, sum_in_ref,
    attf, rden, dgel, z_scr, w_o_ref, w_in_ref, w_out_ref, vec_ref, b_in_ref, sems, *stages
):
    step = pl.program_id(0)
    m = phq_ref.shape[1] // heads
    width = heads * d
    ff = w_in_ref.shape[1]

    def copies():
        if tiled:
            cuts = [0, width, width + ff, width + 2 * ff, width + 2 * ff + 128]
            sources = [ins[0].at[:, i:j] for i, j in zip(cuts, cuts[1:])]
            places = (w_o_ref, w_in_ref) + tuple(stages)
        else:
            sources, places = ins, (w_o_ref, w_in_ref, w_out_ref, vec_ref, b_in_ref)
        return [
            pltpu.make_async_copy(src, dst, sems.at[i])
            for i, (src, dst) in enumerate(zip(sources, places))
        ]

    @pl.when(step == 0)
    def _():
        for c in copies():
            c.start()

    pair = 2 * d
    low = lane_low((block, pair), d)
    rows = x_ref.shape[0]
    seqs = rows // block
    ones = jnp.ones((d, 1), f32)
    for s in range(seqs):
        r = slice(s * block, (s + 1) * block)
        g = gate_ref[r, 2:3]
        zs = total_rows(pre_ref, s, heads, d)
        for p in range(heads // 2):
            tot = []
            for e in range(2):
                h = 2 * p + e
                st = state_rows(pre_ref, s, h, heads, d)
                zb = (ones * zs[h]).astype(bf16)
                rhs = jnp.concatenate([st, zb] if e == 0 else [zb, st], 0)
                tot.append(
                    nd_ref[r, h * pair : (h + 1) * pair]
                    + g * mm_nt(phq_ref[r, h * m : (h + 1) * m], rhs)
                )
            num = jnp.where(low, tot[0], tot[1])
            den = pltpu.roll(jnp.where(low, tot[1], tot[0]), d, 1)
            rd = 1.0 / den
            c = slice(p * pair, (p + 1) * pair)
            att = num * rd
            attf[r, c] = att
            rden[r, c] = rd
            attn_ref[r, c] = att.astype(bf16)

    @pl.when(step == 0)
    def _():
        for c in copies():
            c.wait()
        if tiled:
            fill_rest(shard_rows, w_out_ref, vec_ref, b_in_ref, *stages)

    b_o, gain1, shift1, b_out, gain2, shift2 = (vec_ref[i : i + 1, :] for i in range(6))
    r1 = x_ref[...].astype(f32) + mm(attn_ref[...], w_o_ref[...]) + b_o
    h1, n1, rs1 = layer_norm(r1, gain1, shift1)
    h1b = h1.astype(bf16)
    h1_ref[...] = h1b
    fo = None
    for c0 in range(0, ff, ff_chunk):
        c = slice(c0, c0 + ff_chunk)
        f = mm(h1b, w_in_ref[:, c]) + b_in_ref[6:7, c]
        phi = 0.5 + 0.5 * lax.erf(f * (0.5**0.5))
        act = (f * phi).astype(bf16)
        act_ref[:, c] = act
        dgel[:, c] = phi + f * (jnp.exp(-0.5 * f * f) * (1.0 / (2.0 * math.pi) ** 0.5))
        part = mm(act, w_out_ref[c, :])
        fo = part if fo is None else fo + part
    y, n2, rs2 = layer_norm(h1 + fo + b_out, gain2, shift2)
    y_ref[...] = y.astype(bf16)
    dy = cot_ref[...].astype(f32)

    def add_sum(i, value):
        row = jnp.sum(value, axis=0, keepdims=True)

        @pl.when(step == 0)
        def _():
            sums_ref[i : i + 1, :] = row

        @pl.when(step > 0)
        def _():
            sums_ref[i : i + 1, :] += row

    add_sum(4, dy * n2)
    add_sum(5, dy)
    dr2 = layer_norm_back(dy * gain2, n2, rs2)
    dfo = dr2.astype(bf16)
    dfo_ref[...] = dfo
    add_sum(3, dfo.astype(f32))
    dh1 = dr2
    for c0 in range(0, ff, ff_chunk):
        c = slice(c0, c0 + ff_chunk)
        df = (mm_nt(dfo, w_out_ref[c, :]) * dgel[:, c]).astype(bf16)
        df_ref[:, c] = df
        row = jnp.sum(df.astype(f32), axis=0, keepdims=True)

        @pl.when(step == 0)
        def _():
            sum_in_ref[:, c] = row

        @pl.when(step > 0)
        def _():
            sum_in_ref[:, c] += row

        dh1 = dh1 + mm_nt(df, w_in_ref[:, c])
    add_sum(1, dh1 * n1)
    add_sum(2, dh1)
    dr1 = layer_norm_back(dh1 * gain1, n1, rs1)
    dr1_ref[...] = dr1
    dao = dr1.astype(bf16)
    dao_ref[...] = dao
    add_sum(0, dao.astype(f32))
    dattn = mm_nt(dao, w_o_ref[...])
    dnum_ref[...] = (dattn * rden[...]).astype(bf16)
    prod = dattn * attf[...]
    lane = lax.broadcasted_iota(jnp.int32, (rows, 128), 1)
    low_rows = lane_low((rows, pair), d)
    dden = jnp.zeros((rows, 128), f32)
    for p in range(heads // 2):
        c = slice(p * pair, (p + 1) * pair)
        sums = half_sums(prod[:, c], low_rows)
        for e in range(2):
            col = -sums[e] * rden[:, p * pair + e * d : p * pair + e * d + 1]
            dden = jnp.where(lane == 2 * p + e, col, dden)
    dden = dden.astype(bf16).astype(f32)
    dden_ref[...] = dden
    per = heads // 4
    for s in range(seqs):
        r = slice(s * block, (s + 1) * block)
        g = gate_ref[r, 2:3]
        ddt = (dden[r] * g).T[:16].astype(bf16)
        for p in range(heads // 2):
            gdt = (dnum_ref[r, p * pair : (p + 1) * pair] * g.astype(bf16)).T
            for e in range(2):
                h = 2 * p + e
                lhs = jnp.concatenate([gdt[e * d : (e + 1) * d], ddt], 0)
                res = mm(lhs, phq_ref[r, h * m : (h + 1) * m])
                dpre_ref[s, h // per, pl.ds((h % per) * d, d), :] = res[:d].astype(bf16)
                z_scr[h % per : h % per + 1, :] = res[d + h : d + h + 1]
                if h % per == per - 1:
                    dpre_ref[s, h // per, pl.ds(per * d, 16), :] = z_scr[...].astype(bf16)


def back_query_kernel(
    block, heads, d,
    q_ref, v_ref, phq_ref, phk_ref, amat_ref, dnum_ref, dden_ref, pre_ref, gate_ref, row_ref,
    proj_ref,
    dq_ref, dv_ref, dsct_ref, done_ref,
):
    done_ref[...] = jnp.zeros_like(done_ref)
    m = phq_ref.shape[1] // heads
    pair = 2 * d
    scale = d ** (-0.25)
    low = lane_low((block, pair), d)
    t_ix = lax.broadcasted_iota(jnp.int32, (block, block), 0)
    j_ix = lax.broadcasted_iota(jnp.int32, (block, block), 1)
    causal = t_ix >= j_ix
    for s in range(q_ref.shape[0] // block):
        r = slice(s * block, (s + 1) * block)
        g = gate_ref[r, 2:3]
        gb = g.astype(bf16)
        mask = jnp.logical_and(causal, gate_ref[r, 0:1] == row_ref[s])
        zs = total_rows(pre_ref, s, heads, d)
        for p in range(heads // 2):
            c = slice(p * pair, (p + 1) * pair)
            dn = dnum_ref[r, c]
            v_pair = v_ref[r, c]
            qp = q_ref[r, c].astype(f32)
            st = jnp.concatenate(
                [state_rows(pre_ref, s, 2 * p, heads, d), state_rows(pre_ref, s, 2 * p + 1, heads, d)], 0
            )
            dv = None
            dq = None
            for e in range(2):
                h = 2 * p + e
                mine = low if e == 0 else ~low
                hm = slice(h * m, (h + 1) * m)
                dnm = jnp.where(mine, dn, jnp.zeros_like(dn))
                dd = dden_ref[r, h : h + 1]
                dsc = jnp.where(mask, mm_nt(dnm, v_pair) + dd, 0.0)
                dsct_ref[s, h] = dsc.T.astype(bf16)
                dph = mm(
                    jnp.concatenate([dsc.astype(bf16), dnm * gb], 1),
                    jnp.concatenate([phk_ref[r, hm], st], 0),
                ) + (g * dd) * zs[h]
                t = dph * phq_ref[r, hm].astype(f32)
                part = mm_nt(t.astype(bf16), proj_ref[h]) - jnp.where(
                    mine, jnp.sum(t, axis=1, keepdims=True) * qp, 0.0
                )
                dq = part if dq is None else dq + part
                part = mm(amat_ref[s, h].T, dnm)
                dv = part if dv is None else dv + part
            dq_ref[r, c] = (dq * scale).astype(bf16)
            dv_ref[r, c] = dv


def back_key_kernel(
    block, heads, d,
    k_ref, v_ref, phq_ref, phk_ref, dv_ref, dsct_ref, dtail_ref, gate_ref, proj_ref,
    dkv_ref,
):
    m = phq_ref.shape[1] // heads
    pair = 2 * d
    width = heads * d
    scale = d ** (-0.25)
    low = lane_low((block, pair), d)
    for s in range(k_ref.shape[0] // block):
        r = slice(s * block, (s + 1) * block)
        tg = gate_ref[r, 1:2]
        tgb = tg.astype(bf16)
        zs = total_rows(dtail_ref, s, heads, d)
        for p in range(heads // 2):
            c = slice(p * pair, (p + 1) * pair)
            v_pair = v_ref[r, c]
            kp = k_ref[r, c].astype(f32)
            ds = jnp.concatenate(
                [
                    state_rows(dtail_ref, s, 2 * p, heads, d),
                    state_rows(dtail_ref, s, 2 * p + 1, heads, d),
                ],
                0,
            )
            dk = None
            inter = []
            for e in range(2):
                h = 2 * p + e
                mine = low if e == 0 else ~low
                hm = slice(h * m, (h + 1) * m)
                vm = jnp.where(mine, v_pair, jnp.zeros_like(v_pair)) * tgb
                phk = phk_ref[r, hm]
                dph = mm(
                    jnp.concatenate([dsct_ref[s, h], vm], 1),
                    jnp.concatenate([phq_ref[r, hm], ds], 0),
                ) + tg * zs[h]
                t = dph * phk.astype(f32)
                part = mm_nt(t.astype(bf16), proj_ref[h]) - jnp.where(
                    mine, jnp.sum(t, axis=1, keepdims=True) * kp, 0.0
                )
                dk = part if dk is None else dk + part
                inter.append(mm_nt(phk, ds))
            dkv_ref[r, c] = (dk * scale).astype(bf16)
            dv = dv_ref[r, c] + tg * jnp.where(low, inter[0], inter[1])
            dkv_ref[r, width + p * pair : width + (p + 1) * pair] = dv.astype(bf16)


def params(micros):
    return dict(
        compiler_params=pltpu.CompilerParams(
            dimension_semantics=("arbitrary",), vmem_limit_bytes=VMEM_LIMIT
        ),
        cost_estimate=pl.CostEstimate(
            flops=int(micros * 8e9), bytes_accessed=int(micros * 1e6), transcendentals=0
        ),
    )


def row_spec(rows, cols):
    return pl.BlockSpec((rows, cols), lambda i: (i, 0))


def lead_spec(shape):
    return pl.BlockSpec(shape, lambda i: (i,) + (0,) * (len(shape) - 1))


def whole_spec(shape):
    return pl.BlockSpec(shape, lambda i: (0,) * len(shape))


def sds(shape, dtype):
    return jax.ShapeDtypeStruct(shape, dtype)


STEP_SEQS = 2
STATE_PAD = 16


def state_shape(seqs, heads, d, m):
    return (seqs, 4, heads // 4 * d + STATE_PAD, m)


def call_features(x, wa, wb, b, proj, tg, block, heads, d):
    rows, width = x.shape
    m = proj.shape[2]
    n = STEP_SEQS * block
    st = state_shape(STEP_SEQS, heads, d, m)
    return pl.pallas_call(
        partial(features_kernel, block, heads, d),
        grid=(rows // n,),
        in_specs=[
            row_spec(n, width), whole_spec(wa.shape), whole_spec(wb.shape), whole_spec(b.shape),
            whole_spec(proj.shape), row_spec(n, 1),
        ],
        out_specs=[row_spec(n, width)] * 3 + [row_spec(n, heads * m)] * 2 + [lead_spec(st)],
        out_shape=[sds((rows, width), bf16)] * 3
        + [sds((rows, heads * m), bf16)] * 2
        + [sds((rows // block,) + st[1:], bf16)],
        scratch_shapes=[pltpu.VMEM((16, m), f32)],
        name="features",
        **params(10),
    )(x, wa, wb, b, proj, tg)


def call_features_tiled(x, a, b, proj, tg, shard_rows, block, heads, d):
    rows, width = x.shape
    m = proj.shape[2]
    n = STEP_SEQS * block
    st = state_shape(STEP_SEQS, heads, d, m)
    parts = (a.buf, a.other, b.buf, b.other)
    wa, wb = (width, a.buf.shape[2]), (width, b.buf.shape[2])
    return pl.pallas_call(
        partial(features_tiled_kernel, block, heads, d, (a.order, b.order), shard_rows),
        grid=(rows // n,),
        in_specs=[pl.BlockSpec(memory_space=pltpu.SMEM), row_spec(n, width)]
        + [whole_spec(t.shape) for t in parts]
        + [whole_spec(proj.shape), row_spec(n, 1)],
        out_specs=[row_spec(n, width)] * 3
        + [row_spec(n, heads * m)] * 2
        + [lead_spec(st), whole_spec(wa), whole_spec(wb)],
        out_shape=[sds((rows, width), bf16)] * 3
        + [sds((rows, heads * m), bf16)] * 2
        + [sds((rows // block,) + st[1:], bf16), sds(wa, bf16), sds(wb, bf16)],
        scratch_shapes=[pltpu.VMEM((16, m), f32), pltpu.VMEM((8, 3 * width), f32)],
        name="features",
        **params(12),
    )(my_flat().astype(jnp.int32).reshape(1), x, *parts, proj, tg)


def call_local(phq, phk, v, gates, id_rows, block, heads, d):
    rows = v.shape[0]
    n = STEP_SEQS * block
    return pl.pallas_call(
        partial(local_kernel, block, heads, d),
        grid=(rows // n,),
        in_specs=[
            row_spec(n, phq.shape[1]), row_spec(n, phk.shape[1]), row_spec(n, v.shape[1]),
            row_spec(n, gates.shape[1]), lead_spec((STEP_SEQS, 1, block)),
        ],
        out_specs=[
            lead_spec((STEP_SEQS, heads, block, block)), row_spec(n, heads * 2 * d),
            whole_spec((1, 1)),
        ],
        out_shape=[
            sds((rows // block, heads, block, block), bf16), sds((rows, heads * 2 * d), f32),
            sds((1, 1), f32),
        ],
        name="local",
        **params(8),
    )(phq, phk, v, gates, id_rows)


def call_middle(x, cot, phq, nd, pre, gates, weights, tiled, shard_rows, ff, block, heads, d):
    rows, width = x.shape
    m = phq.shape[1] // heads
    n = STEP_SEQS * block
    st = (STEP_SEQS,) + pre.shape[1:]
    return pl.pallas_call(
        partial(middle_kernel, block, heads, d, 768, tiled, shard_rows),
        grid=(rows // n,),
        in_specs=[
            row_spec(n, width), row_spec(n, width), row_spec(n, phq.shape[1]),
            row_spec(n, nd.shape[1]), lead_spec(st), row_spec(n, gates.shape[1]),
        ]
        + [pl.BlockSpec(memory_space=pl.ANY)] * len(weights),
        out_specs=[
            row_spec(n, width), row_spec(n, width), row_spec(n, width), row_spec(n, 128),
            lead_spec(st), row_spec(n, width), row_spec(n, width), row_spec(n, width),
            row_spec(n, ff), row_spec(n, width), row_spec(n, ff), whole_spec((8, width)),
            whole_spec((1, ff)),
        ],
        out_shape=[
            sds((rows, width), bf16), sds((rows, width), f32), sds((rows, width), bf16),
            sds((rows, 128), f32), sds(pre.shape, bf16), sds((rows, width), bf16),
            sds((rows, width), bf16), sds((rows, width), bf16), sds((rows, ff), bf16),
            sds((rows, width), bf16), sds((rows, ff), bf16), sds((8, width), f32),
            sds((1, ff), f32),
        ],
        scratch_shapes=[
            pltpu.VMEM((n, width), f32), pltpu.VMEM((n, width), f32), pltpu.VMEM((n, ff), f32),
            pltpu.VMEM((16, m), f32), pltpu.VMEM((width, width), bf16),
            pltpu.VMEM((width, ff), bf16), pltpu.VMEM((ff, width), bf16),
            pltpu.VMEM((8, width), f32), pltpu.VMEM((8, ff), f32), pltpu.SemaphoreType.DMA((5,)),
        ]
        + ([pltpu.VMEM((width, ff), bf16), pltpu.VMEM((width, 128), bf16)] if tiled else []),
        name="middle",
        **params(31),
    )(x, cot, phq, nd, pre, gates, *weights)


def call_back_query(
    half, q, v, phq, phk, amat, dnum, dden, pre, gates, id_rows, proj, ties, block, heads, d
):
    rows, width = q.shape
    n = STEP_SEQS * block
    sq = (STEP_SEQS, heads, block, block)

    def rs(cols):
        return pl.BlockSpec((n, cols), lambda i: (half, 0))

    def ls(shape):
        return pl.BlockSpec(shape, lambda i: (half,) + (0,) * (len(shape) - 1))

    def kernel(*refs):
        back_query_kernel(block, heads, d, *refs[:11], *refs[11 + len(ties) :])

    return pl.pallas_call(
        kernel,
        grid=(1,),
        in_specs=[
            rs(width), rs(width), rs(phq.shape[1]), rs(phk.shape[1]), ls(sq), rs(width), rs(128),
            ls((STEP_SEQS,) + pre.shape[1:]), rs(gates.shape[1]), ls((STEP_SEQS, 1, block)),
            whole_spec(proj.shape),
        ]
        + [pl.BlockSpec(memory_space=pl.ANY)] * len(ties),
        out_specs=[row_spec(n, width), row_spec(n, width), lead_spec(sq), whole_spec((1, 1))],
        out_shape=[
            sds((n, width), bf16), sds((n, width), f32), sds(sq, bf16), sds((1, 1), f32),
        ],
        name="back_query",
        **params(8),
    )(q, v, phq, phk, amat, dnum, dden, pre, gates, id_rows, proj, *ties)


def call_back_key(k, v, phq, phk, dvs, dscts, dtail, gates, proj, ties, block, heads, d):
    rows, width = k.shape
    n = STEP_SEQS * block
    sq = (STEP_SEQS, heads, block, block)
    steps = rows // n

    def kernel(k_ref, v_ref, phq_ref, phk_ref, *refs):
        for i in range(steps):

            @pl.when(pl.program_id(0) == i)
            def _():
                back_key_kernel(
                    block, heads, d, k_ref, v_ref, phq_ref, phk_ref, refs[i], refs[steps + i],
                    *refs[2 * steps : 2 * steps + 3], refs[-1],
                )

    return pl.pallas_call(
        kernel,
        grid=(steps,),
        in_specs=[
            row_spec(n, width), row_spec(n, width), row_spec(n, phq.shape[1]),
            row_spec(n, phk.shape[1]),
        ]
        + [whole_spec((n, width))] * steps
        + [whole_spec(sq)] * steps
        + [
            lead_spec((STEP_SEQS,) + dtail.shape[1:]), row_spec(n, gates.shape[1]),
            whole_spec(proj.shape),
        ]
        + [pl.BlockSpec(memory_space=pl.ANY)] * len(ties),
        out_specs=row_spec(n, 2 * width),
        out_shape=sds((rows, 2 * width), bf16),
        name="back_key",
        **params(13),
    )(k, v, phq, phk, *dvs, *dscts, dtail, gates, proj, *ties)


TN = (((0,), (0,)), ((), ()))


def mm_tn(a, b):
    return lax.dot_general(a, b, TN, preferred_element_type=f32)


def pack_kernel(shard_rows, w_o_ref, w_in_ref, w_out_ref, vec_ref, *refs):
    out_ref = refs[-1]
    rows = w_out_ref[...]
    parts = [w_o_ref[...], w_in_ref[...]]
    parts += [rows[i : i + shard_rows] for i in range(0, rows.shape[0], shard_rows)]
    parts += [vec_ref[...]]
    at = 0
    for part in parts:
        out_ref[:, at : at + part.shape[1]] = part
        at += part.shape[1]


def call_pack(w_o, w_in, w_out, vec, ties):
    rows = w_o.shape[0]
    cols = (w_o.size + w_in.size + w_out.size + vec.size) // rows
    return pl.pallas_call(
        partial(pack_kernel, rows),
        in_specs=[pl.BlockSpec(memory_space=pltpu.VMEM)] * 4
        + [pl.BlockSpec(memory_space=pl.ANY)] * len(ties),
        out_shape=sds((rows, cols), bf16),
        name="pack",
    )(w_o, w_in, w_out, vec, *ties)


def part_store(core, refs, index, value):
    kept, sent, rows, cols = refs
    (kept if index % 2 == core else sent)[index // 2, rows, cols] = value


def by_core(kernel, core_ref):
    for core in range(2):
        pl.when(core_ref[0] == core)(partial(kernel, core))


def grads_kernel(
    shard_rows, core_ref, attn_ref, dao_ref, h1_ref, df_ref, act_ref, dfo_ref, sums_ref, sum_in_ref,
    tie_ref, keep_i, send_i, keep_o, send_o, done_ref,
):
    done_ref[...] = jnp.zeros_like(done_ref)
    by_core(
        partial(
            grads_parts, shard_rows, attn_ref, dao_ref, h1_ref, df_ref, act_ref, dfo_ref, sums_ref,
            sum_in_ref, keep_i, send_i, keep_o, send_o,
        ),
        core_ref,
    )


def grads_parts(
    shard_rows, attn_ref, dao_ref, h1_ref, df_ref, act_ref, dfo_ref, sums_ref, sum_in_ref,
    keep_i, send_i, keep_o, send_o, core,
):
    width = dao_ref.shape[1]
    ff = df_ref.shape[1]
    groups = ff // width
    tall = groups * shard_rows
    count = h1_ref.shape[1] // shard_rows
    every = slice(None)
    dfo = dfo_ref[...]
    chunk = act_ref.shape[1] // groups
    per = chunk // tall
    for c in range(groups):
        res = mm_tn(act_ref[:, c * chunk : (c + 1) * chunk], dfo).astype(bf16)
        for j in range(per):
            part_store(
                core, (keep_o, send_o, slice(0, tall), every), c * per + j,
                res[j * tall : (j + 1) * tall],
            )
    res = mm_tn(attn_ref[...], dao_ref[...]).astype(bf16)
    for j in range(count):
        part_store(
            core, (keep_o, send_o, slice(tall, tall + shard_rows), every), j,
            res[j * shard_rows : (j + 1) * shard_rows],
        )
    h1 = h1_ref[...]
    for g in range(groups):
        res = mm_tn(h1, df_ref[:, g * width : (g + 1) * width]).astype(bf16)
        for j in range(count):
            part_store(
                core, (keep_i, send_i, every, slice(g * width, (g + 1) * width)), j,
                res[j * shard_rows : (j + 1) * shard_rows],
            )
    step = pl.program_id(0)
    small = cut_out(sums_ref[...], shard_rows, 2 * count)
    large = cut_out(jnp.broadcast_to(sum_in_ref[...], (8, ff)), groups * shard_rows, 2 * count)
    row = lax.broadcasted_iota(jnp.int32, (8, 128), 0)
    for j in range(count):
        a = jnp.where(step == 0, small[j], small[j + count])
        b = jnp.where(step == 0, large[j], large[j + count])
        value = jnp.concatenate(
            [jnp.where(row == 6, b, a), jnp.zeros((shard_rows - 8, 128), f32)], axis=0
        )
        part_store(core, (keep_i, send_i, every, slice(ff, ff + 128)), j, value.astype(bf16))


def call_grads(core, attn, dao, h1, df, act, dfo, sums, sum_in, tie, shard_rows):
    rows, width = dao.shape
    ff = df.shape[1]
    steps = 2
    n_dev = width // shard_rows
    small = (n_dev // 2, shard_rows, ff + 128)
    tall = (n_dev // 2, shard_rows * (ff // width + 1), width)

    def cut(shape):
        return lead_spec((shape[0] // steps,) + shape[1:])

    return pl.pallas_call(
        partial(grads_kernel, shard_rows),
        grid=(steps,),
        in_specs=[
            pl.BlockSpec(memory_space=pltpu.SMEM),
            pl.BlockSpec((rows, width // steps), lambda i: (0, i)), whole_spec(dao.shape),
            pl.BlockSpec((rows, width // steps), lambda i: (0, i)), whole_spec(df.shape),
            pl.BlockSpec((rows, ff // steps), lambda i: (0, i)), whole_spec(dfo.shape),
            whole_spec(sums.shape), whole_spec(sum_in.shape),
            pl.BlockSpec(memory_space=pl.ANY),
        ],
        out_specs=[cut(small), cut(small), cut(tall), cut(tall), whole_spec((1, 1))],
        out_shape=[sds(small, bf16), sds(small, bf16), sds(tall, bf16), sds(tall, bf16)]
        + [sds((1, 1), f32)],
        name="grads",
        **params(10),
    )(core, attn, dao, h1, df, act, dfo, sums, sum_in, tie)


def first_grads_kernel(
    shard_rows, ties, core_ref, x_ref, dq_ref, dkv_ref, *refs
):
    by_core(partial(first_grads_parts, shard_rows, x_ref, dq_ref, dkv_ref, *refs[ties:]), core_ref)


def first_grads_parts(
    shard_rows, x_ref, dq_ref, dkv_ref, keep_a, send_a, keep_b, send_b, core
):
    width = dq_ref.shape[1]
    chunk = width // 2
    x = x_ref[...]
    step = pl.program_id(0)
    count = x_ref.shape[1] // shard_rows
    n_dev = 2 * count
    every = slice(None)
    sums = []
    for i in range(6):
        src, c0 = (dq_ref, i * chunk) if i < 2 else (dkv_ref, (i - 2) * chunk)
        b = src[:, c0 : c0 + chunk]
        sums.append(jnp.sum(b.astype(f32), axis=0, keepdims=True))
        res = mm_tn(x, b).astype(bf16)
        refs = (keep_a, send_a) if i < 3 else (keep_b, send_b)
        cols = slice((i % 3) * chunk, (i % 3 + 1) * chunk)
        for j in range(count):
            part_store(core, refs + (every, cols), j, res[j * shard_rows : (j + 1) * shard_rows])
    row = jnp.broadcast_to(jnp.concatenate(sums, axis=1), (8, 3 * width))
    pieces = cut_out(row, 3 * width // n_dev, n_dev)
    for j in range(count):
        value = jnp.concatenate(
            [
                jnp.where(step == 0, pieces[j], pieces[j + count]),
                jnp.zeros((shard_rows - 8, 128), f32),
            ],
            axis=0,
        )
        cols = slice(3 * chunk, 3 * chunk + 128)
        part_store(core, (keep_a, send_a, every, cols), j, value.astype(bf16))


def call_first_grads(core, x, dq, dkv, ties, shard_rows):
    rows, width = x.shape
    steps = 2
    half = 3 * width // 2
    n_dev = width // shard_rows
    shapes = [(n_dev // 2, shard_rows, half + 128)] * 2 + [(n_dev // 2, shard_rows, half)] * 2
    return pl.pallas_call(
        partial(first_grads_kernel, shard_rows, len(ties)),
        grid=(steps,),
        in_specs=[
            pl.BlockSpec(memory_space=pltpu.SMEM),
            pl.BlockSpec((rows, width // steps), lambda i: (0, i)), whole_spec(dq.shape),
            whole_spec(dkv.shape),
        ]
        + [pl.BlockSpec(memory_space=pl.ANY)] * len(ties),
        out_specs=[lead_spec((t[0] // steps,) + t[1:]) for t in shapes],
        out_shape=[sds(t, bf16) for t in shapes],
        name="first_grads",
        **params(6),
    )(core, x, dq, dkv, *ties)


def input_grad_kernel(dq_ref, dkv_ref, wa_ref, wb_ref, dr1_ref, *refs):
    out_ref, done_ref = refs[-2:]
    done_ref[...] = jnp.zeros_like(done_ref)
    width = dq_ref.shape[1]
    chunk = width // 2
    acc = dr1_ref[...]
    for i in range(6):
        src, c0 = (dq_ref, i * chunk) if i < 2 else (dkv_ref, (i - 2) * chunk)
        w_ref = wa_ref if i < 3 else wb_ref
        acc = acc + mm_nt(src[:, c0 : c0 + chunk], w_ref[:, (i % 3) * chunk : (i % 3 + 1) * chunk])
    out_ref[...] = acc.astype(bf16)


def call_input_grad(dq, dkv, wa, wb, dr1, ties, n):
    rows, width = dq.shape
    return pl.pallas_call(
        input_grad_kernel,
        grid=(rows // n,),
        in_specs=[
            row_spec(n, width), row_spec(n, 2 * width), whole_spec(wa.shape), whole_spec(wb.shape),
            row_spec(n, width),
        ]
        + [pl.BlockSpec(memory_space=pl.ANY)] * len(ties),
        out_specs=[row_spec(n, width), whole_spec((1, 1))],
        out_shape=[sds((rows, width), bf16), sds((1, 1), f32)],
        name="input_grad",
        **params(6),
    )(dq, dkv, wa, wb, dr1, *ties)


def body(
    inputs,
    seg_ids,
    cotangent,
    projection,
    w_qkv,
    b_qkv,
    w_o,
    b_o,
    ln1_gain,
    ln1_bias,
    w_in,
    b_in,
    w_out,
    b_out,
    ln2_gain,
    ln2_bias,
):
    micro, seqs_micro, block, width = inputs.shape
    heads, d, m = projection.shape
    n_seq = lax.axis_size("seq")
    n_dev = lax.axis_size("batch") * n_seq
    place = lax.axis_index("seq")
    seqs = micro * seqs_micro
    rows = seqs * block

    vectors = (b_qkv, b_o, ln1_gain, ln1_bias, b_in, b_out, ln2_gain, ln2_bias)
    sizes = [v.shape[0] for v in vectors]
    cuts = [sum(sizes[:i]) for i in range(len(sizes) + 1)]
    idents = seg_ids.reshape(seqs, block)
    shard_rows = w_qkv.shape[0]
    tiled = shard_rows % 8 == 0
    ids_b = idents[:, -1].astype(bf16)

    def as_rows(parts):
        t = jnp.stack([jnp.pad(t, (0, 128 - t.shape[0])) for t in parts])
        return jnp.pad(t, ((0, shard_rows - len(parts)), (0, 0)))

    order = (1, 2, 3, 5, 6, 7, 4)
    half = w_qkv.shape[1] // 2
    x = inputs.reshape(rows, width)
    dims = (block, heads, d)
    idents_f = idents.astype(f32)
    tail_gate = (idents_f == idents_f[:, -1:]).astype(f32)
    zero = jnp.zeros_like(projection[::2])
    proj = jnp.stack(
        [
            jnp.concatenate([projection[0::2], zero], axis=1),
            jnp.concatenate([zero, projection[1::2]], axis=1),
        ],
        axis=1,
    ).reshape(heads, 2 * d, m)
    f_cols = w_in.shape[1]
    if tiled:
        first = jnp.concatenate([w_qkv[:, :half], as_rows((b_qkv, ids_b))], axis=1)
        gather_a, gather_b = Gather(first, False), Gather(w_qkv[:, half:], True)
        ties = ()
        for _ in range(1):
            ties = (gather_a.step(), gather_b.step())
        packed = call_pack(w_o, w_in, w_out, as_rows([vectors[i] for i in order]), ties)
        gather_a.rest()
        gather_b.rest()
        weights = (lax.all_gather(packed, AXES, axis=0, tiled=True),)
        ids = jnp.concatenate([t[:, 1, half : half + seqs] for t in (gather_a.buf, gather_a.other)])
        device = lax.axis_index("batch") * n_seq + jnp.arange(n_seq)
        index = slot(gather_a.order, my_flat(), device) + ((device ^ my_flat()) & 1) * (n_dev // 2)
        chosen = (index[:, None] == jnp.arange(n_dev)[None, :]).astype(f32)
        last_all = jnp.sum(chosen[:, :, None] * ids.astype(f32)[None], axis=1)
        q, k, v, phq, phk, tails, w_a, w_b = call_features_tiled(
            x, gather_a, gather_b, proj, tail_gate.reshape(rows, 1), shard_rows, *dims
        )
    else:
        flat = jnp.concatenate(vectors + (ids_b,))
        flat = jnp.pad(flat, (0, -flat.shape[0] % 128)).reshape(-1, 128)
        used = flat.shape[0]
        flat = jnp.pad(flat, ((0, shard_rows - used), (0, 0)))
        w_a = gather_rows(jnp.concatenate([w_qkv[:, :half], flat], axis=1), False)
        w_b = gather_rows(w_qkv[:, half:], True)
        packed = w_a[:, half:].reshape(n_dev, shard_rows, 128)[:, :used].reshape(n_dev, -1)
        whole = [
            packed[:, cuts[i] : cuts[i] + sizes[i]].reshape(1, -1).astype(f32)
            for i in range(len(sizes))
        ]
        ids_all = packed[:, cuts[-1] : cuts[-1] + seqs].reshape(-1, n_seq, seqs).astype(f32)
        last_all = lax.dynamic_index_in_dim(ids_all, lax.axis_index("batch"), 0, False)
        rows_of = [whole[i] for i in order[:6]]
        weights = (
            gather_rows(w_o, False), gather_rows(w_in, True), gather_rows(w_out, False),
            jnp.concatenate(rows_of + rows_of[:2]), jnp.concatenate([whole[4]] * 8),
        )
        q, k, v, phq, phk, tails = call_features(
            x, w_a, w_b, whole[0], proj, tail_gate.reshape(rows, 1), *dims
        )

    pre_all = jnp.concatenate([-jnp.ones_like(last_all[:1]), last_all[:-1]], axis=0)
    pre_ident = lax.dynamic_index_in_dim(pre_all, place, 0, False)
    gates = jnp.stack(
        [
            idents_f,
            tail_gate,
            (idents_f == pre_ident[:, None]).astype(f32),
        ],
        axis=-1,
    ).reshape(rows, 3)
    gates = jnp.pad(gates, ((0, 0), (0, 5)))
    id_rows = idents_f[:, None, :]
    amat, nd, done = call_local(phq, phk, v, gates, id_rows, *dims)
    pre = exclusive_scan(tails, last_all, False, lambda sent: [done])
    (y, dr1, dnum, dden, dpre, attn, dao, h1, act, dfo, df, sums, sum_in) = call_middle(
        x, cotangent.reshape(rows, width), phq, nd, pre, gates, weights, tiled,
        shard_rows, f_cols, *dims,
    )
    core = (place & 1).astype(jnp.int32).reshape(1)

    def grad(a, b):
        return mm_tn(a, b).astype(bf16)

    halves, scatters = [], []

    def run_beside(sent):
        zeros = []
        if tiled:
            keep_i, send_i, keep_o, send_o, done = call_grads(
                core, attn, dao, h1, df, act, dfo, sums, sum_in, sent, shard_rows
            )
            zeros = [0.0]
            wide, tall = (keep_i, True, send_i), (keep_o, False, send_o)
        else:
            pieces = [t.reshape(n_dev, -1) for t in [sums[i] for i in range(6)] + [sum_in[0]]]
            vec = jnp.concatenate(pieces, axis=1)
            vec = jnp.pad(vec, ((0, 0), (0, -vec.shape[1] % 128))).reshape(n_dev, -1, 128)
            vec = jnp.pad(vec, ((0, 0), (0, shard_rows - vec.shape[1]), (0, 0))).astype(bf16)
            wide = jnp.concatenate([grad(h1, df).reshape(n_dev, shard_rows, -1), vec], axis=2)
            tall = [grad(act, dfo).reshape(n_dev, -1, width), grad(attn, dao).reshape(n_dev, -1, width)]
            wide, tall = (wide, True), (jnp.concatenate(tall, axis=1), False)
        scatters.append(Scatter(*wide))
        scatters.append(Scatter(*tall))
        for i in range(seqs // STEP_SEQS):
            halves.append(
                call_back_query(
                    i, q, v, phq, phk, amat, dnum, dden, pre, gates, id_rows, proj,
                    (), *dims
                )
            )
        return zeros + [t[3] for t in halves]

    def start_scatters(value):
        first = [t.step() for t in scatters]
        value, *first = lax.optimization_barrier((value, *first))
        for t, buf in zip(scatters, first):
            t.buf = buf
        return value

    back = exclusive_scan(dpre, pre_all, True, run_beside, start_scatters)
    scatter_i, scatter_o = scatters
    dqs, dvs, dscts, dones = zip(*halves)
    dq = jnp.concatenate(dqs)
    ties = ()
    dkv = call_back_key(k, v, phq, phk, dvs, dscts, back, gates, proj, ties, *dims)
    ties = ()
    if tiled:
        keep_a, send_a, keep_b, send_b = call_first_grads(core, x, dq, dkv, ties, shard_rows)
        scatter_a = Scatter(keep_a, False, send_a)
        scatter_b = Scatter(keep_b, True, send_b)
    else:
        dqkv = jnp.concatenate([dq, dkv], axis=1)
        gw = grad(x, dqkv).reshape(n_dev, shard_rows, -1)
        vec = jnp.sum(dqkv, axis=0, dtype=f32).reshape(n_dev, 1, -1)
        vec = jnp.pad(vec, ((0, 0), (0, shard_rows - 1), (0, 128 - sizes[0]))).astype(bf16)
        scatter_a = Scatter(jnp.concatenate([gw[:, :, :half], vec], axis=2), False)
        scatter_b = Scatter(gw[:, :, half:], True)
    ties = (scatter_a.step(), scatter_b.step()) + (scatter_i.step(), scatter_o.step())
    dx, done = call_input_grad(dq, dkv, w_a, w_b, dr1, ties, STEP_SEQS * block)
    scatter_a.step(done)
    scatter_b.step()
    part_a = scatter_a.rest()
    part_b = scatter_b.rest()
    part_i = scatter_i.rest()
    part_o = scatter_o.rest()
    g_w_out, g_w_o = part_o[: w_out.shape[0]], part_o[w_out.shape[0] :]
    g_w_in = part_i[:, :f_cols]
    lengths = [sizes[i] for i in order]
    if tiled:
        vec_grads = [part_i[i, f_cols : f_cols + n] for i, n in enumerate(lengths)]
    else:
        vec = part_i[:, f_cols:].reshape(-1)
        starts = [sum(lengths[:i]) for i in range(len(lengths))]
        vec_grads = [vec[at : at + n] for at, n in zip(starts, lengths)]
    (g_b_o, g_gain_one, g_shift_one, g_b_out, g_gain_two, g_shift_two, g_b_in) = vec_grads
    g_w_qkv = jnp.concatenate([part_a[:, :half], part_b], axis=1)
    g_b_qkv = part_a[0, half : half + sizes[0]]
    return (
        y.reshape(inputs.shape),
        dx.reshape(inputs.shape),
        g_w_qkv,
        g_b_qkv,
        g_w_o,
        g_b_o,
        g_gain_one,
        g_shift_one,
        g_w_in,
        g_b_in,
        g_w_out,
        g_b_out,
        g_gain_two,
        g_shift_two,
    )


def solution(mesh):
    rows = P(AXES, None)
    vec = P(AXES)
    tok = P(None, "batch", "seq", None)
    in_specs = (
        tok,
        P(None, "batch", "seq"),
        tok,
        P(),
        rows,
        vec,
        rows,
        vec,
        vec,
        vec,
        rows,
        vec,
        rows,
        vec,
        vec,
        vec,
    )
    out_specs = (tok, tok, rows, vec, rows, vec, vec, vec, rows, vec, rows, vec, vec, vec)
    return jax.shard_map(body, mesh=mesh, in_specs=in_specs, out_specs=out_specs, check_vma=False)
```

```python
import math
from functools import partial

import jax
import jax.numpy as jnp
from jax import lax
from jax.experimental import pallas as pl
from jax.experimental.pallas import tpu as pltpu
from jax.sharding import PartitionSpec as P

norm_eps = 1e-05
bf16 = jnp.bfloat16
f32 = jnp.float32
AXES = ("batch", "seq")


def flat_xor(value, mask):
    n = lax.axis_size("batch") * lax.axis_size("seq")
    return lax.ppermute(value, AXES, [(i, i ^ mask) for i in range(n)])


def log2(n):
    return n.bit_length() - 1


def gather_order(nb, ns, swap):
    seq_bits = list(range(log2(ns)))
    batch_bits = [log2(ns) + b for b in range(log2(nb))]
    low, mid, high = seq_bits[0], seq_bits[1], seq_bits[2:]
    cross = [mid] + batch_bits if not swap else batch_bits + [mid]
    return high[::-1] + cross + [low]


def my_flat():
    return lax.axis_index("batch") * lax.axis_size("seq") + lax.axis_index("seq")


def gather_rows(shard, swap):
    nb, ns = lax.axis_size("batch"), lax.axis_size("seq")
    nbits = log2(nb * ns)
    me = my_flat()
    shape = shard.shape
    buf = shard.reshape((1,) * nbits + shape)
    for bit in gather_order(nb, ns, swap):
        axis = nbits - 1 - bit
        other = flat_xor(buf, 1 << bit)
        mine = (me >> bit) & 1
        buf = jnp.where(
            mine == 1,
            jnp.concatenate([other, buf], axis),
            jnp.concatenate([buf, other], axis),
        )
    return buf.reshape((nb * ns * shape[0],) + shape[1:])


class Gather:
    def __init__(self, shard, swap):
        self.bits = gather_order(lax.axis_size("batch"), lax.axis_size("seq"), swap)
        self.order = tuple(self.bits[:-1])
        self.buf = shard.reshape((1,) + shard.shape[-2:])

    def step(self):
        other = flat_xor(self.buf, 1 << self.bits.pop(0))
        if self.bits:
            self.buf = jnp.concatenate([self.buf, other], axis=0)
        else:
            self.other = other
        return self.buf

    def rest(self):
        while self.bits:
            self.step()
        return self.buf, self.other


def slot(order, me, device):
    far = me ^ device
    at = (far >> order[0]) & 1
    for j in range(1, len(order)):
        at = at + (((far >> order[j]) & 1) << j)
    return at


class Scatter:
    def __init__(self, buf, swap, send=None):
        nbits = log2(lax.axis_size("batch") * lax.axis_size("seq"))
        self.bits = gather_order(lax.axis_size("batch"), lax.axis_size("seq"), swap)[::-1]
        self.send = send
        self.buf = buf if send is not None else buf.reshape((2,) * nbits + buf.shape[1:])
        self.tail = buf.shape[1:]
        self.nbits = nbits

    def step(self, beside=0.0):
        bit = self.bits.pop(0)
        axis = self.nbits - 1 - bit
        mine = (my_flat() >> bit) & 1
        if self.send is None:
            keep = lax.dynamic_index_in_dim(self.buf, mine, axis, True)
            send = lax.dynamic_index_in_dim(self.buf, 1 - mine, axis, True)
        else:
            keep, send, self.send = self.buf, self.send, None
        got = flat_xor(send, 1 << bit)
        buf = keep.astype(f32) + got.astype(f32) + beside
        if self.bits:
            buf = buf.astype(bf16)
        else:
            buf = buf.reshape(self.tail)
        if keep.ndim == 3 and self.bits:
            buf = buf.reshape((2,) * (self.nbits - 1) + (1,) + self.tail)
        self.buf = buf
        return buf

    def rest(self):
        while self.bits:
            self.step()
        return self.buf


def seq_perm(value, pairs):
    return lax.ppermute(value, "seq", pairs)


def exclusive_scan(tails, ids, rev, beside, final=lambda value: value):
    n = lax.axis_size("seq")
    place = lax.axis_index("seq")
    if rev:
        ids = ids[::-1]
    p = n - 1 - place if rev else place

    def at(q):
        return n - 1 - q if rev else q

    def move(value, pairs):
        return seq_perm(value, [(at(a), at(b)) for a, b in pairs])

    def gated(g, value):
        return g * value.astype(f32)

    c = p & 1
    x = (p >> 1) & 1
    base = p - (p & 3)
    pair = p - c
    seqs = tails.shape[0]
    rest = tails.shape[2:]
    wanted = [(pair, pair + 1), (base + 1, base + 3), (base - 1, base + 1), (pair - 1, pair)]
    step = 1
    while step * 4 < n:
        wanted += [(base + 3 - 4 * step, base - 1), (base + 3 - 4 * step, base + 3)]
        step *= 2
    where = jnp.stack([jnp.clip(t, 0, n - 1) for pair_of in wanted for t in pair_of])
    chosen = (where[:, None] == jnp.arange(n)[None, :]).astype(f32)
    keys = jnp.sum(chosen[:, :, None] * ids[None], axis=1)
    gates = (keys[0::2] == keys[1::2]).astype(f32)
    gates = jnp.broadcast_to(gates[:, :, None, None], gates.shape + (1, rest[-1]))
    gate_core, gate_pair, gate_plane, gate_entry = (gates[i] for i in range(4))
    parts = tails.reshape((seqs, 2, 2) + rest)

    def pick(a, i, axis):
        return lax.dynamic_index_in_dim(a, i, axis, False)

    core = [(i, i ^ 1) for i in range(n)]
    across = [(i, i ^ 2) for i in range(n)]
    own = pick(parts, c, 2)
    other = move(pick(parts, 1 - c, 2), core)
    first = jnp.where(c == 0, own, other)
    second = jnp.where(c == 0, other, own)
    pair_sum = second.astype(f32) + gated(gate_core[:, None], first)
    pair_mine = pick(pair_sum, x, 1)
    sent = pick(pair_sum, 1 - x, 1).astype(bf16)
    beside = beside(sent)
    pair_other = move(sent, across).astype(f32)
    low = jnp.where(x == 0, pair_mine, pair_other)
    high = jnp.where(x == 0, pair_other, pair_mine)
    total = high + gated(gate_pair, low)
    before = jnp.zeros_like(total)
    step = 1
    while step * 4 < n:
        total = total + (beside.pop(0) if beside else 0.0)
        got = move(
            total.astype(bf16), [(i, i + 4 * step) for i in range(n - 4 * step)]
        )
        at_step = 4 + 2 * log2(step)
        before = before + gated(gates[at_step], got)
        total = total + gated(gates[at_step + 1], got)
        step *= 2
    before_high = low + gated(gate_plane, before)
    mine = jnp.where(x == 0, before, before_high)
    theirs = jnp.where(x == 0, before_high, before) + sum(beside, jnp.zeros((1, 1), f32))
    got = move(theirs.astype(bf16), across)
    mine_b = mine.astype(bf16)
    entry = jnp.where(x == 0, jnp.stack([mine_b, got], 1), jnp.stack([got, mine_b], 1))
    after = first.astype(f32) + gated(gate_entry[:, None], entry)
    after_b = after.astype(bf16)
    mine = jnp.where(c == 0, entry, after_b)
    theirs = final(jnp.where(c == 0, after_b, entry))
    got = move(theirs, core)
    result = jnp.where(c == 0, jnp.stack([mine, got], 2), jnp.stack([got, mine], 2))
    return result.reshape(tails.shape)


NT = (((1,), (1,)), ((), ()))
VMEM_LIMIT = 56 * 1024 * 1024


def mm(a, b):
    return jnp.dot(a, b, preferred_element_type=f32)


def mm_nt(a, b):
    return lax.dot_general(a, b, NT, preferred_element_type=f32)


def lane_low(shape, half):
    return lax.broadcasted_iota(jnp.int32, shape, 1) < half


def half_sums(value, low):
    first = jnp.sum(jnp.where(low, value, 0.0), axis=1, keepdims=True)
    second = jnp.sum(jnp.where(low, 0.0, value), axis=1, keepdims=True)
    return first, second


def state_rows(ref, s, h, heads, d):
    per = heads // 4
    return ref[s, h // per, pl.ds((h % per) * d, d), :]


def total_rows(ref, s, heads, d):
    per = heads // 4
    out = []
    for q in range(4):
        rows = ref[s, q, pl.ds(per * d, 16), :].astype(f32)
        out += [rows[j : j + 1] for j in range(per)]
    return out


def pair_rows(first, second, core):
    return jnp.concatenate([first, second] if core == 0 else [second, first], axis=0)


def lay_out(pieces, width, out_ref):
    tiles = out_ref.shape[1] // 128
    lane = lax.broadcasted_iota(jnp.int32, (8, 128), 1)
    acc = [jnp.zeros((8, 128), f32)] * tiles
    for j, piece in enumerate(pieces):
        t, s = divmod(j * width, 128)
        turned = pltpu.roll(jnp.where(lane < width, piece, 0.0), s, 1) if s else jnp.where(lane < width, piece, 0.0)
        if s + width <= 128:
            acc[t] = acc[t] + turned
        else:
            acc[t] = acc[t] + jnp.where(lane >= s, turned, 0.0)
            acc[t + 1] = acc[t + 1] + jnp.where(lane < s, turned, 0.0)
    for t in range(tiles):
        out_ref[:, t * 128 : (t + 1) * 128] = acc[t]


def cut_out(values, width, count):
    tiles = values.shape[1] // 128
    lane = lax.broadcasted_iota(jnp.int32, (8, 128), 1)
    out = []
    for j in range(count):
        t, s = divmod(j * width, 128)
        piece = values[:, t * 128 : (t + 1) * 128]
        if s + width > 128:
            piece = jnp.where(lane >= s, piece, values[:, (t + 1) * 128 : (t + 2) * 128])
        out.append(pltpu.roll(piece, 128 - s, 1) if s else piece)
    return out


def fill_first(orders, shard_rows, piece, me_ref, wa_ref, wb_ref, bias, own_a, oth_a, own_b, oth_b, core):
    me = me_ref[0]
    unit = 2 * shard_rows
    count = wa_ref.shape[0] // unit

    def one(j, carry):
        rows = pl.ds(pl.multiple_of(j * unit, 16), unit)
        p = slot(orders[0], me, 2 * j)
        wa_ref[rows, :] = pair_rows(own_a[p], oth_a[p], core)
        p = slot(orders[1], me, 2 * j)
        wb_ref[rows, :] = pair_rows(own_b[p], oth_b[p], core)
        return carry

    lax.fori_loop(0, count, one, 0)
    first = wa_ref.shape[1] - 128
    pieces = []
    for j in range(count):
        two = wa_ref[j * unit : (j + 1) * unit, first:].astype(f32)
        pieces += [two[i * shard_rows : i * shard_rows + 8] for i in range(2)]
    lay_out(pieces, piece, bias)


def features_tiled_kernel(
    block, heads, d, orders, shard_rows, me_ref, x_ref, own_a, oth_a, own_b, oth_b, proj_ref, tg_ref,
    k_ref, v_ref, phk_ref, tail_ref, wa_ref, wb_ref, bias, z_scr,
):
    @pl.when(pl.program_id(0) == 0)
    def _():
        piece = bias.shape[1] // (wa_ref.shape[0] // shard_rows)
        for core in range(2):
            pl.when(me_ref[0] % 2 == core)(
                partial(
                    fill_first, orders, shard_rows, piece, me_ref, wa_ref, wb_ref, bias,
                    own_a, oth_a, own_b, oth_b, core,
                )
            )

    parts = ((1, (k_ref, phk_ref)), (2, (v_ref, None)))
    project_parts(block, heads, d, parts, x_ref, wa_ref, wb_ref, bias, proj_ref)
    tail_parts(block, heads, d, tg_ref, v_ref, phk_ref, tail_ref, z_scr)


def features_kernel(
    block, heads, d, x_ref, wa_ref, wb_ref, b_ref, proj_ref, tg_ref,
    q_ref, k_ref, v_ref, phq_ref, phk_ref, tail_ref, z_scr,
):
    parts = ((1, (k_ref, phk_ref)), (2, (v_ref, None)), (0, (q_ref, phq_ref)))
    project_parts(block, heads, d, parts, x_ref, wa_ref, wb_ref, b_ref, proj_ref)
    tail_parts(block, heads, d, tg_ref, v_ref, phk_ref, tail_ref, z_scr)


def query_kernel(block, heads, d, x_ref, wa_ref, b_ref, proj_ref, q_ref, phq_ref):
    project_parts(block, heads, d, ((0, (q_ref, phq_ref)),), x_ref, wa_ref, None, b_ref, proj_ref)


def project_parts(block, heads, d, parts, x_ref, wa_ref, wb_ref, b_ref, proj_ref):
    width = heads * d
    m = proj_ref.shape[2]
    pair = 2 * d
    scale = d ** (-0.25)
    root = m ** (-0.5)
    x = x_ref[...]
    rows = x.shape[0]
    low = lane_low((rows, pair), d)
    chunk = width // 2
    for t, (z_ref, ph_ref) in parts:
        for i in range(2):
            col = t * width + i * chunk
            w = wa_ref[:, col : col + chunk] if col < 3 * chunk else wb_ref[:, col - 3 * chunk : col - 2 * chunk]
            z = mm(x, w) + b_ref[0:1, col : col + chunk]
            z = (z * scale if ph_ref is not None else z).astype(bf16)
            z_ref[:, i * chunk : (i + 1) * chunk] = z
            if ph_ref is None:
                continue
            for p in range(chunk // pair):
                zp = z[:, p * pair : (p + 1) * pair]
                zf = zp.astype(f32)
                sums = half_sums(zf * zf, low)
                for e in range(2):
                    h = 2 * (i * (chunk // pair) + p) + e
                    u = mm(zp, proj_ref[h])
                    ph_ref[:, h * m : (h + 1) * m] = (jnp.exp(u - 0.5 * sums[e]) * root).astype(bf16)


def tail_parts(block, heads, d, tg_ref, v_ref, phk_ref, tail_ref, z_scr):
    m = phk_ref.shape[1] // heads
    pair = 2 * d
    per = heads // 4
    for s in range(v_ref.shape[0] // block):
        r = slice(s * block, (s + 1) * block)
        tg = tg_ref[r, :].astype(bf16)
        for p in range(heads // 2):
            v_t = v_ref[r, p * pair : (p + 1) * pair].T
            for e in range(2):
                h = 2 * p + e
                kt = phk_ref[r, h * m : (h + 1) * m] * tg
                lhs = jnp.concatenate([v_t[e * d : (e + 1) * d], jnp.ones((16, block), bf16)], 0)
                res = mm(lhs, kt)
                tail_ref[s, h // per, pl.ds((h % per) * d, d), :] = res[:d].astype(bf16)
                z_scr[h % per : h % per + 1, :] = res[d : d + 1]
                if h % per == per - 1:
                    tail_ref[s, h // per, pl.ds(per * d, 16), :] = z_scr[...].astype(bf16)


def local_kernel(
    block, heads, d, phq_ref, phk_ref, v_ref, col_ref, row_ref, amat_ref, nd_ref, done_ref
):
    done_ref[...] = jnp.zeros_like(done_ref)
    m = phq_ref.shape[1] // heads
    pair = 2 * d
    low = lane_low((block, pair), d)
    t_ix = lax.broadcasted_iota(jnp.int32, (block, block), 0)
    j_ix = lax.broadcasted_iota(jnp.int32, (block, block), 1)
    causal = t_ix >= j_ix
    for s in range(v_ref.shape[0] // block):
        r = slice(s * block, (s + 1) * block)
        mask = jnp.logical_and(causal, col_ref[r, 0:1] == row_ref[s])
        for p in range(heads // 2):
            v_pair = v_ref[r, p * pair : (p + 1) * pair]
            for e in range(2):
                h = 2 * p + e
                sc = mm_nt(phq_ref[r, h * m : (h + 1) * m], phk_ref[r, h * m : (h + 1) * m])
                am = jnp.where(mask, sc, 0.0).astype(bf16)
                amat_ref[s, h] = am
                v_one = jnp.where(low if e == 0 else ~low, v_pair, jnp.ones_like(v_pair))
                nd_ref[r, h * pair : (h + 1) * pair] = mm(am, v_one)


def layer_norm(row_vals, gain, shift):
    inv = 1.0 / row_vals.shape[1]
    centred = row_vals - jnp.sum(row_vals, axis=1, keepdims=True) * inv
    rs = lax.rsqrt(jnp.sum(centred * centred, axis=1, keepdims=True) * inv + norm_eps)
    normed = centred * rs
    return normed * gain + shift, normed, rs


def layer_norm_back(dn, normed, rs):
    inv = 1.0 / dn.shape[1]
    mean = jnp.sum(dn, axis=1, keepdims=True) * inv
    proj = jnp.sum(dn * normed, axis=1, keepdims=True) * inv
    return rs * (dn - mean - normed * proj)


def group_rows(shard_rows):
    return math.lcm(shard_rows, 16) // shard_rows


def natural_rows(stage, out_ref, shard_rows, width):
    groups = stage.shape[1] // width
    per = group_rows(shard_rows)
    unit = per * shard_rows

    def one(i, carry):
        cols = [
            stage[pl.ds(pl.multiple_of(i * unit, 16), unit), g * width : (g + 1) * width]
            for g in range(groups)
        ]
        pieces = [c[j * shard_rows : (j + 1) * shard_rows] for j in range(per) for c in cols]
        out_ref[pl.ds(pl.multiple_of(i * unit * groups, 16), unit * groups), :] = jnp.concatenate(
            pieces, axis=0
        )
        return carry

    lax.fori_loop(0, stage.shape[0] // unit, one, 0)


def fill_rest(shard_rows, w_out_ref, vec_scr, b_in_scr, stage, vec_stage):
    width = w_out_ref.shape[1]
    natural_rows(stage, w_out_ref, shard_rows, width)
    unit = 2 * shard_rows
    pieces = []
    for j in range(vec_stage.shape[0] // unit):
        two = vec_stage[j * unit : (j + 1) * unit, :].astype(f32)
        pieces += [two[i * shard_rows : i * shard_rows + 8] for i in range(2)]
    lay_out(pieces, shard_rows, vec_scr)
    lay_out(pieces, w_out_ref.shape[0] // len(pieces), b_in_scr)


def middle_kernel(
    block, heads, d, ff_chunk,
    tiled, shard_rows, x_ref, cot_ref, phq_ref, nd_ref, pre_ref, gate_ref,
    *refs
):
    ins = refs[: 1 if tiled else 5]
    middle_parts(
        block, heads, d, ff_chunk, tiled, shard_rows, x_ref, cot_ref, phq_ref, nd_ref,
        pre_ref, gate_ref, ins, *refs[len(ins) :],
    )


def middle_parts(
    block, heads, d, ff_chunk, tiled, shard_rows, x_ref, cot_ref, phq_ref, nd_ref, pre_ref,
    gate_ref, ins,
    y_ref, dr1_ref, dnum_ref, dden_ref, dpre_ref, attn_ref, dao_ref, h1_ref, act_ref, dfo_ref,
    df_ref, sums_ref, sum_in_ref,
    attf, rden, dgel, z_scr, w_o_ref, w_in_ref, w_out_ref, vec_ref, b_in_ref, sems, *stages
):
    step = pl.program_id(0)
    m = phq_ref.shape[1] // heads
    width = heads * d
    ff = w_in_ref.shape[1]

    def copies():
        if tiled:
            cuts = [0, width, width + ff, width + 2 * ff, width + 2 * ff + 128]
            sources = [ins[0].at[:, i:j] for i, j in zip(cuts, cuts[1:])]
            places = (w_o_ref, w_in_ref) + tuple(stages)
        else:
            sources, places = ins, (w_o_ref, w_in_ref, w_out_ref, vec_ref, b_in_ref)
        return [
            pltpu.make_async_copy(src, dst, sems.at[i])
            for i, (src, dst) in enumerate(zip(sources, places))
        ]

    @pl.when(step == 0)
    def _():
        for c in copies():
            c.start()

    pair = 2 * d
    low = lane_low((block, pair), d)
    rows = x_ref.shape[0]
    seqs = rows // block
    ones = jnp.ones((d, 1), f32)
    for s in range(seqs):
        r = slice(s * block, (s + 1) * block)
        g = gate_ref[r, 2:3]
        zs = total_rows(pre_ref, s, heads, d)
        for p in range(heads // 2):
            tot = []
            for e in range(2):
                h = 2 * p + e
                st = state_rows(pre_ref, s, h, heads, d)
                zb = (ones * zs[h]).astype(bf16)
                rhs = jnp.concatenate([st, zb] if e == 0 else [zb, st], 0)
                tot.append(
                    nd_ref[r, h * pair : (h + 1) * pair]
                    + g * mm_nt(phq_ref[r, h * m : (h + 1) * m], rhs)
                )
            num = jnp.where(low, tot[0], tot[1])
            den = pltpu.roll(jnp.where(low, tot[1], tot[0]), d, 1)
            rd = 1.0 / den
            c = slice(p * pair, (p + 1) * pair)
            att = num * rd
            attf[r, c] = att
            rden[r, c] = rd
            attn_ref[r, c] = att.astype(bf16)

    @pl.when(step == 0)
    def _():
        for c in copies():
            c.wait()
        if tiled:
            fill_rest(shard_rows, w_out_ref, vec_ref, b_in_ref, *stages)

    b_o, gain1, shift1, b_out, gain2, shift2 = (vec_ref[i : i + 1, :] for i in range(6))
    r1 = x_ref[...].astype(f32) + mm(attn_ref[...], w_o_ref[...]) + b_o
    h1, n1, rs1 = layer_norm(r1, gain1, shift1)
    h1b = h1.astype(bf16)
    h1_ref[...] = h1b
    fo = None
    for c0 in range(0, ff, ff_chunk):
        c = slice(c0, c0 + ff_chunk)
        f = mm(h1b, w_in_ref[:, c]) + b_in_ref[6:7, c]
        phi = 0.5 + 0.5 * lax.erf(f * (0.5**0.5))
        act = (f * phi).astype(bf16)
        act_ref[:, c] = act
        dgel[:, c] = phi + f * (jnp.exp(-0.5 * f * f) * (1.0 / (2.0 * math.pi) ** 0.5))
        part = mm(act, w_out_ref[c, :])
        fo = part if fo is None else fo + part
    y, n2, rs2 = layer_norm(h1 + fo + b_out, gain2, shift2)
    y_ref[...] = y.astype(bf16)
    dy = cot_ref[...].astype(f32)

    def add_sum(i, value):
        row = jnp.sum(value, axis=0, keepdims=True)

        @pl.when(step == 0)
        def _():
            sums_ref[i : i + 1, :] = row

        @pl.when(step > 0)
        def _():
            sums_ref[i : i + 1, :] += row

    add_sum(4, dy * n2)
    add_sum(5, dy)
    dr2 = layer_norm_back(dy * gain2, n2, rs2)
    dfo = dr2.astype(bf16)
    dfo_ref[...] = dfo
    add_sum(3, dfo.astype(f32))
    dh1 = dr2
    for c0 in range(0, ff, ff_chunk):
        c = slice(c0, c0 + ff_chunk)
        df = (mm_nt(dfo, w_out_ref[c, :]) * dgel[:, c]).astype(bf16)
        df_ref[:, c] = df
        row = jnp.sum(df.astype(f32), axis=0, keepdims=True)

        @pl.when(step == 0)
        def _():
            sum_in_ref[:, c] = row

        @pl.when(step > 0)
        def _():
            sum_in_ref[:, c] += row

        dh1 = dh1 + mm_nt(df, w_in_ref[:, c])
    add_sum(1, dh1 * n1)
    add_sum(2, dh1)
    dr1 = layer_norm_back(dh1 * gain1, n1, rs1)
    dr1_ref[...] = dr1
    dao = dr1.astype(bf16)
    dao_ref[...] = dao
    add_sum(0, dao.astype(f32))
    dattn = mm_nt(dao, w_o_ref[...])
    dnum_ref[...] = (dattn * rden[...]).astype(bf16)
    prod = dattn * attf[...]
    lane = lax.broadcasted_iota(jnp.int32, (rows, 128), 1)
    low_rows = lane_low((rows, pair), d)
    dden = jnp.zeros((rows, 128), f32)
    for p in range(heads // 2):
        c = slice(p * pair, (p + 1) * pair)
        sums = half_sums(prod[:, c], low_rows)
        for e in range(2):
            col = -sums[e] * rden[:, p * pair + e * d : p * pair + e * d + 1]
            dden = jnp.where(lane == 2 * p + e, col, dden)
    dden = dden.astype(bf16).astype(f32)
    dden_ref[...] = dden
    per = heads // 4
    for s in range(seqs):
        r = slice(s * block, (s + 1) * block)
        g = gate_ref[r, 2:3]
        ddt = (dden[r] * g).T[:16].astype(bf16)
        for p in range(heads // 2):
            gdt = (dnum_ref[r, p * pair : (p + 1) * pair] * g.astype(bf16)).T
            for e in range(2):
                h = 2 * p + e
                lhs = jnp.concatenate([gdt[e * d : (e + 1) * d], ddt], 0)
                res = mm(lhs, phq_ref[r, h * m : (h + 1) * m])
                dpre_ref[s, h // per, pl.ds((h % per) * d, d), :] = res[:d].astype(bf16)
                z_scr[h % per : h % per + 1, :] = res[d + h : d + h + 1]
                if h % per == per - 1:
                    dpre_ref[s, h // per, pl.ds(per * d, 16), :] = z_scr[...].astype(bf16)


def back_query_kernel(
    block, heads, d,
    q_ref, v_ref, phq_ref, phk_ref, amat_ref, dnum_ref, dden_ref, pre_ref, gate_ref, row_ref,
    proj_ref,
    dq_ref, dv_ref, dsct_ref, done_ref,
):
    done_ref[...] = jnp.zeros_like(done_ref)
    m = phq_ref.shape[1] // heads
    pair = 2 * d
    scale = d ** (-0.25)
    low = lane_low((block, pair), d)
    t_ix = lax.broadcasted_iota(jnp.int32, (block, block), 0)
    j_ix = lax.broadcasted_iota(jnp.int32, (block, block), 1)
    causal = t_ix >= j_ix
    for s in range(q_ref.shape[0] // block):
        r = slice(s * block, (s + 1) * block)
        g = gate_ref[r, 2:3]
        gb = g.astype(bf16)
        mask = jnp.logical_and(causal, gate_ref[r, 0:1] == row_ref[s])
        zs = total_rows(pre_ref, s, heads, d)
        for p in range(heads // 2):
            c = slice(p * pair, (p + 1) * pair)
            dn = dnum_ref[r, c]
            v_pair = v_ref[r, c]
            qp = q_ref[r, c].astype(f32)
            st = jnp.concatenate(
                [state_rows(pre_ref, s, 2 * p, heads, d), state_rows(pre_ref, s, 2 * p + 1, heads, d)], 0
            )
            dv = None
            dq = None
            for e in range(2):
                h = 2 * p + e
                mine = low if e == 0 else ~low
                hm = slice(h * m, (h + 1) * m)
                dnm = jnp.where(mine, dn, jnp.zeros_like(dn))
                dd = dden_ref[r, h : h + 1]
                dsc = jnp.where(mask, mm_nt(dnm, v_pair) + dd, 0.0)
                dsct_ref[s, h] = dsc.T.astype(bf16)
                dph = mm(
                    jnp.concatenate([dsc.astype(bf16), dnm * gb], 1),
                    jnp.concatenate([phk_ref[r, hm], st], 0),
                ) + (g * dd) * zs[h]
                t = dph * phq_ref[r, hm].astype(f32)
                part = mm_nt(t.astype(bf16), proj_ref[h]) - jnp.where(
                    mine, jnp.sum(t, axis=1, keepdims=True) * qp, 0.0
                )
                dq = part if dq is None else dq + part
                part = mm(amat_ref[s, h].T, dnm)
                dv = part if dv is None else dv + part
            dq_ref[r, c] = (dq * scale).astype(bf16)
            dv_ref[r, c] = dv


def back_key_kernel(
    block, heads, d,
    k_ref, v_ref, phq_ref, phk_ref, dv_ref, dsct_ref, dtail_ref, gate_ref, proj_ref,
    dkv_ref,
):
    m = phq_ref.shape[1] // heads
    pair = 2 * d
    width = heads * d
    scale = d ** (-0.25)
    low = lane_low((block, pair), d)
    for s in range(k_ref.shape[0] // block):
        r = slice(s * block, (s + 1) * block)
        tg = gate_ref[r, 1:2]
        tgb = tg.astype(bf16)
        zs = total_rows(dtail_ref, s, heads, d)
        for p in range(heads // 2):
            c = slice(p * pair, (p + 1) * pair)
            v_pair = v_ref[r, c]
            kp = k_ref[r, c].astype(f32)
            ds = jnp.concatenate(
                [
                    state_rows(dtail_ref, s, 2 * p, heads, d),
                    state_rows(dtail_ref, s, 2 * p + 1, heads, d),
                ],
                0,
            )
            dk = None
            inter = []
            for e in range(2):
                h = 2 * p + e
                mine = low if e == 0 else ~low
                hm = slice(h * m, (h + 1) * m)
                vm = jnp.where(mine, v_pair, jnp.zeros_like(v_pair)) * tgb
                phk = phk_ref[r, hm]
                dph = mm(
                    jnp.concatenate([dsct_ref[s, h], vm], 1),
                    jnp.concatenate([phq_ref[r, hm], ds], 0),
                ) + tg * zs[h]
                t = dph * phk.astype(f32)
                part = mm_nt(t.astype(bf16), proj_ref[h]) - jnp.where(
                    mine, jnp.sum(t, axis=1, keepdims=True) * kp, 0.0
                )
                dk = part if dk is None else dk + part
                inter.append(mm_nt(phk, ds))
            dkv_ref[r, c] = (dk * scale).astype(bf16)
            dv = dv_ref[r, c] + tg * jnp.where(low, inter[0], inter[1])
            dkv_ref[r, width + p * pair : width + (p + 1) * pair] = dv.astype(bf16)


def params(micros):
    return dict(
        compiler_params=pltpu.CompilerParams(
            dimension_semantics=("arbitrary",), vmem_limit_bytes=VMEM_LIMIT
        ),
        cost_estimate=pl.CostEstimate(
            flops=int(micros * 8e9), bytes_accessed=int(micros * 1e6), transcendentals=0
        ),
    )


def row_spec(rows, cols):
    return pl.BlockSpec((rows, cols), lambda i: (i, 0))


def lead_spec(shape):
    return pl.BlockSpec(shape, lambda i: (i,) + (0,) * (len(shape) - 1))


def whole_spec(shape):
    return pl.BlockSpec(shape, lambda i: (0,) * len(shape))


def sds(shape, dtype):
    return jax.ShapeDtypeStruct(shape, dtype)


STEP_SEQS = 2
STATE_PAD = 16


def state_shape(seqs, heads, d, m):
    return (seqs, 4, heads // 4 * d + STATE_PAD, m)


def call_features(x, wa, wb, b, proj, tg, block, heads, d):
    rows, width = x.shape
    m = proj.shape[2]
    n = STEP_SEQS * block
    st = state_shape(STEP_SEQS, heads, d, m)
    return pl.pallas_call(
        partial(features_kernel, block, heads, d),
        grid=(rows // n,),
        in_specs=[
            row_spec(n, width), whole_spec(wa.shape), whole_spec(wb.shape), whole_spec(b.shape),
            whole_spec(proj.shape), row_spec(n, 1),
        ],
        out_specs=[row_spec(n, width)] * 3 + [row_spec(n, heads * m)] * 2 + [lead_spec(st)],
        out_shape=[sds((rows, width), bf16)] * 3
        + [sds((rows, heads * m), bf16)] * 2
        + [sds((rows // block,) + st[1:], bf16)],
        scratch_shapes=[pltpu.VMEM((16, m), f32)],
        name="features",
        **params(10),
    )(x, wa, wb, b, proj, tg)


def call_features_tiled(x, a, b, proj, tg, shard_rows, block, heads, d):
    rows, width = x.shape
    m = proj.shape[2]
    n = STEP_SEQS * block
    st = state_shape(STEP_SEQS, heads, d, m)
    parts = (a.buf, a.other, b.buf, b.other)
    wa, wb = (width, a.buf.shape[2]), (width, b.buf.shape[2])
    return pl.pallas_call(
        partial(features_tiled_kernel, block, heads, d, (a.order, b.order), shard_rows),
        grid=(rows // n,),
        in_specs=[pl.BlockSpec(memory_space=pltpu.SMEM), row_spec(n, width)]
        + [whole_spec(t.shape) for t in parts]
        + [whole_spec(proj.shape), row_spec(n, 1)],
        out_specs=[row_spec(n, width)] * 2
        + [row_spec(n, heads * m), lead_spec(st)]
        + [whole_spec(t) for t in (wa, wb, (8, 3 * width))],
        out_shape=[sds((rows, width), bf16)] * 2
        + [sds((rows, heads * m), bf16), sds((rows // block,) + st[1:], bf16)]
        + [sds(wa, bf16), sds(wb, bf16), sds((8, 3 * width), f32)],
        scratch_shapes=[pltpu.VMEM((16, m), f32)],
        name="features",
        **params(9),
    )(my_flat().astype(jnp.int32).reshape(1), x, *parts, proj, tg)


def call_query(x, wa, bias, proj, block, heads, d):
    rows, width = x.shape
    m = proj.shape[2]
    n = STEP_SEQS * block
    return pl.pallas_call(
        partial(query_kernel, block, heads, d),
        grid=(rows // n,),
        in_specs=[
            row_spec(n, width), pl.BlockSpec((width, width), lambda i: (0, 0)),
            whole_spec(bias.shape), whole_spec(proj.shape),
        ],
        out_specs=[row_spec(n, width), row_spec(n, heads * m)],
        out_shape=[sds((rows, width), bf16), sds((rows, heads * m), bf16)],
        name="query",
        **params(4),
    )(x, wa, bias, proj)


def call_local(phq, phk, v, gates, id_rows, block, heads, d):
    rows = v.shape[0]
    n = STEP_SEQS * block
    return pl.pallas_call(
        partial(local_kernel, block, heads, d),
        grid=(rows // n,),
        in_specs=[
            row_spec(n, phq.shape[1]), row_spec(n, phk.shape[1]), row_spec(n, v.shape[1]),
            row_spec(n, gates.shape[1]), lead_spec((STEP_SEQS, 1, block)),
        ],
        out_specs=[
            lead_spec((STEP_SEQS, heads, block, block)), row_spec(n, heads * 2 * d),
            whole_spec((1, 1)),
        ],
        out_shape=[
            sds((rows // block, heads, block, block), bf16), sds((rows, heads * 2 * d), f32),
            sds((1, 1), f32),
        ],
        name="local",
        **params(8),
    )(phq, phk, v, gates, id_rows)


def call_middle(x, cot, phq, nd, pre, gates, weights, tiled, shard_rows, ff, block, heads, d):
    rows, width = x.shape
    m = phq.shape[1] // heads
    n = STEP_SEQS * block
    st = (STEP_SEQS,) + pre.shape[1:]
    return pl.pallas_call(
        partial(middle_kernel, block, heads, d, 768, tiled, shard_rows),
        grid=(rows // n,),
        in_specs=[
            row_spec(n, width), row_spec(n, width), row_spec(n, phq.shape[1]),
            row_spec(n, nd.shape[1]), lead_spec(st), row_spec(n, gates.shape[1]),
        ]
        + [pl.BlockSpec(memory_space=pl.ANY)] * len(weights),
        out_specs=[
            row_spec(n, width), row_spec(n, width), row_spec(n, width), row_spec(n, 128),
            lead_spec(st), row_spec(n, width), row_spec(n, width), row_spec(n, width),
            row_spec(n, ff), row_spec(n, width), row_spec(n, ff), whole_spec((8, width)),
            whole_spec((1, ff)),
        ],
        out_shape=[
            sds((rows, width), bf16), sds((rows, width), f32), sds((rows, width), bf16),
            sds((rows, 128), f32), sds(pre.shape, bf16), sds((rows, width), bf16),
            sds((rows, width), bf16), sds((rows, width), bf16), sds((rows, ff), bf16),
            sds((rows, width), bf16), sds((rows, ff), bf16), sds((8, width), f32),
            sds((1, ff), f32),
        ],
        scratch_shapes=[
            pltpu.VMEM((n, width), f32), pltpu.VMEM((n, width), f32), pltpu.VMEM((n, ff), f32),
            pltpu.VMEM((16, m), f32), pltpu.VMEM((width, width), bf16),
            pltpu.VMEM((width, ff), bf16), pltpu.VMEM((ff, width), bf16),
            pltpu.VMEM((8, width), f32), pltpu.VMEM((8, ff), f32), pltpu.SemaphoreType.DMA((5,)),
        ]
        + ([pltpu.VMEM((width, ff), bf16), pltpu.VMEM((width, 128), bf16)] if tiled else []),
        name="middle",
        **params(31),
    )(x, cot, phq, nd, pre, gates, *weights)


def call_back_query(
    half, q, v, phq, phk, amat, dnum, dden, pre, gates, id_rows, proj, ties, block, heads, d
):
    rows, width = q.shape
    n = STEP_SEQS * block
    sq = (STEP_SEQS, heads, block, block)

    def rs(cols):
        return pl.BlockSpec((n, cols), lambda i: (half, 0))

    def ls(shape):
        return pl.BlockSpec(shape, lambda i: (half,) + (0,) * (len(shape) - 1))

    def kernel(*refs):
        back_query_kernel(block, heads, d, *refs[:11], *refs[11 + len(ties) :])

    return pl.pallas_call(
        kernel,
        grid=(1,),
        in_specs=[
            rs(width), rs(width), rs(phq.shape[1]), rs(phk.shape[1]), ls(sq), rs(width), rs(128),
            ls((STEP_SEQS,) + pre.shape[1:]), rs(gates.shape[1]), ls((STEP_SEQS, 1, block)),
            whole_spec(proj.shape),
        ]
        + [pl.BlockSpec(memory_space=pl.ANY)] * len(ties),
        out_specs=[row_spec(n, width), row_spec(n, width), lead_spec(sq), whole_spec((1, 1))],
        out_shape=[
            sds((n, width), bf16), sds((n, width), f32), sds(sq, bf16), sds((1, 1), f32),
        ],
        name="back_query",
        **params(8),
    )(q, v, phq, phk, amat, dnum, dden, pre, gates, id_rows, proj, *ties)


def call_back_key(k, v, phq, phk, dvs, dscts, dtail, gates, proj, ties, block, heads, d):
    rows, width = k.shape
    n = STEP_SEQS * block
    sq = (STEP_SEQS, heads, block, block)
    steps = rows // n

    def kernel(k_ref, v_ref, phq_ref, phk_ref, *refs):
        for i in range(steps):

            @pl.when(pl.program_id(0) == i)
            def _():
                back_key_kernel(
                    block, heads, d, k_ref, v_ref, phq_ref, phk_ref, refs[i], refs[steps + i],
                    *refs[2 * steps : 2 * steps + 3], refs[-1],
                )

    return pl.pallas_call(
        kernel,
        grid=(steps,),
        in_specs=[
            row_spec(n, width), row_spec(n, width), row_spec(n, phq.shape[1]),
            row_spec(n, phk.shape[1]),
        ]
        + [whole_spec((n, width))] * steps
        + [whole_spec(sq)] * steps
        + [
            lead_spec((STEP_SEQS,) + dtail.shape[1:]), row_spec(n, gates.shape[1]),
            whole_spec(proj.shape),
        ]
        + [pl.BlockSpec(memory_space=pl.ANY)] * len(ties),
        out_specs=row_spec(n, 2 * width),
        out_shape=sds((rows, 2 * width), bf16),
        name="back_key",
        **params(13),
    )(k, v, phq, phk, *dvs, *dscts, dtail, gates, proj, *ties)


TN = (((0,), (0,)), ((), ()))


def mm_tn(a, b):
    return lax.dot_general(a, b, TN, preferred_element_type=f32)


def pack_kernel(shard_rows, w_o_ref, w_in_ref, w_out_ref, vec_ref, *refs):
    out_ref = refs[-1]
    rows = w_out_ref[...]
    parts = [w_o_ref[...], w_in_ref[...]]
    parts += [rows[i : i + shard_rows] for i in range(0, rows.shape[0], shard_rows)]
    parts += [vec_ref[...]]
    at = 0
    for part in parts:
        out_ref[:, at : at + part.shape[1]] = part
        at += part.shape[1]


def call_pack(w_o, w_in, w_out, vec, ties):
    rows = w_o.shape[0]
    cols = (w_o.size + w_in.size + w_out.size + vec.size) // rows
    return pl.pallas_call(
        partial(pack_kernel, rows),
        in_specs=[pl.BlockSpec(memory_space=pltpu.VMEM)] * 4
        + [pl.BlockSpec(memory_space=pl.ANY)] * len(ties),
        out_shape=sds((rows, cols), bf16),
        name="pack",
    )(w_o, w_in, w_out, vec, *ties)


def part_store(core, refs, index, value):
    kept, sent, rows, cols = refs
    (kept if index % 2 == core else sent)[index // 2, rows, cols] = value


def by_core(kernel, core_ref):
    for core in range(2):
        pl.when(core_ref[0] == core)(partial(kernel, core))


def grads_kernel(
    shard_rows, core_ref, attn_ref, dao_ref, h1_ref, df_ref, act_ref, dfo_ref, sums_ref, sum_in_ref,
    tie_ref, keep_i, send_i, keep_o, send_o, done_ref,
):
    done_ref[...] = jnp.zeros_like(done_ref)
    by_core(
        partial(
            grads_parts, shard_rows, attn_ref, dao_ref, h1_ref, df_ref, act_ref, dfo_ref, sums_ref,
            sum_in_ref, keep_i, send_i, keep_o, send_o,
        ),
        core_ref,
    )


def grads_parts(
    shard_rows, attn_ref, dao_ref, h1_ref, df_ref, act_ref, dfo_ref, sums_ref, sum_in_ref,
    keep_i, send_i, keep_o, send_o, core,
):
    width = dao_ref.shape[1]
    ff = df_ref.shape[1]
    groups = ff // width
    tall = groups * shard_rows
    count = h1_ref.shape[1] // shard_rows
    every = slice(None)
    dfo = dfo_ref[...]
    chunk = act_ref.shape[1] // groups
    per = chunk // tall
    for c in range(groups):
        res = mm_tn(act_ref[:, c * chunk : (c + 1) * chunk], dfo).astype(bf16)
        for j in range(per):
            part_store(
                core, (keep_o, send_o, slice(0, tall), every), c * per + j,
                res[j * tall : (j + 1) * tall],
            )
    res = mm_tn(attn_ref[...], dao_ref[...]).astype(bf16)
    for j in range(count):
        part_store(
            core, (keep_o, send_o, slice(tall, tall + shard_rows), every), j,
            res[j * shard_rows : (j + 1) * shard_rows],
        )
    h1 = h1_ref[...]
    for g in range(groups):
        res = mm_tn(h1, df_ref[:, g * width : (g + 1) * width]).astype(bf16)
        for j in range(count):
            part_store(
                core, (keep_i, send_i, every, slice(g * width, (g + 1) * width)), j,
                res[j * shard_rows : (j + 1) * shard_rows],
            )
    step = pl.program_id(0)
    small = cut_out(sums_ref[...], shard_rows, 2 * count)
    large = cut_out(jnp.broadcast_to(sum_in_ref[...], (8, ff)), groups * shard_rows, 2 * count)
    row = lax.broadcasted_iota(jnp.int32, (8, 128), 0)
    for j in range(count):
        a = jnp.where(step == 0, small[j], small[j + count])
        b = jnp.where(step == 0, large[j], large[j + count])
        value = jnp.concatenate(
            [jnp.where(row == 6, b, a), jnp.zeros((shard_rows - 8, 128), f32)], axis=0
        )
        part_store(core, (keep_i, send_i, every, slice(ff, ff + 128)), j, value.astype(bf16))


def call_grads(core, attn, dao, h1, df, act, dfo, sums, sum_in, tie, shard_rows):
    rows, width = dao.shape
    ff = df.shape[1]
    steps = 2
    n_dev = width // shard_rows
    small = (n_dev // 2, shard_rows, ff + 128)
    tall = (n_dev // 2, shard_rows * (ff // width + 1), width)

    def cut(shape):
        return lead_spec((shape[0] // steps,) + shape[1:])

    return pl.pallas_call(
        partial(grads_kernel, shard_rows),
        grid=(steps,),
        in_specs=[
            pl.BlockSpec(memory_space=pltpu.SMEM),
            pl.BlockSpec((rows, width // steps), lambda i: (0, i)), whole_spec(dao.shape),
            pl.BlockSpec((rows, width // steps), lambda i: (0, i)), whole_spec(df.shape),
            pl.BlockSpec((rows, ff // steps), lambda i: (0, i)), whole_spec(dfo.shape),
            whole_spec(sums.shape), whole_spec(sum_in.shape),
            pl.BlockSpec(memory_space=pl.ANY),
        ],
        out_specs=[cut(small), cut(small), cut(tall), cut(tall), whole_spec((1, 1))],
        out_shape=[sds(small, bf16), sds(small, bf16), sds(tall, bf16), sds(tall, bf16)]
        + [sds((1, 1), f32)],
        name="grads",
        **params(10),
    )(core, attn, dao, h1, df, act, dfo, sums, sum_in, tie)


def first_grads_kernel(
    shard_rows, ties, core_ref, x_ref, dq_ref, dkv_ref, *refs
):
    by_core(partial(first_grads_parts, shard_rows, x_ref, dq_ref, dkv_ref, *refs[ties:]), core_ref)


def first_grads_parts(
    shard_rows, x_ref, dq_ref, dkv_ref, keep_a, send_a, keep_b, send_b, core
):
    width = dq_ref.shape[1]
    chunk = width // 2
    x = x_ref[...]
    step = pl.program_id(0)
    count = x_ref.shape[1] // shard_rows
    n_dev = 2 * count
    every = slice(None)
    sums = []
    for i in range(6):
        src, c0 = (dq_ref, i * chunk) if i < 2 else (dkv_ref, (i - 2) * chunk)
        b = src[:, c0 : c0 + chunk]
        sums.append(jnp.sum(b.astype(f32), axis=0, keepdims=True))
        res = mm_tn(x, b).astype(bf16)
        refs = (keep_a, send_a) if i < 3 else (keep_b, send_b)
        cols = slice((i % 3) * chunk, (i % 3 + 1) * chunk)
        for j in range(count):
            part_store(core, refs + (every, cols), j, res[j * shard_rows : (j + 1) * shard_rows])
    row = jnp.broadcast_to(jnp.concatenate(sums, axis=1), (8, 3 * width))
    pieces = cut_out(row, 3 * width // n_dev, n_dev)
    for j in range(count):
        value = jnp.concatenate(
            [
                jnp.where(step == 0, pieces[j], pieces[j + count]),
                jnp.zeros((shard_rows - 8, 128), f32),
            ],
            axis=0,
        )
        cols = slice(3 * chunk, 3 * chunk + 128)
        part_store(core, (keep_a, send_a, every, cols), j, value.astype(bf16))


def call_first_grads(core, x, dq, dkv, ties, shard_rows):
    rows, width = x.shape
    steps = 2
    half = 3 * width // 2
    n_dev = width // shard_rows
    shapes = [(n_dev // 2, shard_rows, half + 128)] * 2 + [(n_dev // 2, shard_rows, half)] * 2
    return pl.pallas_call(
        partial(first_grads_kernel, shard_rows, len(ties)),
        grid=(steps,),
        in_specs=[
            pl.BlockSpec(memory_space=pltpu.SMEM),
            pl.BlockSpec((rows, width // steps), lambda i: (0, i)), whole_spec(dq.shape),
            whole_spec(dkv.shape),
        ]
        + [pl.BlockSpec(memory_space=pl.ANY)] * len(ties),
        out_specs=[lead_spec((t[0] // steps,) + t[1:]) for t in shapes],
        out_shape=[sds(t, bf16) for t in shapes],
        name="first_grads",
        **params(6),
    )(core, x, dq, dkv, *ties)


def input_grad_kernel(dq_ref, dkv_ref, wa_ref, wb_ref, dr1_ref, *refs):
    out_ref, done_ref = refs[-2:]
    done_ref[...] = jnp.zeros_like(done_ref)
    width = dq_ref.shape[1]
    chunk = width // 2
    acc = dr1_ref[...]
    for i in range(6):
        src, c0 = (dq_ref, i * chunk) if i < 2 else (dkv_ref, (i - 2) * chunk)
        w_ref = wa_ref if i < 3 else wb_ref
        acc = acc + mm_nt(src[:, c0 : c0 + chunk], w_ref[:, (i % 3) * chunk : (i % 3 + 1) * chunk])
    out_ref[...] = acc.astype(bf16)


def call_input_grad(dq, dkv, wa, wb, dr1, ties, n):
    rows, width = dq.shape
    return pl.pallas_call(
        input_grad_kernel,
        grid=(rows // n,),
        in_specs=[
            row_spec(n, width), row_spec(n, 2 * width), whole_spec(wa.shape), whole_spec(wb.shape),
            row_spec(n, width),
        ]
        + [pl.BlockSpec(memory_space=pl.ANY)] * len(ties),
        out_specs=[row_spec(n, width), whole_spec((1, 1))],
        out_shape=[sds((rows, width), bf16), sds((1, 1), f32)],
        name="input_grad",
        **params(6),
    )(dq, dkv, wa, wb, dr1, *ties)


def body(
    inputs,
    seg_ids,
    cotangent,
    projection,
    w_qkv,
    b_qkv,
    w_o,
    b_o,
    ln1_gain,
    ln1_bias,
    w_in,
    b_in,
    w_out,
    b_out,
    ln2_gain,
    ln2_bias,
):
    micro, seqs_micro, block, width = inputs.shape
    heads, d, m = projection.shape
    n_seq = lax.axis_size("seq")
    n_dev = lax.axis_size("batch") * n_seq
    place = lax.axis_index("seq")
    seqs = micro * seqs_micro
    rows = seqs * block

    vectors = (b_qkv, b_o, ln1_gain, ln1_bias, b_in, b_out, ln2_gain, ln2_bias)
    sizes = [v.shape[0] for v in vectors]
    cuts = [sum(sizes[:i]) for i in range(len(sizes) + 1)]
    idents = seg_ids.reshape(seqs, block)
    shard_rows = w_qkv.shape[0]
    tiled = shard_rows % 8 == 0
    ids_b = idents[:, -1].astype(bf16)

    def as_rows(parts):
        t = jnp.stack([jnp.pad(t, (0, 128 - t.shape[0])) for t in parts])
        return jnp.pad(t, ((0, shard_rows - len(parts)), (0, 0)))

    order = (1, 2, 3, 5, 6, 7, 4)
    half = w_qkv.shape[1] // 2
    x = inputs.reshape(rows, width)
    dims = (block, heads, d)
    idents_f = idents.astype(f32)
    tail_gate = (idents_f == idents_f[:, -1:]).astype(f32)
    zero = jnp.zeros_like(projection[::2])
    proj = jnp.stack(
        [
            jnp.concatenate([projection[0::2], zero], axis=1),
            jnp.concatenate([zero, projection[1::2]], axis=1),
        ],
        axis=1,
    ).reshape(heads, 2 * d, m)
    f_cols = w_in.shape[1]
    if tiled:
        first = jnp.concatenate([w_qkv[:, :half], as_rows((b_qkv, ids_b))], axis=1)
        gather_a, gather_b = Gather(first, False), Gather(w_qkv[:, half:], True)
        ties = ()
        for _ in range(1):
            ties = (gather_a.step(), gather_b.step())
        packed = call_pack(w_o, w_in, w_out, as_rows([vectors[i] for i in order]), ties)
        gather_a.rest()
        gather_b.rest()
        weights = (lax.all_gather(packed, AXES, axis=0, tiled=True),)
        ids = jnp.concatenate([t[:, 1, half : half + seqs] for t in (gather_a.buf, gather_a.other)])
        device = lax.axis_index("batch") * n_seq + jnp.arange(n_seq)
        index = slot(gather_a.order, my_flat(), device) + ((device ^ my_flat()) & 1) * (n_dev // 2)
        chosen = (index[:, None] == jnp.arange(n_dev)[None, :]).astype(f32)
        last_all = jnp.sum(chosen[:, :, None] * ids.astype(f32)[None], axis=1)
        k, v, phk, tails, w_a, w_b, bias = call_features_tiled(
            x, gather_a, gather_b, proj, tail_gate.reshape(rows, 1), shard_rows, *dims
        )
        q, phq = call_query(x, w_a, bias, proj, *dims)
    else:
        flat = jnp.concatenate(vectors + (ids_b,))
        flat = jnp.pad(flat, (0, -flat.shape[0] % 128)).reshape(-1, 128)
        used = flat.shape[0]
        flat = jnp.pad(flat, ((0, shard_rows - used), (0, 0)))
        w_a = gather_rows(jnp.concatenate([w_qkv[:, :half], flat], axis=1), False)
        w_b = gather_rows(w_qkv[:, half:], True)
        packed = w_a[:, half:].reshape(n_dev, shard_rows, 128)[:, :used].reshape(n_dev, -1)
        whole = [
            packed[:, cuts[i] : cuts[i] + sizes[i]].reshape(1, -1).astype(f32)
            for i in range(len(sizes))
        ]
        ids_all = packed[:, cuts[-1] : cuts[-1] + seqs].reshape(-1, n_seq, seqs).astype(f32)
        last_all = lax.dynamic_index_in_dim(ids_all, lax.axis_index("batch"), 0, False)
        rows_of = [whole[i] for i in order[:6]]
        weights = (
            gather_rows(w_o, False), gather_rows(w_in, True), gather_rows(w_out, False),
            jnp.concatenate(rows_of + rows_of[:2]), jnp.concatenate([whole[4]] * 8),
        )
        q, k, v, phq, phk, tails = call_features(
            x, w_a, w_b, whole[0], proj, tail_gate.reshape(rows, 1), *dims
        )

    pre_all = jnp.concatenate([-jnp.ones_like(last_all[:1]), last_all[:-1]], axis=0)
    pre_ident = lax.dynamic_index_in_dim(pre_all, place, 0, False)
    gates = jnp.stack(
        [
            idents_f,
            tail_gate,
            (idents_f == pre_ident[:, None]).astype(f32),
        ],
        axis=-1,
    ).reshape(rows, 3)
    gates = jnp.pad(gates, ((0, 0), (0, 5)))
    id_rows = idents_f[:, None, :]
    amat, nd, done = call_local(phq, phk, v, gates, id_rows, *dims)
    pre = exclusive_scan(tails, last_all, False, lambda sent: [done])
    (y, dr1, dnum, dden, dpre, attn, dao, h1, act, dfo, df, sums, sum_in) = call_middle(
        x, cotangent.reshape(rows, width), phq, nd, pre, gates, weights, tiled,
        shard_rows, f_cols, *dims,
    )
    core = (place & 1).astype(jnp.int32).reshape(1)

    def grad(a, b):
        return mm_tn(a, b).astype(bf16)

    halves, scatters = [], []

    def run_beside(sent):
        zeros = []
        if tiled:
            keep_i, send_i, keep_o, send_o, done = call_grads(
                core, attn, dao, h1, df, act, dfo, sums, sum_in, sent, shard_rows
            )
            zeros = [0.0]
            wide, tall = (keep_i, True, send_i), (keep_o, False, send_o)
        else:
            pieces = [t.reshape(n_dev, -1) for t in [sums[i] for i in range(6)] + [sum_in[0]]]
            vec = jnp.concatenate(pieces, axis=1)
            vec = jnp.pad(vec, ((0, 0), (0, -vec.shape[1] % 128))).reshape(n_dev, -1, 128)
            vec = jnp.pad(vec, ((0, 0), (0, shard_rows - vec.shape[1]), (0, 0))).astype(bf16)
            wide = jnp.concatenate([grad(h1, df).reshape(n_dev, shard_rows, -1), vec], axis=2)
            tall = [grad(act, dfo).reshape(n_dev, -1, width), grad(attn, dao).reshape(n_dev, -1, width)]
            wide, tall = (wide, True), (jnp.concatenate(tall, axis=1), False)
        scatters.append(Scatter(*wide))
        scatters.append(Scatter(*tall))
        for i in range(seqs // STEP_SEQS):
            halves.append(
                call_back_query(
                    i, q, v, phq, phk, amat, dnum, dden, pre, gates, id_rows, proj,
                    (), *dims
                )
            )
        return zeros + [t[3] for t in halves]

    def start_scatters(value):
        first = [t.step() for t in scatters]
        value, *first = lax.optimization_barrier((value, *first))
        for t, buf in zip(scatters, first):
            t.buf = buf
        return value

    back = exclusive_scan(dpre, pre_all, True, run_beside, start_scatters)
    scatter_i, scatter_o = scatters
    dqs, dvs, dscts, dones = zip(*halves)
    dq = jnp.concatenate(dqs)
    ties = ()
    dkv = call_back_key(k, v, phq, phk, dvs, dscts, back, gates, proj, ties, *dims)
    ties = ()
    if tiled:
        keep_a, send_a, keep_b, send_b = call_first_grads(core, x, dq, dkv, ties, shard_rows)
        scatter_a = Scatter(keep_a, False, send_a)
        scatter_b = Scatter(keep_b, True, send_b)
    else:
        dqkv = jnp.concatenate([dq, dkv], axis=1)
        gw = grad(x, dqkv).reshape(n_dev, shard_rows, -1)
        vec = jnp.sum(dqkv, axis=0, dtype=f32).reshape(n_dev, 1, -1)
        vec = jnp.pad(vec, ((0, 0), (0, shard_rows - 1), (0, 128 - sizes[0]))).astype(bf16)
        scatter_a = Scatter(jnp.concatenate([gw[:, :, :half], vec], axis=2), False)
        scatter_b = Scatter(gw[:, :, half:], True)
    ties = (scatter_a.step(), scatter_b.step()) + (scatter_i.step(), scatter_o.step())
    dx, done = call_input_grad(dq, dkv, w_a, w_b, dr1, ties, STEP_SEQS * block)
    scatter_a.step(done)
    scatter_b.step()
    part_a = scatter_a.rest()
    part_b = scatter_b.rest()
    part_i = scatter_i.rest()
    part_o = scatter_o.rest()
    g_w_out, g_w_o = part_o[: w_out.shape[0]], part_o[w_out.shape[0] :]
    g_w_in = part_i[:, :f_cols]
    lengths = [sizes[i] for i in order]
    if tiled:
        vec_grads = [part_i[i, f_cols : f_cols + n] for i, n in enumerate(lengths)]
    else:
        vec = part_i[:, f_cols:].reshape(-1)
        starts = [sum(lengths[:i]) for i in range(len(lengths))]
        vec_grads = [vec[at : at + n] for at, n in zip(starts, lengths)]
    (g_b_o, g_gain_one, g_shift_one, g_b_out, g_gain_two, g_shift_two, g_b_in) = vec_grads
    g_w_qkv = jnp.concatenate([part_a[:, :half], part_b], axis=1)
    g_b_qkv = part_a[0, half : half + sizes[0]]
    return (
        y.reshape(inputs.shape),
        dx.reshape(inputs.shape),
        g_w_qkv,
        g_b_qkv,
        g_w_o,
        g_b_o,
        g_gain_one,
        g_shift_one,
        g_w_in,
        g_b_in,
        g_w_out,
        g_b_out,
        g_gain_two,
        g_shift_two,
    )


def solution(mesh):
    rows = P(AXES, None)
    vec = P(AXES)
    tok = P(None, "batch", "seq", None)
    in_specs = (
        tok,
        P(None, "batch", "seq"),
        tok,
        P(),
        rows,
        vec,
        rows,
        vec,
        vec,
        vec,
        rows,
        vec,
        rows,
        vec,
        vec,
        vec,
    )
    out_specs = (tok, tok, rows, vec, rows, vec, vec, vec, rows, vec, rows, vec, vec, vec)
    return jax.shard_map(body, mesh=mesh, in_specs=in_specs, out_specs=out_specs, check_vma=False)
```
